32 devices in a mesh: groups: 2 (over y), ep: 4 (over z), pf: 4 (over x, core).
Axes of the slice: x: 2, y: 2, z: 4, core: 2. Of those that a mesh axis runs over, the one named last changes fastest.
Arguments:
- cache_codes: bfloat16 [128, 32, 576], P(('groups', 'pf'), 'ep'), parts along dimension 0, may hold values from -4 to 4
- cache_scales: bfloat16 [128, 32, 5], P(('groups', 'pf'), 'ep'), parts along dimension 0, may hold values from 0.29 to 3.1, as said below
- queries: bfloat16 [128, 128, 576], P(('groups', 'pf', 'ep')), parts along dimension 0, may hold values from -8192 to 8192
- new_latent: bfloat16 [128, 576], P(('groups', 'pf', 'ep')), parts along dimension 0, may hold values from -16 to 16
- prompt_lengths: int32 [128], P(('groups', 'pf', 'ep')), parts along dimension 0, may hold values from 1 to 32, 1228 in all
- tokens: bfloat16 [128, 7168], P(('groups', 'ep')), parts along dimension 0, may hold values from -6 to 6
- expert_ids: int32 [128, 8], P(('groups', 'ep')), parts along dimension 0, may hold values from 0 to 31, all different within a row; in each aligned block of 16 rows (0 to 15, 16 to 31, ...) at most 8 rows name the same one
- routing_weights: float32 [128, 8], P(('groups', 'ep')), parts along dimension 0, may hold values from 0.25 to 2.5
- w_gate: bfloat16 [32, 7168, 1024], P('ep', None, 'pf'), may hold values from -0.0625 to 0.0625
- w_up: bfloat16 [32, 7168, 1024], P('ep', None, 'pf'), may hold values from -0.0625 to 0.0625
Outputs:
- attention_out: bfloat16 [128, 128, 512], P(('groups', 'pf', 'ep')), parts along dimension 0
- moe_hidden: bfloat16 [128, 8, 1024], P(('groups', 'ep'), None, 'pf'), parts along dimension 0
The draws below stay inside these ranges and needn't reach their ends.
There are 2 independent parts, one for each index of `groups`. The reference program is written for one: setup_inputs(seed, part) draws one part's arguments, and reference() takes and returns one part's arrays. A program takes and returns all parts, laid end to end along the dimension named above; an argument that names none is the same for every part. Nothing has to cross between parts.
Inputs may be any that keep to these rules, and one draw needn't show every extreme that they name: `cache_scales`: positive scales. `prompt_lengths`: the largest length is exactly 32. `expert_ids`: each row names 8 different experts; within the rows of one ep device no expert is named more than 8 times, a bound that some block reaches.
All inputs are finite; a program needn't handle non-finite values. No bound on the sum of `prompt_lengths` on one device may be relied on, other than what follows from the above.
Results may differ from the reference program's by a relative error of at most 0.012.
Values may be sent and summed in bfloat16 or wider, within the bound.
No kernel may reach another device: no remote copies, remote signals or barrier semaphores. Data moves between devices by JAX's collectives and lax.ppermute only.
A program may use at most 192 MiB of HBM per device.

```python
import math
import jax
import jax.numpy as jnp
import numpy as np
from jax import lax

D = 7168
H = 128
LAT = 512
ROPE = 64
TOP = 8
GROUP = 128
FF_WIN = 1024
EXPERTS = 32
ROWS_DEV = 4
LMAX = 32
ROWS = 64
CAP = 8
N_PF = 4


def latent_blocks(key):
    code_key = jax.random.fold_in(key, 101)
    scale_key = jax.random.fold_in(key, 102)
    codes_drawn = jnp.clip(jax.random.normal(code_key, (ROWS, LMAX, LAT + ROPE), jnp.float32), -4.0, 4.0)
    codes_drawn = codes_drawn.astype(jnp.bfloat16).astype(jnp.float32)
    scales_drawn = jnp.exp(jax.random.uniform(scale_key, (ROWS, LMAX, LAT // GROUP + 1), jnp.float32, jnp.log(0.3), jnp.log(3.0)))
    scales_drawn = scales_drawn.astype(jnp.bfloat16).astype(jnp.float32)
    return (codes_drawn, scales_drawn)


def draw_cache_codes(key, part):
    base_key = key
    codes_drawn, scales_drawn = latent_blocks(base_key)
    return codes_drawn.astype(jnp.bfloat16)


def draw_cache_scales(key, part):
    base_key = key
    codes_drawn, scales_drawn = latent_blocks(base_key)
    return scales_drawn.astype(jnp.bfloat16)


def draw_queries(key, part):
    key = jax.random.fold_in(key, 7)
    sample = jnp.clip(jax.random.normal(key, (ROWS, H, LAT + ROPE), jnp.float32), -4.0, 4.0)
    return sample.astype(jnp.bfloat16)


def draw_new_latent(key, part):
    key = jax.random.fold_in(key, 11)
    sample = jnp.clip(1.3 * jax.random.normal(key, (ROWS, LAT + ROPE), jnp.float32), -5.0, 5.0)
    return sample.astype(jnp.bfloat16)


def block_scale(rng, dims, cuts, smallest, top_value):
    gain, own = 1.0, jax.random.fold_in(rng, 6)
    for position, shards_of in cuts:
        steps = jnp.exp(jax.random.uniform(jax.random.fold_in(own, position), (shards_of,), jnp.float32, smallest / len(cuts), top_value / len(cuts)))
        gain = gain * jnp.repeat(steps, dims[position] // shards_of).reshape([-1 if axis == position else 1 for axis in range(len(dims))])
    return gain


def profile(number_of, total, limit, slope):
    loads = [(1 << 20) // math.isqrt(rank ** slope) + 1 for rank in range(2, number_of + 1)]
    rest, counts = total - limit - (number_of - 1), [1] * (number_of - 1)
    while rest > 0:
        candidates = [i for i in range(number_of - 1) if counts[i] < limit]
        mass, remaining = sum([loads[i] for i in candidates]), rest
        for i in candidates:
            addition = min(limit - counts[i], max(1, remaining * loads[i] // mass), rest)
            counts[i] = counts[i] + addition
            rest = rest - addition
    return np.array([limit] + counts)


def uneven(own_key, count, total, most, skew):
    if count == 2:
        one = jax.random.randint(own_key, (), max(1, total - most), min(most, total - 1) + 1)
        return jnp.stack([one, total - one])
    tallies = jnp.asarray(profile(count, total, most, skew), jnp.int32)
    couples = (count - 1) // 2
    donor, sink = tallies[1:1 + 2 * couples:2], tallies[2:2 + 2 * couples:2]
    margin = jnp.minimum(donor - 1, most - sink)
    shifted = jax.random.randint(jax.random.fold_in(own_key, 1), (couples,), 0, 1 << 20) % (margin + 1)
    tallies = tallies.at[1:1 + 2 * couples:2].set(donor - shifted).at[2:2 + 2 * couples:2].set(sink + shifted)
    return tallies[jax.random.permutation(jax.random.fold_in(own_key, 2), count)]


def routed_block(key, own, number, rows, number_of, top, limit, slope):
    order = jax.random.permutation(key, number_of)
    packed, ordinary = shares(number_of, rows * top, limit, slope, True), shares(number_of, rows * top, limit, slope, False)
    places = jnp.arange(number_of)

    def named(lengths, rotation):
        used = int((lengths > 0).sum())
        fixed = max(1, used // 4)
        passed = fixed + (places - fixed + rotation * (used - fixed)) % max(1, number_of - fixed)
        return jnp.zeros((number_of,), jnp.int32).at[order[jnp.where(places < fixed, places, passed)]].set(jnp.asarray(lengths, jnp.int32))

    lengths = jnp.where(number % 4 == 0, named(packed, number // 4), named(ordinary, number - number // 4 - 1))
    mixed = jax.random.permutation(jax.random.fold_in(own, 3), number_of)
    source_of, receiver = mixed[0:number_of // 2 * 2:2], mixed[1:number_of // 2 * 2:2]
    room = jnp.minimum(lengths[source_of] - 1, limit - lengths[receiver]) // 2
    room = jnp.where((source_of == order[0]) | (receiver == order[0]) | (lengths[receiver] == 0), 0, jnp.maximum(room, 0))
    passed = jax.random.randint(jax.random.fold_in(own, 4), (number_of // 2,), 0, 1 << 20) % (room + 1)
    lengths = lengths.at[source_of].add(-passed).at[receiver].add(passed)
    items = jnp.searchsorted(jnp.cumsum(lengths), jnp.arange(rows * top), side="right").astype(jnp.int32)
    listing = items.reshape(top, rows).T
    listing = listing[jax.random.permutation(jax.random.fold_in(own, 1), rows)]
    rotation = jax.random.randint(jax.random.fold_in(own, 2), (rows, 1), 0, top)
    return jnp.take_along_axis(listing, (jnp.arange(top)[None, :] + rotation) % top, axis=1)


def shares(number_of, total, limit, lean, full):
    portions = [(1 << 20) // math.isqrt(rank ** lean) + 1 for rank in range(1, number_of + 1)]
    largest = limit if full else min(limit, max(-(-total // number_of), total * portions[0] // sum(portions)))
    least = 1 if total - largest >= number_of - 1 else 0
    given, surplus = [largest] + [least] * (number_of - 1), total - largest - least * (number_of - 1)
    while surplus > 0:
        free = [i for i in range(1, number_of) if given[i] < largest] or [i for i in range(1, number_of) if given[i] < limit]
        pool, remaining = sum([portions[i] for i in free]), surplus
        for i in free:
            addition = min(limit - given[i], max(1, remaining * portions[i] // pool), surplus)
            given[i] = given[i] + addition
            surplus = surplus - addition
    return np.array(given)


def gaussian(key, extent, deviation, reach, split=(), kind=jnp.bfloat16):
    gain = block_scale(key, extent, split, -0.22, 0.18) if split else 1.0
    entries = jax.random.normal(key, extent, jnp.float32) * deviation * gain
    return jnp.minimum(jnp.maximum(entries, -reach), reach).astype(kind)


def setup_inputs(seed: int = 0, part: int = 0) -> dict:
    key_list = jax.random.split(jax.random.key(seed), 11)
    part_keys = jax.random.split(jax.random.fold_in(key_list[10], part), 11)
    cache_codes = draw_cache_codes(jax.random.fold_in(jax.random.fold_in(key_list[10], part), 71), part)
    cache_scales = draw_cache_scales(jax.random.fold_in(jax.random.fold_in(key_list[10], part), 71), part)
    queries = draw_queries(jax.random.fold_in(jax.random.fold_in(key_list[10], part), 71), part)
    new_latent = draw_new_latent(jax.random.fold_in(jax.random.fold_in(key_list[10], part), 71), part)
    prompt_lengths = uneven(part_keys[4], ROWS, ROWS * LMAX * 3 // 5, LMAX, 2).astype(jnp.int32)
    tokens = gaussian(part_keys[5], (ROWS, D), 1.0, 6.0, ((0, 4),))
    expert_ids_keys = jax.random.split(jax.random.fold_in(part_keys[6], 1), ROWS // (ROWS_DEV * N_PF))
    expert_ids_turns = jax.random.permutation(jax.random.fold_in(part_keys[6], 3), ROWS // (ROWS_DEV * N_PF))
    expert_ids = jax.vmap(lambda own, number: routed_block(jax.random.fold_in(part_keys[6], 2), own, number, ROWS_DEV * N_PF, EXPERTS, TOP, CAP, 2))(expert_ids_keys, expert_ids_turns).reshape((ROWS, TOP))
    routing_weights = jnp.clip(jnp.exp(math.log(2.5) - 2.3025851 * jax.random.uniform(part_keys[7], (ROWS, TOP), jnp.float32) ** block_scale(part_keys[7], (ROWS, TOP), ((0, 4),), -0.2, 0.2)), 0.25, 2.5)
    w_gate = gaussian(key_list[8], (EXPERTS, D, FF_WIN), D ** -0.5, 0.0625, ((0, 4), (2, 4)))
    w_up = gaussian(key_list[9], (EXPERTS, D, FF_WIN), D ** -0.5, 0.0625, ((0, 4), (2, 4)))
    return dict(cache_codes=cache_codes, cache_scales=cache_scales, queries=queries, new_latent=new_latent, prompt_lengths=prompt_lengths, tokens=tokens, expert_ids=expert_ids, routing_weights=routing_weights, w_gate=w_gate, w_up=w_up)


qk_scale = 192.0 ** -0.5


def spread_scales(scale_block):
    latent_part = jnp.repeat(scale_block[..., :-1], GROUP, axis=-1, total_repeat_length=LAT)
    rope_part = jnp.repeat(scale_block[..., -1:], ROPE, axis=-1, total_repeat_length=ROPE)
    return jnp.concatenate([latent_part, rope_part], axis=-1)


def attend(query_block, latent_cache, latent_new, length_block):
    query_wide = query_block.astype(jnp.float32)
    cache_wide = latent_cache.astype(jnp.float32)
    new_wide = latent_new.astype(jnp.float32)
    scores = jnp.einsum("rhc,rtc->rht", query_wide, cache_wide) * qk_scale
    own_score = jnp.einsum("rhc,rc->rh", query_wide, new_wide) * qk_scale
    positions = jnp.arange(latent_cache.shape[1], dtype=jnp.int32)
    live_mask = (positions[None, :] < length_block[:, None])[:, None, :]
    peak = jnp.maximum(jnp.max(jnp.where(live_mask, scores, -jnp.inf), axis=2), own_score)
    exponent = jnp.where(live_mask, jnp.exp(scores - peak[..., None]), 0.0)
    own_exponent = jnp.exp(own_score - peak)
    denominator = jnp.sum(exponent, axis=2) + own_exponent
    weights = (exponent / denominator[..., None]).astype(jnp.bfloat16)
    own_weight = (own_exponent / denominator).astype(jnp.bfloat16)
    mixed = jnp.einsum("rht,rtc->rhc", weights.astype(jnp.float32), cache_wide[:, :, :LAT])
    mixed = mixed + own_weight.astype(jnp.float32)[..., None] * new_wide[:, None, :LAT]
    return mixed.astype(jnp.bfloat16)


def reference(cache_codes, cache_scales, queries, new_latent, prompt_lengths, tokens, expert_ids, routing_weights, w_gate, w_up):
    def attend_rows(inputs):
        code_block, scale_block, query_block, latent_new, length_block = inputs
        latent_cache = (code_block.astype(jnp.float32) * spread_scales(scale_block.astype(jnp.float32))).astype(jnp.bfloat16)
        return attend(query_block, latent_cache, latent_new, length_block)

    def by_rows(stacked):
        return stacked.reshape((ROWS // ROWS_DEV, ROWS_DEV) + stacked.shape[1:])

    attention_out = lax.map(attend_rows, (by_rows(cache_codes), by_rows(cache_scales), by_rows(queries), by_rows(new_latent), by_rows(prompt_lengths)))
    attention_out = attention_out.reshape(ROWS, H, LAT)

    def expert_step(running, inputs):
        gate_weight, up_weight, expert_index = inputs
        gate_part = jnp.dot(tokens, gate_weight, preferred_element_type=jnp.float32)
        up_part = jnp.dot(tokens, up_weight, preferred_element_type=jnp.float32)
        hidden = (jax.nn.silu(gate_part) * up_part).astype(jnp.bfloat16)
        hidden = lax.optimization_barrier(hidden).astype(jnp.float32)
        matches = (expert_ids == expert_index).astype(jnp.float32)
        return running + matches[:, :, None] * hidden[:, None, :], None

    running = jnp.zeros((ROWS, TOP, FF_WIN), jnp.float32)
    running, unused = lax.scan(expert_step, running, (w_gate, w_up, jnp.arange(EXPERTS, dtype=jnp.int32)))
    moe_hidden = (running * routing_weights[:, :, None]).astype(jnp.bfloat16)
    return attention_out, moe_hidden
```

```python
import functools

import jax
import jax.numpy as jnp
from jax import lax
from jax.experimental import pallas as pl
from jax.experimental.pallas import tpu as pltpu
from jax.sharding import PartitionSpec as P

LAT = 512
ROPE = 64
GROUP = 128
CHANNELS = 640

qk_scale = 192.0 ** (-0.5)
VM = pl.BlockSpec(memory_space=pltpu.VMEM)
SM = pl.BlockSpec(memory_space=pltpu.SMEM)
ANY = pl.BlockSpec(memory_space=pl.ANY)


def spread_scales(scale_block):
    latent_part = jnp.repeat(scale_block[..., :-1], GROUP, axis=-1, total_repeat_length=LAT)
    rope_part = jnp.repeat(scale_block[..., -1:], ROPE, axis=-1, total_repeat_length=ROPE)
    return jnp.concatenate([latent_part, rope_part], axis=-1)


def decode_cache(codes, scales):
    return (codes.astype(jnp.float32) * spread_scales(scales.astype(jnp.float32))).astype(
        jnp.bfloat16
    )


def attend_kernel(per, q_ref, new_ref, len_ref, at_ref, *refs):
    pieces, (o_ref, kv_ref) = refs[:-2], refs[-2:]
    rows, width, heads = q_ref.shape
    total = kv_ref.shape[0]
    block = rows * per
    count = len(pieces) * block
    kv_ref[pl.ds(count, total - count), :] = jnp.zeros((total - count, width), jnp.bfloat16)
    for d, piece in enumerate(pieces):
        kv_ref[pl.ds(d * block, block), :] = piece[:, piece.shape[1] - CHANNELS :][:, :width]
    kv_ref[pl.ds(count, rows), :] = new_ref[...]
    kv = kv_ref[...]
    place = lax.broadcasted_iota(jnp.int32, (total, 1), 0)
    start = jnp.zeros_like(place)
    for d in range(len(pieces)):
        start = jnp.where(place // block == d, at_ref[d], start)
    row_of = place % block // per
    position = start + place % per
    for r in range(rows):
        live = ((place < count) & (row_of == r) & (position < len_ref[r])) | (place == count + r)
        scores = jnp.dot(kv, q_ref[r], preferred_element_type=jnp.float32) * qk_scale
        scores = jnp.where(live, scores, -jnp.inf)
        exponent = jnp.exp(scores - jnp.max(scores, axis=0, keepdims=True))
        weights = exponent / jnp.sum(exponent, axis=0, keepdims=True)
        o_ref[r] = lax.dot_general(
            weights.astype(jnp.bfloat16),
            kv[:, :LAT],
            (((0,), (0,)), ((), ())),
            preferred_element_type=jnp.float32,
        ).astype(jnp.bfloat16)


def attend(queries, new_latent, prompt_lengths, starts, per, pieces):
    rows, heads, width = queries.shape
    count = sum(p.shape[0] for p in pieces)
    total = -(-(count + rows) // 128) * 128
    return pl.pallas_call(
        functools.partial(attend_kernel, per),
        in_specs=[VM, VM, SM, SM] + [VM] * len(pieces),
        out_specs=VM,
        out_shape=jax.ShapeDtypeStruct((rows, heads, LAT), jnp.bfloat16),
        scratch_shapes=[pltpu.VMEM((total, width), jnp.bfloat16)],
        cost_estimate=pl.CostEstimate(
            flops=4 * rows * heads * total * width,
            bytes_accessed=2 * rows * heads * (width + LAT),
            transcendentals=rows * heads * total,
        ),
        compiler_params=pltpu.CompilerParams(vmem_limit_bytes=8 << 20),
        name="attend",
    )(queries.swapaxes(1, 2), new_latent, prompt_lengths, starts, *pieces)


def pack_kernel(n_ep, codes_ref, scales_ref, tokens_ref, *refs):
    outs, own = refs[:-1], refs[-1]
    total, width = codes_ref.shape
    block = total // n_ep
    here, me = lax.axis_index("ep"), lax.axis_index("pf")
    group = lax.broadcasted_iota(jnp.int32, (scales_ref.shape[1], width), 1) // GROUP
    spread = group == lax.broadcasted_iota(jnp.int32, group.shape, 0)
    scales = jnp.dot(
        scales_ref[...],
        jnp.where(spread, 1.0, 0.0).astype(jnp.bfloat16),
        preferred_element_type=jnp.float32,
    )
    latent = (codes_ref[...].astype(jnp.float32) * scales).astype(jnp.bfloat16)
    rows = tokens_ref.shape[0]
    half = tokens_ref.shape[1] // 8
    fill = jnp.zeros((block, CHANNELS - width), jnp.bfloat16)
    for j in range(n_ep):
        part = latent[j * block : (j + 1) * block]

        @pl.when(here == j)
        def _():
            own[:, :width] = part
            own[:, width:] = fill

        for d, out in enumerate(outs, 1):

            @pl.when(lax.rem(here + d, n_ep) == j)
            def _():
                out[:, half : half + width] = part
                out[:, half + width :] = fill

    for out in outs:
        for c in range(2):
            start = pl.multiple_of((2 * me + c) * half, 128)
            out[c * rows : (c + 1) * rows, :half] = tokens_ref[:, pl.ds(start, half)]


def pack(codes, scales, tokens, n_ep):
    rows, per, width = codes.shape
    block = rows * per // n_ep
    wide = tokens.shape[1] // 8 + CHANNELS
    return pl.pallas_call(
        functools.partial(pack_kernel, n_ep),
        in_specs=[VM] * 3,
        out_specs=[VM] * n_ep,
        out_shape=[jax.ShapeDtypeStruct((block, wide), jnp.bfloat16)] * (n_ep - 1)
        + [jax.ShapeDtypeStruct((block, CHANNELS), jnp.bfloat16)],
        name="pack",
    )(codes.reshape(rows * per, width), scales.reshape(rows * per, -1), tokens)


def hold_kernel(g_ref, u_ref, go_ref, uo_ref, sems):
    copies = []
    for e in range(go_ref.shape[0]):
        copies.append(pltpu.make_async_copy(g_ref.at[e], go_ref.at[e], sems.at[0, e]))
        copies.append(pltpu.make_async_copy(u_ref.at[e], uo_ref.at[e], sems.at[1, e]))
    for copy in copies:
        copy.start()
    for copy in copies:
        copy.wait()


def hold(w_gate, w_up, count):
    shape = (count,) + w_gate.shape[1:]
    return pl.pallas_call(
        hold_kernel,
        in_specs=[ANY, ANY],
        out_specs=[VM, VM],
        out_shape=[pltpu.VMEM(shape, jnp.bfloat16)] * 2,
        scratch_shapes=[pltpu.SemaphoreType.DMA((2, count))],
        cost_estimate=pl.CostEstimate(
            flops=0, bytes_accessed=4 * count * shape[1] * shape[2], transcendentals=0
        ),
        compiler_params=pltpu.CompilerParams(vmem_limit_bytes=2 << 20),
        name="hold",
    )(w_gate, w_up)


def experts_kernel(n_ep, slots, *refs):
    own, xs, (hg, hu, g_hbm, u_hbm), rest = refs[0], refs[1:5], refs[5:9], refs[9:]
    outs, (x_all, gb, ub, sems) = rest[:n_ep], rest[n_ep:]
    held = hg.shape[0]
    experts = g_hbm.shape[0]
    quarter = xs[0].shape[1]
    part = own.shape[0]
    me = lax.axis_index("pf")

    def copies(e, s):
        return (
            pltpu.make_async_copy(g_hbm.at[e], gb.at[s], sems.at[0, s]),
            pltpu.make_async_copy(u_hbm.at[e], ub.at[s], sems.at[1, s]),
        )

    for s in range(min(slots, experts - held)):
        for copy in copies(held + s, s):
            copy.start()
    x_all[:part, :] = own[...]
    for b in range(4):
        start = pl.multiple_of((me ^ b) * quarter, 128)
        x_all[part:, pl.ds(start, quarter)] = xs[b][...]

    def run(e, g_weights, u_weights, at):
        gate = up = jnp.zeros((x_all.shape[0], gb.shape[2]), jnp.float32)
        for k in range(0, x_all.shape[1], quarter):
            x = x_all[:, k : k + quarter]
            gate += jnp.dot(
                x, g_weights[at, k : k + quarter], preferred_element_type=jnp.float32
            )
            up += jnp.dot(x, u_weights[at, k : k + quarter], preferred_element_type=jnp.float32)
        hidden = (gate * jax.nn.sigmoid(gate) * up).astype(jnp.bfloat16)
        for d in range(n_ep):
            outs[d][e] = hidden[d * part : (d + 1) * part]

    @pl.loop(0, held)
    def _(e):
        run(e, hg, hu, e)

    @pl.loop(held, experts)
    def _(e):
        s = lax.rem(e - held, slots)
        for copy in copies(e, s):
            copy.wait()
        run(e, gb, ub, s)

        @pl.when(e + slots < experts)
        def _():
            for copy in copies(e + slots, s):
                copy.start()


def experts_call(own, xs, held_gate, held_up, w_gate, w_up, n_ep):
    experts, depth, wide = w_gate.shape
    rows = own.shape[0] * n_ep
    held = held_gate.shape[0]
    slots = 2
    out = jax.ShapeDtypeStruct((experts, rows // n_ep, wide), jnp.bfloat16)
    return pl.pallas_call(
        functools.partial(experts_kernel, n_ep, slots),
        in_specs=[VM] * 7 + [ANY] * 2,
        out_specs=[VM] * n_ep,
        out_shape=[out] * n_ep,
        scratch_shapes=[
            pltpu.VMEM((rows, depth), jnp.bfloat16),
            pltpu.VMEM((slots, depth, wide), jnp.bfloat16),
            pltpu.VMEM((slots, depth, wide), jnp.bfloat16),
            pltpu.SemaphoreType.DMA((2, slots)),
        ],
        cost_estimate=pl.CostEstimate(
            flops=4 * rows * depth * wide * experts,
            bytes_accessed=4 * (experts - held) * depth * wide,
            transcendentals=experts * rows * wide,
        ),
        compiler_params=pltpu.CompilerParams(vmem_limit_bytes=18 << 20),
        name="experts",
    )(
        own,
        *xs,
        pltpu.with_memory_space_constraint(held_gate, pltpu.VMEM),
        pltpu.with_memory_space_constraint(held_up, pltpu.VMEM),
        w_gate,
        w_up,
    )


def pick_kernel(ids_ref, weight_ref, base_ref, *refs):
    blocks, o_ref = refs[:-1], refs[-1]
    experts, rows, wide = blocks[0].shape
    pairs = ids_ref.shape[0]
    top = pairs // rows
    row = lax.broadcasted_iota(jnp.int32, (pairs, 1), 0) // top
    column = lax.broadcasted_iota(jnp.int32, (1, experts * rows), 1)
    total = jnp.zeros((pairs, wide), jnp.float32)
    for d, block in enumerate(blocks):
        match = (ids_ref[...] == base_ref[d] + column // rows) & (row == column % rows)
        total += jnp.dot(
            jnp.where(match, 1.0, 0.0).astype(jnp.bfloat16),
            block[...].reshape(experts * rows, wide),
            preferred_element_type=jnp.float32,
        )
    o_ref[...] = (total * weight_ref[...]).astype(jnp.bfloat16)


def pick(expert_ids, routing_weights, bases, blocks):
    rows, top = expert_ids.shape
    wide = blocks[0].shape[2]
    out = pl.pallas_call(
        pick_kernel,
        in_specs=[VM, VM, SM] + [VM] * len(blocks),
        out_specs=VM,
        out_shape=jax.ShapeDtypeStruct((rows * top, wide), jnp.bfloat16),
        name="pick",
    )(expert_ids.reshape(-1, 1), routing_weights.reshape(-1, 1), bases, *blocks)
    return out.reshape(rows, top, wide)


def shifted(x, axis, d):
    n = lax.axis_size(axis)
    return lax.ppermute(x, axis, [(s, (s + d) % n) for s in range(n)])


def crossed(x, axis, bit):
    n = lax.axis_size(axis)
    return lax.ppermute(x, axis, [(s, s ^ bit) for s in range(n)])


def local_ring(
    cache_codes,
    cache_scales,
    queries,
    new_latent,
    prompt_lengths,
    tokens,
    expert_ids,
    routing_weights,
    w_gate,
    w_up,
):
    n_ep = lax.axis_size("ep")
    here = lax.axis_index("ep")
    per = cache_codes.shape[1]
    half = tokens.shape[1] // 8
    rows = tokens.shape[0]
    *sent, own_piece = pack(cache_codes, cache_scales, tokens, n_ep)
    came = [shifted(x, "ep", d) for d, x in enumerate(sent, 1)]
    held_gate, held_up = hold(w_gate, w_up, 4)
    x0 = jnp.concatenate(
        [jnp.concatenate([x[:rows, :half], x[rows:, :half]], axis=1) for x in came], axis=0
    )
    x1 = crossed(x0, "pf", 1)
    x2 = crossed(x0, "pf", 2)
    x3 = crossed(x2, "pf", 1)
    order = jnp.arange(n_ep, dtype=jnp.int32)
    starts = (here - order) % n_ep * per
    attention_out = attend(
        queries, new_latent, prompt_lengths, starts, per, [own_piece] + came
    )
    blocks = experts_call(tokens, [x0, x1, x2, x3], held_gate, held_up, w_gate, w_up, n_ep)
    back = [blocks[0]] + [shifted(blocks[d], "ep", -d) for d in range(1, n_ep)]
    bases = (here + order) % n_ep * w_gate.shape[0]
    return attention_out, pick(expert_ids, routing_weights, bases, back)


def local_wide(
    cache_codes,
    cache_scales,
    queries,
    new_latent,
    prompt_lengths,
    tokens,
    expert_ids,
    routing_weights,
    w_gate,
    w_up,
):
    n_ep = lax.axis_size("ep")
    here = lax.axis_index("ep")
    latent = decode_cache(cache_codes, cache_scales)
    rows_dev = queries.shape[0]
    cache = lax.all_to_all(latent, "ep", split_axis=0, concat_axis=1, tiled=True)
    per = cache.shape[1]
    cache = jnp.pad(cache, ((0, 0), (0, 0), (0, CHANNELS - cache.shape[2])))
    starts = jnp.zeros((1,), jnp.int32)
    attention_out = attend(
        queries, new_latent, prompt_lengths, starts, per, [cache.reshape(-1, CHANNELS)]
    )
    x = lax.all_gather(tokens, "ep", axis=0, tiled=True)
    gate = jnp.einsum("rd,edf->erf", x, w_gate, preferred_element_type=jnp.float32)
    up = jnp.einsum("rd,edf->erf", x, w_up, preferred_element_type=jnp.float32)
    hidden = (jax.nn.silu(gate) * up).astype(jnp.bfloat16)
    back = lax.all_to_all(hidden, "ep", split_axis=1, concat_axis=0, tiled=True)
    match = expert_ids[:, :, None] == jnp.arange(back.shape[0], dtype=jnp.int32)
    picked = jnp.einsum(
        "rke,erf->rkf", match.astype(jnp.bfloat16), back, preferred_element_type=jnp.float32
    )
    return attention_out, (picked * routing_weights[:, :, None]).astype(jnp.bfloat16)


def solution(mesh):
    near = mesh.shape["ep"] == 4 and mesh.shape["pf"] == 4
    return jax.shard_map(
        local_ring if near else local_wide,
        mesh=mesh,
        in_specs=(
            P(("groups", "pf"), "ep", None),
            P(("groups", "pf"), "ep", None),
            P(("groups", "pf", "ep"), None, None),
            P(("groups", "pf", "ep"), None),
            P(("groups", "pf", "ep")),
            P(("groups", "ep"), None),
            P(("groups", "ep"), None),
            P(("groups", "ep"), None),
            P("ep", None, "pf"),
            P("ep", None, "pf"),
        ),
        out_specs=(P(("groups", "pf", "ep"), None, None), P(("groups", "ep"), None, "pf")),
        check_vma=False,
    )
```

```python
import functools

import jax
import jax.numpy as jnp
from jax import lax
from jax.experimental import pallas as pl
from jax.experimental.pallas import tpu as pltpu
from jax.sharding import PartitionSpec as P

LAT = 512
ROPE = 64
GROUP = 128
CHANNELS = 640

qk_scale = 192.0 ** (-0.5)
VM = pl.BlockSpec(memory_space=pltpu.VMEM)
SM = pl.BlockSpec(memory_space=pltpu.SMEM)
HBM = pl.BlockSpec(memory_space=pltpu.HBM)


def spread_scales(scale_block):
    latent_part = jnp.repeat(scale_block[..., :-1], GROUP, axis=-1, total_repeat_length=LAT)
    rope_part = jnp.repeat(scale_block[..., -1:], ROPE, axis=-1, total_repeat_length=ROPE)
    return jnp.concatenate([latent_part, rope_part], axis=-1)


def decode_cache(codes, scales):
    return (codes.astype(jnp.float32) * spread_scales(scales.astype(jnp.float32))).astype(
        jnp.bfloat16
    )


def attend_kernel(per, q_ref, new_ref, len_ref, at_ref, *refs):
    pieces, (o_ref, kv_ref) = refs[:-2], refs[-2:]
    rows, width, heads = q_ref.shape
    total = kv_ref.shape[0]
    block = rows * per
    count = len(pieces) * block
    kv_ref[pl.ds(count, total - count), :] = jnp.zeros((total - count, width), jnp.bfloat16)
    for d, piece in enumerate(pieces):
        kv_ref[pl.ds(d * block, block), :] = piece[:, piece.shape[1] - CHANNELS :][:, :width]
    kv_ref[pl.ds(count, rows), :] = new_ref[...]
    kv = kv_ref[...]
    place = lax.broadcasted_iota(jnp.int32, (total, 1), 0)
    start = jnp.zeros_like(place)
    for d in range(len(pieces)):
        start = jnp.where(place // block == d, at_ref[d], start)
    row_of = place % block // per
    position = start + place % per
    for r in range(rows):
        live = ((place < count) & (row_of == r) & (position < len_ref[r])) | (place == count + r)
        scores = jnp.dot(kv, q_ref[r], preferred_element_type=jnp.float32) * qk_scale
        scores = jnp.where(live, scores, -jnp.inf)
        exponent = jnp.exp(scores - jnp.max(scores, axis=0, keepdims=True))
        weights = exponent / jnp.sum(exponent, axis=0, keepdims=True)
        o_ref[r] = lax.dot_general(
            weights.astype(jnp.bfloat16),
            kv[:, :LAT],
            (((0,), (0,)), ((), ())),
            preferred_element_type=jnp.float32,
        ).astype(jnp.bfloat16)


def attend(queries, new_latent, prompt_lengths, starts, per, pieces):
    rows, heads, width = queries.shape
    count = sum(p.shape[0] for p in pieces)
    total = -(-(count + rows) // 128) * 128
    return pl.pallas_call(
        functools.partial(attend_kernel, per),
        in_specs=[VM, VM, SM, SM] + [VM] * len(pieces),
        out_specs=VM,
        out_shape=jax.ShapeDtypeStruct((rows, heads, LAT), jnp.bfloat16),
        scratch_shapes=[pltpu.VMEM((total, width), jnp.bfloat16)],
        cost_estimate=pl.CostEstimate(
            flops=4 * rows * heads * total * width,
            bytes_accessed=2 * rows * heads * (width + LAT),
            transcendentals=rows * heads * total,
        ),
        compiler_params=pltpu.CompilerParams(vmem_limit_bytes=8 << 20),
        name="attend",
    )(queries.swapaxes(1, 2), new_latent, prompt_lengths, starts, *pieces)


def pack_kernel(codes_ref, scales_ref, tokens_ref, *refs):
    outs, own, lat_ref = refs[:-2], refs[-2], refs[-1]
    rows, per, width = codes_ref.shape
    groups = scales_ref.shape[0]
    block = own.shape[0]
    here, me = lax.axis_index("ep"), lax.axis_index("pf")
    scales = scales_ref[...].astype(jnp.float32)
    lat_ref[:, width:] = jnp.zeros((rows * per, CHANNELS - width), jnp.float32)
    for r in range(rows):
        for g in range(groups):
            columns = slice(g * GROUP, min((g + 1) * GROUP, width))
            lat_ref[r * per : (r + 1) * per, columns] = (
                codes_ref[r, :, columns].astype(jnp.float32) * scales[g, :, r : r + 1]
            )
    half = tokens_ref.shape[1] // 8
    for d in range(len(outs) + 1):
        start = pl.multiple_of((here ^ d) * block, block)
        part = lat_ref[pl.ds(start, block), :].astype(jnp.bfloat16)
        if d == 0:
            own[...] = part
            continue
        outs[d - 1][:, half:] = part
        for c in range(2):
            start = pl.multiple_of((2 * me + c) * half, 128)
            outs[d - 1][c * block // 2 : (c + 1) * block // 2, :half] = tokens_ref[
                :, pl.ds(start, half)
            ]


def pack(codes, scales, tokens, n_ep):
    rows, per, width = codes.shape
    block = rows * per // n_ep
    wide = tokens.shape[1] // 8 + CHANNELS
    return pl.pallas_call(
        pack_kernel,
        in_specs=[VM] * 3,
        out_specs=[VM] * n_ep,
        out_shape=[jax.ShapeDtypeStruct((block, wide), jnp.bfloat16)] * (n_ep - 1)
        + [jax.ShapeDtypeStruct((block, CHANNELS), jnp.bfloat16)],
        scratch_shapes=[pltpu.VMEM((rows * per, CHANNELS), jnp.float32)],
        name="pack",
    )(codes, scales.transpose(2, 1, 0), tokens)


def part_copies(b, g_ref, u_ref, g_to, u_to, sems):
    depth = g_to.shape[1]
    start = pl.multiple_of((lax.axis_index("pf") ^ b) * depth, 128)
    return [
        (
            pltpu.make_async_copy(g_ref.at[e, pl.ds(start, depth)], g_to.at[e], sems.at[0, e]),
            pltpu.make_async_copy(u_ref.at[e, pl.ds(start, depth)], u_to.at[e], sems.at[1, e]),
        )
        for e in range(g_to.shape[0])
    ]


def hold_kernel(ids_ref, weight_ref, g_ref, u_ref, go_ref, uo_ref, select_ref, column_ref, sems):
    copies = part_copies(0, g_ref, u_ref, go_ref, uo_ref, sems)
    for pair in copies:
        for copy in pair:
            copy.start()
    top, rows = ids_ref.shape
    experts = g_ref.shape[0]
    here = lax.axis_index("ep")
    pair = lax.broadcasted_iota(jnp.int32, (top * rows, 1), 0)
    ids = jnp.zeros((top * rows, rows), jnp.int32)
    weight = jnp.zeros((top * rows, rows), jnp.float32)
    mine = lax.broadcasted_iota(jnp.int32, (top * rows, rows), 1) == pair // top
    for k in range(top):
        chosen = mine & (pair % top == k)
        ids = jnp.where(chosen, ids_ref[k : k + 1, :], ids)
        weight = jnp.where(chosen, weight_ref[k : k + 1, :], weight)
    ids = jnp.sum(ids, axis=1, keepdims=True)
    column_ref[...] = jnp.sum(weight, axis=1, keepdims=True)
    column = lax.broadcasted_iota(jnp.int32, (1, experts * rows), 1)
    for d in range(select_ref.shape[1] // (experts * rows)):
        match = (ids == (here ^ d) * experts + column // rows) & (column % rows == pair // top)
        select_ref[:, d * experts * rows : (d + 1) * experts * rows] = jnp.where(
            match, 1.0, 0.0
        ).astype(jnp.bfloat16)
    for pair in copies:
        for copy in pair:
            copy.wait()


def hold(expert_ids, routing_weights, w_gate, w_up, n_ep):
    experts, depth, wide = w_gate.shape
    rows, top = expert_ids.shape
    shape = (experts, depth // 4, wide)
    return pl.pallas_call(
        hold_kernel,
        in_specs=[VM, VM, HBM, HBM],
        out_specs=[VM] * 4,
        out_shape=[pltpu.VMEM(shape, jnp.bfloat16)] * 2
        + [
            jax.ShapeDtypeStruct((rows * top, n_ep * experts * rows), jnp.bfloat16),
            jax.ShapeDtypeStruct((rows * top, 1), jnp.float32),
        ],
        scratch_shapes=[pltpu.SemaphoreType.DMA((2, experts))],
        cost_estimate=pl.CostEstimate(
            flops=0, bytes_accessed=4 * experts * shape[1] * wide, transcendentals=0
        ),
        compiler_params=pltpu.CompilerParams(vmem_limit_bytes=4 << 20),
        name="hold",
    )(expert_ids.T, routing_weights.T, w_gate, w_up)


def set_rows(b, x_ref, own_ref, came_ref):
    rows, quarter = own_ref.shape[0], came_ref.shape[1]
    start = pl.multiple_of((lax.axis_index("pf") ^ b) * quarter, 128)
    x_ref[:rows, :] = own_ref[:, pl.ds(start, quarter)]
    x_ref[rows:, :] = came_ref[...]


def times(x_ref, w_ref, e):
    return jnp.dot(x_ref[...], w_ref[e], preferred_element_type=jnp.float32)


def stage_kernel(b, own, came, hg, hu, g_hbm, u_hbm, *refs):
    total, (gate, up, g_next, u_next, x_ref, sems) = refs[:-6], refs[-6:]
    copies = part_copies(b + 1, g_hbm, u_hbm, g_next, u_next, sems)
    for pair in copies:
        for copy in pair:
            copy.start()
    set_rows(b, x_ref, own, came)

    @pl.loop(0, hg.shape[0])
    def _(e):
        gate_part, up_part = times(x_ref, hg, e), times(x_ref, hu, e)
        gate[e] = gate_part + total[0][e] if total else gate_part
        up[e] = up_part + total[1][e] if total else up_part

    for pair in copies:
        for copy in pair:
            copy.wait()


def in_vmem(x):
    return pltpu.with_memory_space_constraint(x, pltpu.VMEM)


def stage(b, own, came, held, total, w_gate, w_up):
    experts, depth, wide = w_gate.shape
    rows = own.shape[0] + came.shape[0]
    sums = jax.ShapeDtypeStruct((experts, rows, wide), jnp.float32)
    *total, g_next, u_next = pl.pallas_call(
        functools.partial(stage_kernel, b),
        in_specs=[VM] * 4 + [HBM] * 2 + [VM] * len(total),
        out_specs=[VM] * 4,
        out_shape=[sums] * 2 + [pltpu.VMEM((experts, depth // 4, wide), jnp.bfloat16)] * 2,
        scratch_shapes=[
            pltpu.VMEM((rows, depth // 4), jnp.bfloat16),
            pltpu.SemaphoreType.DMA((2, experts)),
        ],
        cost_estimate=pl.CostEstimate(
            flops=rows * depth * wide * experts,
            bytes_accessed=experts * depth * wide,
            transcendentals=0,
        ),
        compiler_params=pltpu.CompilerParams(vmem_limit_bytes=8 << 20),
        name="stage",
    )(own, came, *[in_vmem(x) for x in held], w_gate, w_up, *total)
    return total, (g_next, u_next)


def last_kernel(n_ep, own, came, came_too, hg, hu, g_hbm, u_hbm, gate, up, *refs):
    outs, (x_ref, y_ref, gb, ub, sems) = refs[:n_ep], refs[n_ep:]
    experts, part = hg.shape[0], own.shape[0]
    copies = part_copies(3, g_hbm, u_hbm, gb, ub, sems)
    for pair in copies:
        for copy in pair:
            copy.start()
    set_rows(2, x_ref, own, came)
    set_rows(3, y_ref, own, came_too)
    for e in range(experts):
        gate_part = gate[e] + times(x_ref, hg, e)
        up_part = up[e] + times(x_ref, hu, e)
        for copy in copies[e]:
            copy.wait()
        gate_part += times(y_ref, gb, e)
        up_part += times(y_ref, ub, e)
        hidden = (gate_part * jax.nn.sigmoid(gate_part) * up_part).astype(jnp.bfloat16)
        for d in range(n_ep):
            outs[d][e] = hidden[d * part : (d + 1) * part]


def last(n_ep, own, came, came_too, held, total, w_gate, w_up):
    experts, depth, wide = w_gate.shape
    rows = own.shape[0] + came.shape[0]
    held_shape = (experts, depth // 4, wide)
    out = jax.ShapeDtypeStruct((experts, own.shape[0], wide), jnp.bfloat16)
    return pl.pallas_call(
        functools.partial(last_kernel, n_ep),
        in_specs=[VM] * 5 + [HBM] * 2 + [VM] * 2,
        out_specs=[VM] * n_ep,
        out_shape=[out] * n_ep,
        scratch_shapes=[
            pltpu.VMEM((rows, depth // 4), jnp.bfloat16),
            pltpu.VMEM((rows, depth // 4), jnp.bfloat16),
            pltpu.VMEM(held_shape, jnp.bfloat16),
            pltpu.VMEM(held_shape, jnp.bfloat16),
            pltpu.SemaphoreType.DMA((2, experts)),
        ],
        cost_estimate=pl.CostEstimate(
            flops=2 * rows * depth * wide * experts,
            bytes_accessed=experts * depth * wide,
            transcendentals=experts * rows * wide,
        ),
        compiler_params=pltpu.CompilerParams(vmem_limit_bytes=24 << 20),
        name="last",
    )(own, came, came_too, *[in_vmem(x) for x in held], w_gate, w_up, *total)


def pick_kernel(select_ref, column_ref, *refs):
    blocks, o_ref = refs[:-1], refs[-1]
    experts, rows, wide = blocks[0].shape
    total = jnp.zeros((select_ref.shape[0], wide), jnp.float32)
    for d, block in enumerate(blocks):
        total += jnp.dot(
            select_ref[:, d * experts * rows : (d + 1) * experts * rows],
            block[...].reshape(experts * rows, wide),
            preferred_element_type=jnp.float32,
        )
    o_ref[...] = (total * column_ref[...]).astype(jnp.bfloat16)


def pick(select, column, blocks):
    pairs, wide = select.shape[0], blocks[0].shape[2]
    return pl.pallas_call(
        pick_kernel,
        in_specs=[VM] * (2 + len(blocks)),
        out_specs=VM,
        out_shape=jax.ShapeDtypeStruct((pairs, wide), jnp.bfloat16),
        name="pick",
    )(select, column, *blocks)


def crossed(x, axis, bit):
    n = lax.axis_size(axis)
    return lax.ppermute(x, axis, [(s, s ^ bit) for s in range(n)])


def local_ring(
    cache_codes,
    cache_scales,
    queries,
    new_latent,
    prompt_lengths,
    tokens,
    expert_ids,
    routing_weights,
    w_gate,
    w_up,
):
    n_ep = lax.axis_size("ep")
    here = lax.axis_index("ep")
    per = cache_codes.shape[1]
    half = tokens.shape[1] // 8
    rows = tokens.shape[0]
    *sent, own_piece = pack(cache_codes, cache_scales, tokens, n_ep)
    came = [crossed(x, "ep", d) for d, x in enumerate(sent, 1)]
    w_gate, w_up = [pltpu.with_memory_space_constraint(w, pltpu.HBM) for w in (w_gate, w_up)]
    *held, select, column = hold(expert_ids, routing_weights, w_gate, w_up, n_ep)
    came, held, select, column = lax.optimization_barrier((came, held, select, column))
    x0 = jnp.concatenate(
        [jnp.concatenate([x[:rows, :half], x[rows:, :half]], axis=1) for x in came], axis=0
    )
    x1 = crossed(x0, "pf", 1)
    x2 = crossed(x0, "pf", 2)
    total, held = stage(0, tokens, x0, held, (), w_gate, w_up)
    x2, total = lax.optimization_barrier((x2, total))
    x3 = crossed(x2, "pf", 1)
    total, held = stage(1, tokens, x1, held, total, w_gate, w_up)
    blocks = last(n_ep, tokens, x2, x3, held, total, w_gate, w_up)
    back = [blocks[0]] + [crossed(blocks[d], "ep", d) for d in range(1, n_ep)]
    starts = (here ^ jnp.arange(n_ep, dtype=jnp.int32)) * per
    attention_out = attend(
        queries, new_latent, prompt_lengths, starts, per, [own_piece] + came
    )
    moe_hidden = pick(select, column, back)
    return attention_out, moe_hidden.reshape(rows, -1, moe_hidden.shape[1])


def local_wide(
    cache_codes,
    cache_scales,
    queries,
    new_latent,
    prompt_lengths,
    tokens,
    expert_ids,
    routing_weights,
    w_gate,
    w_up,
):
    n_ep = lax.axis_size("ep")
    here = lax.axis_index("ep")
    latent = decode_cache(cache_codes, cache_scales)
    rows_dev = queries.shape[0]
    cache = lax.all_to_all(latent, "ep", split_axis=0, concat_axis=1, tiled=True)
    per = cache.shape[1]
    cache = jnp.pad(cache, ((0, 0), (0, 0), (0, CHANNELS - cache.shape[2])))
    starts = jnp.zeros((1,), jnp.int32)
    attention_out = attend(
        queries, new_latent, prompt_lengths, starts, per, [cache.reshape(-1, CHANNELS)]
    )
    x = lax.all_gather(tokens, "ep", axis=0, tiled=True)
    gate = jnp.einsum("rd,edf->erf", x, w_gate, preferred_element_type=jnp.float32)
    up = jnp.einsum("rd,edf->erf", x, w_up, preferred_element_type=jnp.float32)
    hidden = (jax.nn.silu(gate) * up).astype(jnp.bfloat16)
    back = lax.all_to_all(hidden, "ep", split_axis=1, concat_axis=0, tiled=True)
    match = expert_ids[:, :, None] == jnp.arange(back.shape[0], dtype=jnp.int32)
    picked = jnp.einsum(
        "rke,erf->rkf", match.astype(jnp.bfloat16), back, preferred_element_type=jnp.float32
    )
    return attention_out, (picked * routing_weights[:, :, None]).astype(jnp.bfloat16)


def solution(mesh):
    near = mesh.shape["ep"] == 4 and mesh.shape["pf"] == 4
    return jax.shard_map(
        local_ring if near else local_wide,
        mesh=mesh,
        in_specs=(
            P(("groups", "pf"), "ep", None),
            P(("groups", "pf"), "ep", None),
            P(("groups", "pf", "ep"), None, None),
            P(("groups", "pf", "ep"), None),
            P(("groups", "pf", "ep")),
            P(("groups", "ep"), None),
            P(("groups", "ep"), None),
            P(("groups", "ep"), None),
            P("ep", None, "pf"),
            P("ep", None, "pf"),
        ),
        out_specs=(P(("groups", "pf", "ep"), None, None), P(("groups", "ep"), None, "pf")),
        check_vma=False,
    )
```

```python
import functools

import jax
import jax.numpy as jnp
from jax import lax
from jax.experimental import pallas as pl
from jax.experimental.pallas import tpu as pltpu
from jax.sharding import PartitionSpec as P

LAT = 512
ROPE = 64
GROUP = 128
CHANNELS = 640
SCOPE = 4 << 20
HELD = 14 << 20

qk_scale = 192.0 ** (-0.5)
VM = pl.BlockSpec(memory_space=pltpu.VMEM)
SM = pl.BlockSpec(memory_space=pltpu.SMEM)
HBM = pl.BlockSpec(memory_space=pltpu.HBM)


def spread_scales(scale_block):
    latent_part = jnp.repeat(scale_block[..., :-1], GROUP, axis=-1, total_repeat_length=LAT)
    rope_part = jnp.repeat(scale_block[..., -1:], ROPE, axis=-1, total_repeat_length=ROPE)
    return jnp.concatenate([latent_part, rope_part], axis=-1)


def decode_cache(codes, scales):
    return (codes.astype(jnp.float32) * spread_scales(scales.astype(jnp.float32))).astype(
        jnp.bfloat16
    )


def attend_kernel(per, q_ref, new_ref, len_ref, *refs):
    pieces, (o_ref, kv_ref) = refs[:-2], refs[-2:]
    rows, width, heads = q_ref.shape
    total = kv_ref.shape[0]
    block = rows * per
    count = len(pieces) * block
    kv_ref[pl.ds(count, total - count), :] = jnp.zeros((total - count, width), jnp.bfloat16)
    for d, piece in enumerate(pieces):
        kv_ref[pl.ds(d * block, block), :] = piece[:, piece.shape[1] - CHANNELS :][:, :width]
    kv_ref[pl.ds(count, rows), :] = new_ref[...]
    kv = kv_ref[...]
    place = lax.broadcasted_iota(jnp.int32, (total, 1), 0)
    start = jnp.zeros_like(place)
    for d in range(len(pieces)) if len(pieces) > 1 else ():
        start = jnp.where(place // block == d, (lax.axis_index("ep") ^ d) * per, start)
    row_of = place % block // per
    position = start + place % per
    for r in range(rows):
        live = ((place < count) & (row_of == r) & (position < len_ref[r])) | (place == count + r)
        scores = jnp.dot(kv, q_ref[r], preferred_element_type=jnp.float32) * qk_scale
        scores = jnp.where(live, scores, -jnp.inf)
        exponent = jnp.exp(scores - jnp.max(scores, axis=0, keepdims=True))
        weights = exponent / jnp.sum(exponent, axis=0, keepdims=True)
        o_ref[r] = lax.dot_general(
            weights.astype(jnp.bfloat16),
            kv[:, :LAT],
            (((0,), (0,)), ((), ())),
            preferred_element_type=jnp.float32,
        ).astype(jnp.bfloat16)


def attend(queries, new_latent, prompt_lengths, per, pieces):
    rows, heads, width = queries.shape
    count = sum(p.shape[0] for p in pieces)
    total = -(-(count + rows) // 128) * 128
    return pl.pallas_call(
        functools.partial(attend_kernel, per),
        in_specs=[VM, VM, SM] + [VM] * len(pieces),
        out_specs=VM,
        out_shape=jax.ShapeDtypeStruct((rows, heads, LAT), jnp.bfloat16),
        scratch_shapes=[pltpu.VMEM((total, width), jnp.bfloat16)],
        cost_estimate=pl.CostEstimate(
            flops=4 * rows * heads * total * width,
            bytes_accessed=2 * rows * heads * (width + LAT),
            transcendentals=rows * heads * total,
        ),
        compiler_params=pltpu.CompilerParams(vmem_limit_bytes=SCOPE),
        name="attend",
    )(queries.swapaxes(1, 2), new_latent, prompt_lengths, *pieces)


def pack_kernel(codes_ref, scales_ref, tokens_ref, *refs):
    outs, own, lat_ref = refs[:-2], refs[-2], refs[-1]
    rows, per, width = codes_ref.shape
    groups = scales_ref.shape[0]
    block = own.shape[0]
    here, me = lax.axis_index("ep"), lax.axis_index("pf")
    scales = scales_ref[...].astype(jnp.float32)
    lat_ref[:, width:] = jnp.zeros((rows * per, CHANNELS - width), jnp.float32)
    for r in range(rows):
        for g in range(groups):
            columns = slice(g * GROUP, min((g + 1) * GROUP, width))
            lat_ref[r * per : (r + 1) * per, columns] = (
                codes_ref[r, :, columns].astype(jnp.float32) * scales[g, :, r : r + 1]
            )
    half = tokens_ref.shape[1] // 8
    for d in range(len(outs) + 1):
        start = pl.multiple_of((here ^ d) * block, block)
        part = lat_ref[pl.ds(start, block), :].astype(jnp.bfloat16)
        if d == 0:
            own[...] = part
            continue
        outs[d - 1][:, half:] = part
        for c in range(2):
            start = pl.multiple_of((2 * me + c) * half, 128)
            outs[d - 1][c * block // 2 : (c + 1) * block // 2, :half] = tokens_ref[
                :, pl.ds(start, half)
            ]


def pack(codes, scales, tokens, n_ep):
    rows, per, width = codes.shape
    block = rows * per // n_ep
    wide = tokens.shape[1] // 8 + CHANNELS
    return pl.pallas_call(
        pack_kernel,
        in_specs=[VM] * 3,
        out_specs=[VM] * n_ep,
        out_shape=[jax.ShapeDtypeStruct((block, wide), jnp.bfloat16)] * (n_ep - 1)
        + [jax.ShapeDtypeStruct((block, CHANNELS), jnp.bfloat16)],
        scratch_shapes=[pltpu.VMEM((rows * per, CHANNELS), jnp.float32)],
        compiler_params=pltpu.CompilerParams(vmem_limit_bytes=SCOPE),
        name="pack",
    )(codes, scales.transpose(2, 1, 0), tokens)


def merge_kernel(*refs):
    sources, out = refs[:-1], refs[-1]
    rows, half = out.shape[0] // len(sources), out.shape[1] // 2
    for d, source in enumerate(sources):
        for c in range(2):
            out[d * rows : (d + 1) * rows, c * half : (c + 1) * half] = source[
                c * rows : (c + 1) * rows, :half
            ]


def merge(came, rows, half):
    return pl.pallas_call(
        merge_kernel,
        in_specs=[VM] * len(came),
        out_specs=VM,
        out_shape=jax.ShapeDtypeStruct((len(came) * rows, 2 * half), jnp.bfloat16),
        compiler_params=pltpu.CompilerParams(vmem_limit_bytes=SCOPE),
        name="merge",
    )(*came)


def part_copies(b, g_ref, u_ref, g_to, u_to, sems):
    depth = g_to.shape[1]
    start = pl.multiple_of((lax.axis_index("pf") ^ b) * depth, 128)
    return [
        (
            pltpu.make_async_copy(g_ref.at[e, pl.ds(start, depth)], g_to.at[e], sems.at[0, e]),
            pltpu.make_async_copy(u_ref.at[e, pl.ds(start, depth)], u_to.at[e], sems.at[1, e]),
        )
        for e in range(g_to.shape[0])
    ]


def hold_kernel(ids_ref, weight_ref, g_ref, u_ref, go_ref, uo_ref, select_ref, column_ref, sems):
    copies = part_copies(0, g_ref, u_ref, go_ref, uo_ref, sems)
    for pair in copies:
        for copy in pair:
            copy.start()
    top, rows = ids_ref.shape
    experts = g_ref.shape[0]
    here = lax.axis_index("ep")
    pair = lax.broadcasted_iota(jnp.int32, (top * rows, 1), 0)
    ids = jnp.zeros((top * rows, rows), jnp.int32)
    weight = jnp.zeros((top * rows, rows), jnp.float32)
    mine = lax.broadcasted_iota(jnp.int32, (top * rows, rows), 1) == pair // top
    for k in range(top):
        chosen = mine & (pair % top == k)
        ids = jnp.where(chosen, ids_ref[k : k + 1, :], ids)
        weight = jnp.where(chosen, weight_ref[k : k + 1, :], weight)
    ids = jnp.sum(ids, axis=1, keepdims=True)
    column_ref[...] = jnp.sum(weight, axis=1, keepdims=True)
    column = lax.broadcasted_iota(jnp.int32, (1, experts * rows), 1)
    for d in range(select_ref.shape[1] // (experts * rows)):
        match = (ids == (here ^ d) * experts + column // rows) & (column % rows == pair // top)
        select_ref[:, d * experts * rows : (d + 1) * experts * rows] = jnp.where(
            match, 1.0, 0.0
        ).astype(jnp.bfloat16)
    for pair in copies:
        for copy in pair:
            copy.wait()


def hold(expert_ids, routing_weights, w_gate, w_up, n_ep):
    experts, depth, wide = w_gate.shape
    rows, top = expert_ids.shape
    shape = (experts, depth // 4, wide)
    return pl.pallas_call(
        hold_kernel,
        in_specs=[VM, VM, HBM, HBM],
        out_specs=[VM] * 4,
        out_shape=[pltpu.VMEM(shape, jnp.bfloat16)] * 2
        + [
            jax.ShapeDtypeStruct((rows * top, n_ep * experts * rows), jnp.bfloat16),
            jax.ShapeDtypeStruct((rows * top, 1), jnp.float32),
        ],
        scratch_shapes=[pltpu.SemaphoreType.DMA((2, experts))],
        cost_estimate=pl.CostEstimate(
            flops=0, bytes_accessed=4 * experts * shape[1] * wide, transcendentals=0
        ),
        compiler_params=pltpu.CompilerParams(vmem_limit_bytes=SCOPE),
        name="hold",
    )(expert_ids.T, routing_weights.T, w_gate, w_up)


def set_rows(b, x_ref, own_ref, came_ref):
    rows, quarter = own_ref.shape[0], came_ref.shape[1]
    start = pl.multiple_of((lax.axis_index("pf") ^ b) * quarter, 128)
    x_ref[:rows, :] = own_ref[:, pl.ds(start, quarter)]
    x_ref[rows:, :] = came_ref[...]


def times(x_ref, w_ref, e):
    return jnp.dot(x_ref[...], w_ref[e], preferred_element_type=jnp.float32)


def stage_kernel(b, first, own, came, hg, hu, g_hbm, u_hbm, *refs):
    total, (gate, up, g_next, u_next, x_ref, sems) = refs[:-6], refs[-6:]
    copies = part_copies(b + 1, g_hbm, u_hbm, g_next, u_next, sems)
    for pair in copies:
        for copy in pair:
            copy.start()
    set_rows(b, x_ref, own, came)

    @pl.loop(0, hg.shape[0])
    def _(e):
        gate_part, up_part = times(x_ref, hg, e), times(x_ref, hu, e)
        gate[e] = gate_part if first else gate_part + total[0][e]
        up[e] = up_part if first else up_part + total[1][e]

    for pair in copies:
        for copy in pair:
            copy.wait()


def in_vmem(x):
    return pltpu.with_memory_space_constraint(x, pltpu.VMEM)


def stage(b, own, came, held, total, w_gate, w_up):
    experts, depth, wide = w_gate.shape
    rows = own.shape[0] + came.shape[0]
    sums = jax.ShapeDtypeStruct((experts, rows, wide), jnp.float32)
    *total, g_next, u_next = pl.pallas_call(
        functools.partial(stage_kernel, b, not total),
        in_specs=[VM] * 4 + [HBM] * 2 + [VM] * len(total),
        out_specs=[VM] * 4,
        out_shape=[sums] * 2 + [pltpu.VMEM((experts, depth // 4, wide), jnp.bfloat16)] * 2,
        scratch_shapes=[
            pltpu.VMEM((rows, depth // 4), jnp.bfloat16),
            pltpu.SemaphoreType.DMA((2, experts)),
        ],
        cost_estimate=pl.CostEstimate(
            flops=rows * depth * wide * experts,
            bytes_accessed=experts * depth * wide,
            transcendentals=0,
        ),
        compiler_params=pltpu.CompilerParams(vmem_limit_bytes=SCOPE + b * HELD),
        name="stage",
    )(own, came, *map(in_vmem, held), w_gate, w_up, *total)
    return total, (g_next, u_next)


def last_kernel(n_ep, own, came, came_too, hg, hu, g_hbm, u_hbm, gate, up, *refs):
    outs, (gb, ub, x_ref, y_ref, sems) = refs[:-5], refs[-5:]
    experts, part = hg.shape[0], own.shape[0]
    copies = part_copies(3, g_hbm, u_hbm, gb, ub, sems)
    for pair in copies:
        for copy in pair:
            copy.start()
    set_rows(2, x_ref, own, came)
    set_rows(3, y_ref, own, came_too)
    for e in range(experts):
        gate_part = gate[e] + times(x_ref, hg, e)
        up_part = up[e] + times(x_ref, hu, e)
        for copy in copies[e]:
            copy.wait()
        gate_part += times(y_ref, gb, e)
        up_part += times(y_ref, ub, e)
        hidden = (gate_part * jax.nn.sigmoid(gate_part) * up_part).astype(jnp.bfloat16)
        for d in range(n_ep):
            outs[d][e] = hidden[d * part : (d + 1) * part]


def last(n_ep, own, came, came_too, held, total, w_gate, w_up):
    experts, depth, wide = w_gate.shape
    rows = own.shape[0] + came.shape[0]
    out = jax.ShapeDtypeStruct((experts, own.shape[0], wide), jnp.bfloat16)
    return pl.pallas_call(
        functools.partial(last_kernel, n_ep),
        in_specs=[VM] * 5 + [HBM] * 2 + [VM] * 2,
        out_specs=[VM] * n_ep,
        out_shape=[out] * n_ep,
        scratch_shapes=[
            pltpu.VMEM((experts, depth // 4, wide), jnp.bfloat16),
            pltpu.VMEM((experts, depth // 4, wide), jnp.bfloat16),
            pltpu.VMEM((rows, depth // 4), jnp.bfloat16),
            pltpu.VMEM((rows, depth // 4), jnp.bfloat16),
            pltpu.SemaphoreType.DMA((2, experts)),
        ],
        cost_estimate=pl.CostEstimate(
            flops=2 * rows * depth * wide * experts,
            bytes_accessed=experts * depth * wide,
            transcendentals=experts * rows * wide,
        ),
        compiler_params=pltpu.CompilerParams(vmem_limit_bytes=SCOPE + 2 * HELD),
        name="last",
    )(own, came, came_too, *map(in_vmem, held), w_gate, w_up, *total)


def pick_kernel(select_ref, column_ref, *refs):
    blocks, o_ref = refs[:-1], refs[-1]
    experts, rows, wide = blocks[0].shape
    total = jnp.zeros((select_ref.shape[0], wide), jnp.float32)
    for d, block in enumerate(blocks):
        total += jnp.dot(
            select_ref[:, d * experts * rows : (d + 1) * experts * rows],
            block[...].reshape(experts * rows, wide),
            preferred_element_type=jnp.float32,
        )
    o_ref[...] = (total * column_ref[...]).astype(jnp.bfloat16)


def pick(select, column, blocks):
    pairs, wide = select.shape[0], blocks[0].shape[2]
    return pl.pallas_call(
        pick_kernel,
        in_specs=[VM] * (2 + len(blocks)),
        out_specs=VM,
        out_shape=jax.ShapeDtypeStruct((pairs, wide), jnp.bfloat16),
        compiler_params=pltpu.CompilerParams(vmem_limit_bytes=SCOPE),
        name="pick",
    )(select, column, *blocks)


def crossed(x, axis, bit):
    n = lax.axis_size(axis)
    return lax.ppermute(x, axis, [(s, s ^ bit) for s in range(n)])


def local_ring(
    cache_codes,
    cache_scales,
    queries,
    new_latent,
    prompt_lengths,
    tokens,
    expert_ids,
    routing_weights,
    w_gate,
    w_up,
):
    n_ep = lax.axis_size("ep")
    per = cache_codes.shape[1]
    half = tokens.shape[1] // 8
    rows = tokens.shape[0]
    *sent, own_piece = pack(cache_codes, cache_scales, tokens, n_ep)
    came = [crossed(x, "ep", d) for d, x in enumerate(sent, 1)]
    w_gate, w_up = [pltpu.with_memory_space_constraint(w, pltpu.HBM) for w in (w_gate, w_up)]
    *held, select, column = hold(expert_ids, routing_weights, w_gate, w_up, n_ep)
    came, held, select, column = lax.optimization_barrier((came, held, select, column))
    x0 = merge(came, rows, half)
    x1 = crossed(x0, "pf", 1)
    x2 = crossed(x0, "pf", 2)
    x3 = crossed(x0, "pf", 3)
    total, held = stage(0, tokens, x0, held, (), w_gate, w_up)
    total, held = stage(1, tokens, x1, held, total, w_gate, w_up)
    blocks = last(n_ep, tokens, x2, x3, held, total, w_gate, w_up)
    back = [blocks[0]] + [crossed(blocks[d], "ep", d) for d in range(1, n_ep)]
    attention_out = attend(queries, new_latent, prompt_lengths, per, [own_piece] + came)
    moe_hidden = pick(select, column, back)
    return attention_out, moe_hidden.reshape(rows, -1, moe_hidden.shape[1])


def local_wide(
    cache_codes,
    cache_scales,
    queries,
    new_latent,
    prompt_lengths,
    tokens,
    expert_ids,
    routing_weights,
    w_gate,
    w_up,
):
    latent = decode_cache(cache_codes, cache_scales)
    cache = lax.all_to_all(latent, "ep", split_axis=0, concat_axis=1, tiled=True)
    per = cache.shape[1]
    cache = jnp.pad(cache, ((0, 0), (0, 0), (0, CHANNELS - cache.shape[2])))
    cache = cache.reshape(-1, CHANNELS)
    attention_out = attend(queries, new_latent, prompt_lengths, per, [cache])
    x = lax.all_gather(tokens, "ep", axis=0, tiled=True)
    gate = jnp.einsum("rd,edf->erf", x, w_gate, preferred_element_type=jnp.float32)
    up = jnp.einsum("rd,edf->erf", x, w_up, preferred_element_type=jnp.float32)
    hidden = (jax.nn.silu(gate) * up).astype(jnp.bfloat16)
    back = lax.all_to_all(hidden, "ep", split_axis=1, concat_axis=0, tiled=True)
    match = expert_ids[:, :, None] == jnp.arange(back.shape[0], dtype=jnp.int32)
    picked = jnp.einsum(
        "rke,erf->rkf", match.astype(jnp.bfloat16), back, preferred_element_type=jnp.float32
    )
    return attention_out, (picked * routing_weights[:, :, None]).astype(jnp.bfloat16)


def solution(mesh):
    near = mesh.shape["ep"] == 4 and mesh.shape["pf"] == 4
    return jax.shard_map(
        local_ring if near else local_wide,
        mesh=mesh,
        in_specs=(
            P(("groups", "pf"), "ep", None),
            P(("groups", "pf"), "ep", None),
            P(("groups", "pf", "ep"), None, None),
            P(("groups", "pf", "ep"), None),
            P(("groups", "pf", "ep")),
            P(("groups", "ep"), None),
            P(("groups", "ep"), None),
            P(("groups", "ep"), None),
            P("ep", None, "pf"),
            P("ep", None, "pf"),
        ),
        out_specs=(P(("groups", "pf", "ep"), None, None), P(("groups", "ep"), None, "pf")),
        check_vma=False,
    )
```

```python
import functools

import jax
import jax.numpy as jnp
from jax import lax
from jax.experimental import pallas as pl
from jax.experimental.pallas import tpu as pltpu
from jax.sharding import PartitionSpec as P

LAT = 512
ROPE = 64
GROUP = 128
TOP = 8
EARLY = 2
CHANNELS = 640
SCOPE = 4 << 20
ORDER = (2, 3, 1)
HELD = 14 << 20

qk_scale = 192.0 ** (-0.5)
VM = pl.BlockSpec(memory_space=pltpu.VMEM)
SM = pl.BlockSpec(memory_space=pltpu.SMEM)
HBM = pl.BlockSpec(memory_space=pltpu.HBM)


def spread_scales(scale_block):
    latent_part = jnp.repeat(scale_block[..., :-1], GROUP, axis=-1, total_repeat_length=LAT)
    rope_part = jnp.repeat(scale_block[..., -1:], ROPE, axis=-1, total_repeat_length=ROPE)
    return jnp.concatenate([latent_part, rope_part], axis=-1)


def decode_cache(codes, scales):
    return (codes.astype(jnp.float32) * spread_scales(scales.astype(jnp.float32))).astype(
        jnp.bfloat16
    )


def attend_kernel(per, q_ref, new_ref, len_ref, *refs):
    pieces, (o_ref, kv_ref) = refs[:-2], refs[-2:]
    rows, width, heads = q_ref.shape
    total = kv_ref.shape[0]
    block = rows * per
    count = len(pieces) * block
    kv_ref[pl.ds(count, total - count), :] = jnp.zeros((total - count, width), jnp.bfloat16)
    for d, piece in enumerate(pieces):
        kv_ref[pl.ds(d * block, block), :] = piece[:, piece.shape[1] - CHANNELS :][:, :width]
    kv_ref[pl.ds(count, rows), :] = new_ref[...]
    kv = kv_ref[...]
    place = lax.broadcasted_iota(jnp.int32, (total, 1), 0)
    start = jnp.zeros_like(place)
    for d in range(len(pieces)) if len(pieces) > 1 else ():
        start = jnp.where(place // block == d, (lax.axis_index("ep") ^ d) * per, start)
    row_of = place % block // per
    position = start + place % per
    for r in range(rows):
        live = ((place < count) & (row_of == r) & (position < len_ref[r])) | (place == count + r)
        scores = jnp.dot(kv, q_ref[r], preferred_element_type=jnp.float32) * qk_scale
        scores = jnp.where(live, scores, -jnp.inf)
        exponent = jnp.exp(scores - jnp.max(scores, axis=0, keepdims=True))
        weights = exponent / jnp.sum(exponent, axis=0, keepdims=True)
        o_ref[r] = lax.dot_general(
            weights.astype(jnp.bfloat16),
            kv[:, :LAT],
            (((0,), (0,)), ((), ())),
            preferred_element_type=jnp.float32,
        ).astype(jnp.bfloat16)


def attend(queries, new_latent, prompt_lengths, per, pieces):
    rows, heads, width = queries.shape
    count = sum(p.shape[0] for p in pieces)
    total = -(-(count + rows) // 128) * 128
    return pl.pallas_call(
        functools.partial(attend_kernel, per),
        in_specs=[VM, VM, SM] + [VM] * len(pieces),
        out_specs=VM,
        out_shape=jax.ShapeDtypeStruct((rows, heads, LAT), jnp.bfloat16),
        scratch_shapes=[pltpu.VMEM((total, width), jnp.bfloat16)],
        cost_estimate=pl.CostEstimate(
            flops=4 * rows * heads * total * width,
            bytes_accessed=2 * rows * heads * (width + LAT),
            transcendentals=rows * heads * total,
        ),
        compiler_params=pltpu.CompilerParams(vmem_limit_bytes=SCOPE),
        name="attend",
    )(queries.swapaxes(1, 2), new_latent, prompt_lengths, *pieces)


def pack_kernel(codes_hbm, scales_hbm, tokens_hbm, ids_hbm, *refs):
    outs, own, (codes_ref, scales_ref, ids_ref, lat_ref, sems, token_sems) = (
        refs[:-7],
        refs[-7],
        refs[-6:],
    )
    rows, per, width = codes_ref.shape
    groups = scales_ref.shape[0]
    block = own.shape[0]
    half = tokens_hbm.shape[1] // 8
    here, me = lax.axis_index("ep"), lax.axis_index("pf")
    cache = [
        pltpu.make_async_copy(codes_hbm, codes_ref, sems.at[0]),
        pltpu.make_async_copy(scales_hbm, scales_ref, sems.at[1]),
        pltpu.make_async_copy(ids_hbm, ids_ref, sems.at[2]),
    ]
    token_copies = []
    for d, out in enumerate(outs):
        for c in range(2):
            start = pl.multiple_of((2 * me + c) * half, 128)
            token_copies.append(
                pltpu.make_async_copy(
                    tokens_hbm.at[:, pl.ds(start, half)],
                    out.at[pl.ds(c * block // 2, block // 2), pl.ds(0, half)],
                    token_sems.at[d, c],
                )
            )
    for copy in cache + token_copies:
        copy.start()
    lat_ref[:, width:] = jnp.zeros((rows * per, CHANNELS - width), jnp.float32)
    for copy in cache:
        copy.wait()
    scales = scales_ref[...].astype(jnp.float32)
    top, named = ids_ref.shape
    for d in range(len(outs) + 1):
        lat_ref[d * block : d * block + top, width : width + named] = ids_ref[...].astype(
            jnp.float32
        )
    for r in range(rows):
        for g in range(groups):
            columns = slice(g * GROUP, min((g + 1) * GROUP, width))
            lat_ref[r * per : (r + 1) * per, columns] = (
                codes_ref[r, :, columns].astype(jnp.float32) * scales[g, :, r : r + 1]
            )
    for d in range(len(outs) + 1):
        start = pl.multiple_of((here ^ d) * block, block)
        part = lat_ref[pl.ds(start, block), :].astype(jnp.bfloat16)
        if d == 0:
            own[...] = part
        else:
            outs[ORDER.index(d)][:, half:] = part
    for copy in token_copies:
        copy.wait()


def in_hbm(x):
    return pltpu.with_memory_space_constraint(x, pltpu.HBM)


def in_vmem(x):
    return pltpu.with_memory_space_constraint(x, pltpu.VMEM)


def pack(codes, scales, tokens, expert_ids, n_ep):
    rows, per, width = codes.shape
    block = rows * per // n_ep
    wide = tokens.shape[1] // 8 + CHANNELS
    scales, ids = scales.transpose(2, 1, 0), expert_ids.T
    return pl.pallas_call(
        pack_kernel,
        in_specs=[HBM] * 4,
        out_specs=[VM] * n_ep,
        out_shape=[jax.ShapeDtypeStruct((block, wide), jnp.bfloat16)] * (n_ep - 1)
        + [jax.ShapeDtypeStruct((block, CHANNELS), jnp.bfloat16)],
        scratch_shapes=[
            pltpu.VMEM(codes.shape, jnp.bfloat16),
            pltpu.VMEM(scales.shape, jnp.bfloat16),
            pltpu.VMEM(ids.shape, jnp.int32),
            pltpu.VMEM((rows * per, CHANNELS), jnp.float32),
            pltpu.SemaphoreType.DMA((3,)),
            pltpu.SemaphoreType.DMA((n_ep - 1, 2)),
        ],
        compiler_params=pltpu.CompilerParams(vmem_limit_bytes=SCOPE),
        name="pack",
    )(in_hbm(codes), in_hbm(scales), in_hbm(tokens), in_hbm(ids))


def merge_kernel(*refs):
    sources, out = refs[:-1], refs[-1]
    rows, half = out.shape[0] // len(sources), out.shape[1] // 2
    for d, source in enumerate(sources):
        for c in range(2):
            out[d * rows : (d + 1) * rows, c * half : (c + 1) * half] = source[
                c * rows : (c + 1) * rows, :half
            ]


def merge(came, rows, half):
    return pl.pallas_call(
        merge_kernel,
        in_specs=[VM] * len(came),
        out_specs=VM,
        out_shape=jax.ShapeDtypeStruct((len(came) * rows, 2 * half), jnp.bfloat16),
        compiler_params=pltpu.CompilerParams(vmem_limit_bytes=SCOPE),
        name="merge",
    )(*came)


def part_copies(b, first, g_ref, u_ref, g_to, u_to, sems):
    depth = g_to.shape[1]
    start = pl.multiple_of((lax.axis_index("pf") ^ b) * depth, 128)
    rows = pl.ds(start, depth)
    return [
        (
            pltpu.make_async_copy(g_ref.at[first + e, rows], g_to.at[e], sems.at[0, e]),
            pltpu.make_async_copy(u_ref.at[first + e, rows], u_to.at[e], sems.at[1, e]),
        )
        for e in range(g_to.shape[0])
    ]


def start_all(pairs):
    for pair in pairs:
        for copy in pair:
            copy.start()


def wait_all(pairs):
    for pair in pairs:
        for copy in pair:
            copy.wait()


def hold_kernel(ids_hbm, weight_hbm, g_ref, u_ref, *refs):
    own_gate, own_up, next_gate, next_up, select_ref, column_ref = refs[:6]
    ids_ref, weight_ref, few_sems, sems, next_sems = refs[6:]
    few = [
        (
            pltpu.make_async_copy(ids_hbm, ids_ref, few_sems.at[0]),
            pltpu.make_async_copy(weight_hbm, weight_ref, few_sems.at[1]),
        )
    ]
    copies = part_copies(0, 0, g_ref, u_ref, own_gate, own_up, sems)
    copies += part_copies(1, 0, g_ref, u_ref, next_gate, next_up, next_sems)
    start_all(few)
    start_all(copies)
    wait_all(few)
    top, rows = ids_ref.shape
    experts = g_ref.shape[0]
    slots = rows // 2
    here = lax.axis_index("ep")
    pair = lax.broadcasted_iota(jnp.int32, (top * rows, 1), 0)
    other = lax.broadcasted_iota(jnp.int32, (top * rows, rows), 1)
    ids = jnp.zeros((top * rows, rows), jnp.int32)
    weight = jnp.zeros((top * rows, rows), jnp.float32)
    for k in range(top):
        chosen = (other == pair // top) & (pair % top == k)
        ids = jnp.where(chosen, ids_ref[k : k + 1, :], ids)
        weight = jnp.where(chosen, weight_ref[k : k + 1, :], weight)
    ids = jnp.sum(ids, axis=1, keepdims=True)
    column_ref[...] = jnp.sum(weight, axis=1, keepdims=True)
    earlier = jnp.zeros((top * rows, rows), jnp.int32)
    for k in range(top):
        earlier += jnp.where((ids_ref[k : k + 1, :] == ids) & (other < pair // top), 1, 0)
    slot = jnp.sum(earlier, axis=1, keepdims=True)
    column = lax.broadcasted_iota(jnp.int32, (1, experts * slots), 1)
    for i, d in enumerate((0,) + ORDER):
        match = (ids == (here ^ d) * experts + column // slots) & (column % slots == slot)
        select_ref[:, i * experts * slots : (i + 1) * experts * slots] = jnp.where(
            match, 1.0, 0.0
        ).astype(jnp.bfloat16)
    wait_all(copies)


def hold(expert_ids, routing_weights, w_gate, w_up, n_ep):
    experts, depth, wide = w_gate.shape
    rows, top = expert_ids.shape
    shapes = [(n, depth // 4, wide) for n in (experts, experts, EARLY, EARLY)]
    return pl.pallas_call(
        hold_kernel,
        in_specs=[HBM] * 4,
        out_specs=[VM] * 6,
        out_shape=[pltpu.VMEM(shape, jnp.bfloat16) for shape in shapes]
        + [
            jax.ShapeDtypeStruct((rows * top, n_ep * experts * rows // 2), jnp.bfloat16),
            jax.ShapeDtypeStruct((rows * top, 1), jnp.float32),
        ],
        scratch_shapes=[
            pltpu.VMEM((top, rows), jnp.int32),
            pltpu.VMEM((top, rows), jnp.float32),
            pltpu.SemaphoreType.DMA((2,)),
            pltpu.SemaphoreType.DMA((2, experts)),
            pltpu.SemaphoreType.DMA((2, EARLY)),
        ],
        cost_estimate=pl.CostEstimate(
            flops=0, bytes_accessed=(experts + EARLY) * depth * wide, transcendentals=0
        ),
        compiler_params=pltpu.CompilerParams(vmem_limit_bytes=SCOPE),
        name="hold",
    )(in_hbm(expert_ids.T), in_hbm(routing_weights.T), w_gate, w_up)


def set_rows(b, x_ref, own_ref, came_ref):
    rows, quarter = own_ref.shape[0], came_ref.shape[1]
    start = pl.multiple_of((lax.axis_index("pf") ^ b) * quarter, 128)
    x_ref[:rows, :] = own_ref[:, pl.ds(start, quarter)]
    x_ref[rows:, :] = came_ref[...]


def times(x_ref, w_ref, e):
    return jnp.dot(x_ref[...], w_ref[e], preferred_element_type=jnp.float32)


def set_slots(pieces, slots_ref, experts, rows, top):
    n_ep = len(pieces)
    slots = rows // 2
    wide = CHANNELS - LAT
    ids = jnp.zeros((top, n_ep * rows), jnp.float32)
    for d, piece in enumerate(pieces):
        tail = piece[: 2 * top, piece.shape[1] - wide :][:top]
        lane = lax.broadcasted_iota(jnp.int32, (wide, n_ep * rows), 0)
        column = lax.broadcasted_iota(jnp.int32, (wide, n_ep * rows), 1)
        take = (lane == ROPE + column % rows) & (column // rows == d)
        ids += jnp.dot(
            tail, jnp.where(take, 1.0, 0.0).astype(jnp.bfloat16), preferred_element_type=jnp.float32
        )
    shape = slots_ref.shape
    place = lax.broadcasted_iota(jnp.int32, shape, 0)
    column = lax.broadcasted_iota(jnp.int32, shape, 1)
    expert = lax.axis_index("ep") * experts + place // (n_ep * slots)
    named = jnp.zeros(shape, jnp.float32)
    for k in range(top):
        named += jnp.where(ids[k : k + 1, :].astype(jnp.int32) == expert, 1.0, 0.0)
    named = jnp.where(place % (n_ep * slots) // slots == column // rows, named, 0.0)
    above = lax.broadcasted_iota(jnp.int32, (n_ep * rows,) * 2, 0)
    below = lax.broadcasted_iota(jnp.int32, (n_ep * rows,) * 2, 1)
    before = jnp.where((above // rows == below // rows) & (above < below), 1.0, 0.0)
    rank = jnp.dot(
        named.astype(jnp.bfloat16), before.astype(jnp.bfloat16), preferred_element_type=jnp.float32
    )
    slot = (place % slots).astype(jnp.float32)
    slots_ref[...] = jnp.where((named > 0.5) & (rank == slot), 1.0, 0.0).astype(jnp.bfloat16)


def first_kernel(own, came, hg, hu, next_gate, next_up, g_hbm, u_hbm, *refs):
    pieces, (gate, up, g_to, u_to, slots_ref, x_ref, sems) = refs[:-7], refs[-7:]
    experts = hg.shape[0]
    copies = part_copies(1, EARLY, g_hbm, u_hbm, g_to, u_to, sems)
    start_all(copies)
    set_rows(0, x_ref, own, came)

    @pl.loop(0, experts)
    def _(e):
        gate[e] = times(x_ref, hg, e)
        up[e] = times(x_ref, hu, e)

    set_slots(pieces, slots_ref, experts, own.shape[0], TOP)
    wait_all(copies)


def second_kernel(own, came, hg, hu, mg, mu, g_hbm, u_hbm, gate_in, up_in, *refs):
    gate, up, g_to, u_to, x_ref, sems = refs
    copies = part_copies(2, 0, g_hbm, u_hbm, g_to, u_to, sems)
    start_all(copies)
    set_rows(1, x_ref, own, came)
    done = 0
    for g_from, u_from in ((hg, hu), (mg, mu)):

        @pl.loop(0, g_from.shape[0])
        def _(e):
            at = done + e
            gate[at] = gate_in[at] + times(x_ref, g_from, e)
            up[at] = up_in[at] + times(x_ref, u_from, e)

        done += g_from.shape[0]
    wait_all(copies)


def stages(own, x0, x1, held, pieces, w_gate, w_up):
    experts, depth, wide = w_gate.shape
    rows = own.shape[0] + x0.shape[0]
    part = depth // 4
    later = experts - EARLY
    sums = [jax.ShapeDtypeStruct((experts, rows, wide), jnp.float32)] * 2
    weights = [pltpu.VMEM((later, part, wide), jnp.bfloat16)] * 2
    scratch = [pltpu.VMEM((rows, part), jnp.bfloat16), pltpu.SemaphoreType.DMA((2, later))]
    cost = pl.CostEstimate(
        flops=rows * depth * wide * experts,
        bytes_accessed=later * depth * wide,
        transcendentals=0,
    )
    held = [in_vmem(x) for x in held]
    gate, up, mid_gate, mid_up, slots = pl.pallas_call(
        first_kernel,
        in_specs=[VM] * 6 + [HBM] * 2 + [VM] * len(pieces),
        out_specs=[VM] * 5,
        out_shape=sums
        + weights
        + [jax.ShapeDtypeStruct((experts * rows // 2, rows), jnp.bfloat16)],
        scratch_shapes=scratch,
        cost_estimate=cost,
        compiler_params=pltpu.CompilerParams(vmem_limit_bytes=SCOPE),
        name="first",
    )(own, x0, *held, w_gate, w_up, *pieces)
    gate, up, *weights = pl.pallas_call(
        second_kernel,
        in_specs=[VM] * 6 + [HBM] * 2 + [VM] * 2,
        out_specs=[VM] * 4,
        out_shape=sums + weights,
        scratch_shapes=scratch,
        cost_estimate=cost,
        compiler_params=pltpu.CompilerParams(vmem_limit_bytes=SCOPE + HELD),
        name="second",
    )(own, x1, *held[2:], in_vmem(mid_gate), in_vmem(mid_up), w_gate, w_up, gate, up)
    return gate, up, weights, slots


def last_kernel(n_ep, own, came, came_too, hg, hu, g_hbm, u_hbm, gate, up, slots_ref, *refs):
    outs, (tg, tu, gb, ub, x_ref, y_ref, few_sems, sems) = refs[:-8], refs[-8:]
    experts, held = gate.shape[0], hg.shape[0]
    slots = outs[0].shape[1]
    copies = part_copies(3, 0, g_hbm, u_hbm, gb, ub, sems)
    few = part_copies(2, held, g_hbm, u_hbm, tg, tu, few_sems)
    start_all(copies[:held])
    for pairs in zip(few, copies[held:]):
        start_all(pairs)
    set_rows(2, x_ref, own, came)
    set_rows(3, y_ref, own, came_too)
    for e in range(experts):
        if e < held:
            gate_part = gate[e] + times(x_ref, hg, e)
            up_part = up[e] + times(x_ref, hu, e)
        else:
            wait_all(few[e - held : e - held + 1])
            gate_part = gate[e] + times(x_ref, tg, e - held)
            up_part = up[e] + times(x_ref, tu, e - held)
        wait_all(copies[e : e + 1])
        gate_part += times(y_ref, gb, e)
        up_part += times(y_ref, ub, e)
        hidden = (gate_part * jax.nn.sigmoid(gate_part) * up_part).astype(jnp.bfloat16)
        back = jnp.dot(
            slots_ref[e * n_ep * slots : (e + 1) * n_ep * slots, :],
            hidden,
            preferred_element_type=jnp.float32,
        ).astype(jnp.bfloat16)
        for d in range(n_ep):
            outs[d][e] = back[d * slots : (d + 1) * slots]


def last(n_ep, own, came, came_too, held, gate, up, slots, w_gate, w_up):
    experts, depth, wide = w_gate.shape
    rows, part = own.shape[0] + came.shape[0], depth // 4
    rest = experts - held[0].shape[0]
    out = jax.ShapeDtypeStruct((experts, own.shape[0] // 2, wide), jnp.bfloat16)
    return pl.pallas_call(
        functools.partial(last_kernel, n_ep),
        in_specs=[VM] * 5 + [HBM] * 2 + [VM] * 3,
        out_specs=[VM] * n_ep,
        out_shape=[out] * n_ep,
        scratch_shapes=[pltpu.VMEM((n, part, wide), jnp.bfloat16) for n in (rest, rest, experts, experts)]
        + [pltpu.VMEM((rows, part), jnp.bfloat16)] * 2
        + [pltpu.SemaphoreType.DMA((2, rest)), pltpu.SemaphoreType.DMA((2, experts))],
        cost_estimate=pl.CostEstimate(
            flops=2 * rows * depth * wide * experts,
            bytes_accessed=(experts + rest) * depth * wide,
            transcendentals=experts * rows * wide,
        ),
        compiler_params=pltpu.CompilerParams(vmem_limit_bytes=SCOPE + 2 * HELD),
        name="last",
    )(own, came, came_too, *[in_vmem(x) for x in held], w_gate, w_up, gate, up, slots)


def pick_kernel(select_ref, column_ref, *refs):
    blocks, o_ref = refs[:-1], refs[-1]
    experts, rows, wide = blocks[0].shape
    total = jnp.zeros((select_ref.shape[0], wide), jnp.float32)
    for d, block in enumerate(blocks):
        total += jnp.dot(
            select_ref[:, d * experts * rows : (d + 1) * experts * rows],
            block[...].reshape(experts * rows, wide),
            preferred_element_type=jnp.float32,
        )
    o_ref[...] = (total * column_ref[...]).astype(jnp.bfloat16)


def pick(select, column, blocks):
    pairs, wide = select.shape[0], blocks[0].shape[2]
    return pl.pallas_call(
        pick_kernel,
        in_specs=[VM] * (2 + len(blocks)),
        out_specs=VM,
        out_shape=jax.ShapeDtypeStruct((pairs, wide), jnp.bfloat16),
        compiler_params=pltpu.CompilerParams(vmem_limit_bytes=SCOPE),
        name="pick",
    )(select, column, *blocks)


def crossed(x, axis, bit):
    n = lax.axis_size(axis)
    return lax.ppermute(x, axis, [(s, s ^ bit) for s in range(n)])


def local_ring(
    cache_codes,
    cache_scales,
    queries,
    new_latent,
    prompt_lengths,
    tokens,
    expert_ids,
    routing_weights,
    w_gate,
    w_up,
):
    n_ep = lax.axis_size("ep")
    per = cache_codes.shape[1]
    half = tokens.shape[1] // 8
    rows = tokens.shape[0]
    *sent, own_piece = pack(cache_codes, cache_scales, tokens, expert_ids, n_ep)
    came = [crossed(x, "ep", d) for d, x in zip(ORDER, sent)]
    w_gate, w_up = in_hbm(w_gate), in_hbm(w_up)
    *held, select, column = hold(expert_ids, routing_weights, w_gate, w_up, n_ep)
    came, held, select, column = lax.optimization_barrier((came, held, select, column))
    came = [came[ORDER.index(d)] for d in range(1, n_ep)]
    x0 = merge(came, rows, half)
    x1 = crossed(x0, "pf", 1)
    x2 = crossed(x0, "pf", 2)
    x3 = crossed(x0, "pf", 3)
    pieces = [own_piece] + came
    gate, up, held, slots = stages(tokens, x0, x1, held, pieces, w_gate, w_up)
    blocks = last(n_ep, tokens, x2, x3, held, gate, up, slots, w_gate, w_up)
    back = [blocks[0]] + [crossed(blocks[d], "ep", d) for d in ORDER]
    attention_out = attend(queries, new_latent, prompt_lengths, per, pieces)
    moe_hidden = pick(select, column, back)
    return attention_out, moe_hidden.reshape(rows, -1, moe_hidden.shape[1])


def local_wide(
    cache_codes,
    cache_scales,
    queries,
    new_latent,
    prompt_lengths,
    tokens,
    expert_ids,
    routing_weights,
    w_gate,
    w_up,
):
    latent = decode_cache(cache_codes, cache_scales)
    cache = lax.all_to_all(latent, "ep", split_axis=0, concat_axis=1, tiled=True)
    per = cache.shape[1]
    cache = jnp.pad(cache, ((0, 0), (0, 0), (0, CHANNELS - cache.shape[2])))
    cache = cache.reshape(-1, CHANNELS)
    attention_out = attend(queries, new_latent, prompt_lengths, per, [cache])
    x = lax.all_gather(tokens, "ep", axis=0, tiled=True)
    gate = jnp.einsum("rd,edf->erf", x, w_gate, preferred_element_type=jnp.float32)
    up = jnp.einsum("rd,edf->erf", x, w_up, preferred_element_type=jnp.float32)
    hidden = (jax.nn.silu(gate) * up).astype(jnp.bfloat16)
    back = lax.all_to_all(hidden, "ep", split_axis=1, concat_axis=0, tiled=True)
    match = expert_ids[:, :, None] == jnp.arange(back.shape[0], dtype=jnp.int32)
    picked = jnp.einsum(
        "rke,erf->rkf", match.astype(jnp.bfloat16), back, preferred_element_type=jnp.float32
    )
    return attention_out, (picked * routing_weights[:, :, None]).astype(jnp.bfloat16)


def solution(mesh):
    near = mesh.shape["ep"] == 4 and mesh.shape["pf"] == 4
    return jax.shard_map(
        local_ring if near else local_wide,
        mesh=mesh,
        in_specs=(
            P(("groups", "pf"), "ep", None),
            P(("groups", "pf"), "ep", None),
            P(("groups", "pf", "ep"), None, None),
            P(("groups", "pf", "ep"), None),
            P(("groups", "pf", "ep")),
            P(("groups", "ep"), None),
            P(("groups", "ep"), None),
            P(("groups", "ep"), None),
            P("ep", None, "pf"),
            P("ep", None, "pf"),
        ),
        out_specs=(P(("groups", "pf", "ep"), None, None), P(("groups", "ep"), None, "pf")),
        check_vma=False,
    )
```

```python
import functools

import jax
import jax.numpy as jnp
from jax import lax
from jax.experimental import pallas as pl
from jax.experimental.pallas import tpu as pltpu
from jax.sharding import PartitionSpec as P

LAT = 512
ROPE = 64
GROUP = 128
TOP = 8
EARLY = 2
AHEAD = 6
CHANNELS = 640
SCOPE = 4 << 20
GRANT = 16 << 20
ORDER = (3, 2, 1)
HELD = 14 << 20

qk_scale = 192.0 ** (-0.5)
VM = pl.BlockSpec(memory_space=pltpu.VMEM)
SM = pl.BlockSpec(memory_space=pltpu.SMEM)
HBM = pl.BlockSpec(memory_space=pltpu.HBM)


def spread_scales(scale_block):
    latent_part = jnp.repeat(scale_block[..., :-1], GROUP, axis=-1, total_repeat_length=LAT)
    rope_part = jnp.repeat(scale_block[..., -1:], ROPE, axis=-1, total_repeat_length=ROPE)
    return jnp.concatenate([latent_part, rope_part], axis=-1)


def decode_cache(codes, scales):
    return (codes.astype(jnp.float32) * spread_scales(scales.astype(jnp.float32))).astype(
        jnp.bfloat16
    )


def attend_kernel(per, q_ref, new_ref, len_ref, *refs):
    pieces, (o_ref, kv_ref) = refs[:-2], refs[-2:]
    rows, width, heads = q_ref.shape
    total = kv_ref.shape[0]
    block = rows * per
    count = len(pieces) * block
    kv_ref[pl.ds(count, total - count), :] = jnp.zeros((total - count, width), jnp.bfloat16)
    for d, piece in enumerate(pieces):
        kv_ref[pl.ds(d * block, block), :] = piece[:, piece.shape[1] - CHANNELS :][:, :width]
    kv_ref[pl.ds(count, rows), :] = new_ref[...]
    kv = kv_ref[...]
    place = lax.broadcasted_iota(jnp.int32, (total, 1), 0)
    start = jnp.zeros_like(place)
    for d in range(len(pieces)) if len(pieces) > 1 else ():
        start = jnp.where(place // block == d, (lax.axis_index("ep") ^ d) * per, start)
    row_of = place % block // per
    position = start + place % per
    for r in range(rows):
        live = ((place < count) & (row_of == r) & (position < len_ref[r])) | (place == count + r)
        scores = jnp.dot(kv, q_ref[r], preferred_element_type=jnp.float32) * qk_scale
        scores = jnp.where(live, scores, -jnp.inf)
        exponent = jnp.exp(scores - jnp.max(scores, axis=0, keepdims=True))
        weights = exponent / jnp.sum(exponent, axis=0, keepdims=True)
        o_ref[r] = lax.dot_general(
            weights.astype(jnp.bfloat16),
            kv[:, :LAT],
            (((0,), (0,)), ((), ())),
            preferred_element_type=jnp.float32,
        ).astype(jnp.bfloat16)


def attend(queries, new_latent, prompt_lengths, per, pieces):
    rows, heads, width = queries.shape
    count = sum(p.shape[0] for p in pieces)
    total = -(-(count + rows) // 128) * 128
    return pl.pallas_call(
        functools.partial(attend_kernel, per),
        in_specs=[VM, VM, SM] + [VM] * len(pieces),
        out_specs=VM,
        out_shape=jax.ShapeDtypeStruct((rows, heads, LAT), jnp.bfloat16),
        scratch_shapes=[pltpu.VMEM((total, width), jnp.bfloat16)],
        cost_estimate=pl.CostEstimate(
            flops=4 * rows * heads * total * width,
            bytes_accessed=2 * rows * heads * (width + LAT),
            transcendentals=rows * heads * total,
        ),
        compiler_params=pltpu.CompilerParams(vmem_limit_bytes=SCOPE),
        name="attend",
    )(queries.swapaxes(1, 2), new_latent, prompt_lengths, *pieces)


def pack_kernel(codes_hbm, scales_hbm, tokens_hbm, ids_hbm, *refs):
    outs, own, (codes_ref, scales_ref, ids_ref, lat_ref, sems, token_sems) = (
        refs[:-7],
        refs[-7],
        refs[-6:],
    )
    rows, per, width = codes_ref.shape
    groups = scales_ref.shape[0]
    block = own.shape[0]
    half = tokens_hbm.shape[1] // 8
    here, me = lax.axis_index("ep"), lax.axis_index("pf")
    cache = [
        pltpu.make_async_copy(codes_hbm, codes_ref, sems.at[0]),
        pltpu.make_async_copy(scales_hbm, scales_ref, sems.at[1]),
        pltpu.make_async_copy(ids_hbm, ids_ref, sems.at[2]),
    ]
    token_copies = []
    for d, out in enumerate(outs):
        for c in range(2):
            start = pl.multiple_of((2 * me + c) * half, 128)
            token_copies.append(
                pltpu.make_async_copy(
                    tokens_hbm.at[:, pl.ds(start, half)],
                    out.at[pl.ds(c * block // 2, block // 2), pl.ds(0, half)],
                    token_sems.at[d, c],
                )
            )
    for copy in cache + token_copies:
        copy.start()
    lat_ref[:, width:] = jnp.zeros((rows * per, CHANNELS - width), jnp.float32)
    for copy in cache:
        copy.wait()
    scales = scales_ref[...].astype(jnp.float32)
    top, named = ids_ref.shape
    for d in range(len(outs) + 1):
        lat_ref[d * block : d * block + top, width : width + named] = ids_ref[...].astype(
            jnp.float32
        )
    for r in range(rows):
        for g in range(groups):
            columns = slice(g * GROUP, min((g + 1) * GROUP, width))
            lat_ref[r * per : (r + 1) * per, columns] = (
                codes_ref[r, :, columns].astype(jnp.float32) * scales[g, :, r : r + 1]
            )
    for d in range(len(outs) + 1):
        start = pl.multiple_of((here ^ d) * block, block)
        part = lat_ref[pl.ds(start, block), :].astype(jnp.bfloat16)
        if d == 0:
            own[...] = part
        else:
            outs[ORDER.index(d)][:, half:] = part
    for copy in token_copies:
        copy.wait()


def in_hbm(x):
    return pltpu.with_memory_space_constraint(x, pltpu.HBM)


def in_vmem(x):
    return pltpu.with_memory_space_constraint(x, pltpu.VMEM)


def pack(codes, scales, tokens, expert_ids, n_ep):
    rows, per, width = codes.shape
    block = rows * per // n_ep
    wide = tokens.shape[1] // 8 + CHANNELS
    scales, ids = scales.transpose(2, 1, 0), expert_ids.T
    return pl.pallas_call(
        pack_kernel,
        in_specs=[HBM] * 4,
        out_specs=[VM] * n_ep,
        out_shape=[jax.ShapeDtypeStruct((block, wide), jnp.bfloat16)] * (n_ep - 1)
        + [jax.ShapeDtypeStruct((block, CHANNELS), jnp.bfloat16)],
        scratch_shapes=[
            pltpu.VMEM(codes.shape, jnp.bfloat16),
            pltpu.VMEM(scales.shape, jnp.bfloat16),
            pltpu.VMEM(ids.shape, jnp.int32),
            pltpu.VMEM((rows * per, CHANNELS), jnp.float32),
            pltpu.SemaphoreType.DMA((3,)),
            pltpu.SemaphoreType.DMA((n_ep - 1, 2)),
        ],
        compiler_params=pltpu.CompilerParams(vmem_limit_bytes=SCOPE),
        name="pack",
    )(in_hbm(codes), in_hbm(scales), in_hbm(tokens), in_hbm(ids))


def merge_kernel(*refs):
    sources, out = refs[:-1], refs[-1]
    rows, half = out.shape[0] // len(sources), out.shape[1] // 2
    for d, source in enumerate(sources):
        for c in range(2):
            out[d * rows : (d + 1) * rows, c * half : (c + 1) * half] = source[
                c * rows : (c + 1) * rows, :half
            ]


def merge(came, rows, half):
    return pl.pallas_call(
        merge_kernel,
        in_specs=[VM] * len(came),
        out_specs=VM,
        out_shape=jax.ShapeDtypeStruct((len(came) * rows, 2 * half), jnp.bfloat16),
        compiler_params=pltpu.CompilerParams(vmem_limit_bytes=SCOPE),
        name="merge",
    )(*came)


def part_copies(b, first, g_ref, u_ref, g_to, u_to, sems):
    depth = g_to.shape[1]
    rows = pl.ds(pl.multiple_of((lax.axis_index("pf") ^ b) * depth, 128), depth)

    def pair(e):
        return (
            pltpu.make_async_copy(g_ref.at[first + e, rows], g_to.at[e], sems.at[0, e]),
            pltpu.make_async_copy(u_ref.at[first + e, rows], u_to.at[e], sems.at[1, e]),
        )

    def start(e):
        for copy in pair(e):
            copy.start()

    def wait(e):
        for copy in pair(e):
            copy.wait()

    return start, wait


def for_all(act, count):
    @pl.loop(0, count)
    def _(e):
        act(e)


def hold_kernel(ids_hbm, weight_hbm, g_ref, u_ref, *refs):
    own_gate, own_up, next_gate, next_up, select_ref, column_ref = refs[:6]
    ids_ref, weight_ref, few_sems, sems, next_sems = refs[6:]
    few = [
        pltpu.make_async_copy(ids_hbm, ids_ref, few_sems.at[0]),
        pltpu.make_async_copy(weight_hbm, weight_ref, few_sems.at[1]),
    ]
    for copy in few:
        copy.start()
    start, wait = part_copies(0, 0, g_ref, u_ref, own_gate, own_up, sems)
    start_next, wait_next = part_copies(1, 0, g_ref, u_ref, next_gate, next_up, next_sems)
    for_all(start, g_ref.shape[0])
    for_all(start_next, EARLY)
    for copy in few:
        copy.wait()
    top, rows = ids_ref.shape
    experts = g_ref.shape[0]
    slots = rows // 2
    here = lax.axis_index("ep")
    pair = lax.broadcasted_iota(jnp.int32, (top * rows, 1), 0)
    other = lax.broadcasted_iota(jnp.int32, (top * rows, rows), 1)
    ids = jnp.zeros((top * rows, rows), jnp.int32)
    weight = jnp.zeros((top * rows, rows), jnp.float32)
    for k in range(top):
        chosen = (other == pair // top) & (pair % top == k)
        ids = jnp.where(chosen, ids_ref[k : k + 1, :], ids)
        weight = jnp.where(chosen, weight_ref[k : k + 1, :], weight)
    ids = jnp.sum(ids, axis=1, keepdims=True)
    column_ref[...] = jnp.sum(weight, axis=1, keepdims=True)
    earlier = jnp.zeros((top * rows, rows), jnp.int32)
    for k in range(top):
        earlier += jnp.where((ids_ref[k : k + 1, :] == ids) & (other < pair // top), 1, 0)
    slot = jnp.sum(earlier, axis=1, keepdims=True)
    column = lax.broadcasted_iota(jnp.int32, (1, experts * slots), 1)
    for i, d in enumerate((0,) + ORDER):
        match = (ids == (here ^ d) * experts + column // slots) & (column % slots == slot)
        select_ref[:, i * experts * slots : (i + 1) * experts * slots] = jnp.where(
            match, 1.0, 0.0
        ).astype(jnp.bfloat16)
    for_all(wait, experts)
    for_all(wait_next, EARLY)


def hold(expert_ids, routing_weights, w_gate, w_up, n_ep):
    experts, depth, wide = w_gate.shape
    rows, top = expert_ids.shape
    shapes = [(n, depth // 4, wide) for n in (experts, experts, EARLY, EARLY)]
    return pl.pallas_call(
        hold_kernel,
        in_specs=[HBM] * 4,
        out_specs=[VM] * 6,
        out_shape=[pltpu.VMEM(shape, jnp.bfloat16) for shape in shapes]
        + [
            jax.ShapeDtypeStruct((rows * top, n_ep * experts * rows // 2), jnp.bfloat16),
            jax.ShapeDtypeStruct((rows * top, 1), jnp.float32),
        ],
        scratch_shapes=[
            pltpu.VMEM((top, rows), jnp.int32),
            pltpu.VMEM((top, rows), jnp.float32),
            pltpu.SemaphoreType.DMA((2,)),
            pltpu.SemaphoreType.DMA((2, experts)),
            pltpu.SemaphoreType.DMA((2, EARLY)),
        ],
        cost_estimate=pl.CostEstimate(
            flops=0, bytes_accessed=(experts + EARLY) * depth * wide, transcendentals=0
        ),
        compiler_params=pltpu.CompilerParams(vmem_limit_bytes=GRANT),
        name="hold",
    )(in_hbm(expert_ids.T), in_hbm(routing_weights.T), w_gate, w_up)


def set_rows(b, x_ref, own_ref, came_ref):
    rows, quarter = own_ref.shape[0], came_ref.shape[1]
    start = pl.multiple_of((lax.axis_index("pf") ^ b) * quarter, 128)
    x_ref[:rows, :] = own_ref[:, pl.ds(start, quarter)]
    x_ref[rows : rows + came_ref.shape[0], :] = came_ref[...]


def times(x_ref, w_ref, e):
    rows = x_ref.shape[0] // 2
    return jnp.dot(x_ref[...], w_ref[e], preferred_element_type=jnp.float32)[:rows]


def set_slots(pieces, slots_ref, experts, rows, top):
    n_ep = len(pieces)
    slots = rows // 2
    wide = CHANNELS - LAT
    ids = jnp.zeros((top, n_ep * rows), jnp.float32)
    for d, piece in enumerate(pieces):
        tail = piece[: 2 * top, piece.shape[1] - wide :][:top]
        lane = lax.broadcasted_iota(jnp.int32, (wide, n_ep * rows), 0)
        column = lax.broadcasted_iota(jnp.int32, (wide, n_ep * rows), 1)
        take = (lane == ROPE + column % rows) & (column // rows == d)
        ids += jnp.dot(
            tail, jnp.where(take, 1.0, 0.0).astype(jnp.bfloat16), preferred_element_type=jnp.float32
        )
    shape = slots_ref.shape
    place = lax.broadcasted_iota(jnp.int32, shape, 0)
    column = lax.broadcasted_iota(jnp.int32, shape, 1)
    expert = lax.axis_index("ep") * experts + place // (n_ep * slots)
    named = jnp.zeros(shape, jnp.float32)
    for k in range(top):
        named += jnp.where(ids[k : k + 1, :].astype(jnp.int32) == expert, 1.0, 0.0)
    named = jnp.where(place % (n_ep * slots) // slots == column // rows, named, 0.0)
    above = lax.broadcasted_iota(jnp.int32, (n_ep * rows,) * 2, 0)
    below = lax.broadcasted_iota(jnp.int32, (n_ep * rows,) * 2, 1)
    before = jnp.where((above // rows == below // rows) & (above < below), 1.0, 0.0)
    rank = jnp.dot(
        named.astype(jnp.bfloat16), before.astype(jnp.bfloat16), preferred_element_type=jnp.float32
    )
    slot = (place % slots).astype(jnp.float32)
    slots_ref[...] = jnp.where((named > 0.5) & (rank == slot), 1.0, 0.0).astype(jnp.bfloat16)


def front_kernel(own, came, came_too, hg, hu, mg, mu, g_hbm, u_hbm, *refs):
    pieces, (gate, up, g_to, u_to, slots_ref) = refs[:-11], refs[-11:-6]
    tg, tu, x_ref, y_ref, few_sems, sems = refs[-6:]
    experts, early = hg.shape[0], mg.shape[0]
    start_few, wait_few = part_copies(1, early, g_hbm, u_hbm, tg, tu, few_sems)
    start, wait = part_copies(2, 0, g_hbm, u_hbm, g_to, u_to, sems)
    for_all(start_few, experts - early)
    set_rows(0, x_ref, own, came)
    set_rows(1, y_ref, own, came_too)

    @pl.loop(0, experts, unroll=2)
    def _(e):
        @pl.when(e >= experts - AHEAD)
        def _():
            start(e - (experts - AHEAD))

        gate[e] = times(x_ref, hg, e)
        up[e] = times(x_ref, hu, e)

    @pl.loop(0, early)
    def _(e):
        gate[e] += times(y_ref, mg, e)
        up[e] += times(y_ref, mu, e)

    set_slots(pieces, slots_ref, experts, own.shape[0], TOP)

    @pl.loop(0, experts - early)
    def _(e):
        wait_few(e)
        gate[early + e] += times(y_ref, tg, e)
        up[early + e] += times(y_ref, tu, e)

    for_all(wait, AHEAD)


def front(own, x0, x1, held, pieces, w_gate, w_up):
    experts, depth, wide = w_gate.shape
    rows = own.shape[0] + x0.shape[0]
    part = depth // 4
    rest = experts - EARLY
    sums = [jax.ShapeDtypeStruct((experts, rows, wide), jnp.float32)] * 2
    *sums, gate, up, slots = pl.pallas_call(
        front_kernel,
        in_specs=[VM] * 7 + [HBM] * 2 + [VM] * len(pieces),
        out_specs=[VM] * 5,
        out_shape=sums
        + [pltpu.VMEM((AHEAD, part, wide), jnp.bfloat16)] * 2
        + [jax.ShapeDtypeStruct((experts * rows // 2, rows), jnp.bfloat16)],
        scratch_shapes=[pltpu.VMEM((rest, part, wide), jnp.bfloat16)] * 2
        + [pltpu.VMEM((2 * rows, part), jnp.bfloat16)] * 2
        + [pltpu.SemaphoreType.DMA((2, rest)), pltpu.SemaphoreType.DMA((2, AHEAD))],
        cost_estimate=pl.CostEstimate(
            flops=2 * rows * depth * wide * experts,
            bytes_accessed=(rest + AHEAD) * depth * wide,
            transcendentals=0,
        ),
        compiler_params=pltpu.CompilerParams(vmem_limit_bytes=GRANT),
        name="front",
    )(own, x0, x1, *map(in_vmem, held), w_gate, w_up, *pieces)
    return sums, (gate, up), slots


def last_kernel(n_ep, own, came, came_too, hg, hu, g_hbm, u_hbm, gate, up, slots_ref, *refs):
    outs, (gate_sum, up_sum, tg, tu, gb, ub, x_ref, y_ref, few_sems, sems) = refs[:-10], refs[-10:]
    experts, held = gate.shape[0], hg.shape[0]
    slots = outs[0].shape[1]
    start_few, wait_few = part_copies(2, held, g_hbm, u_hbm, tg, tu, few_sems)
    start, wait = part_copies(3, 0, g_hbm, u_hbm, gb, ub, sems)
    for_all(start_few, experts - held)
    start(0)
    set_rows(2, x_ref, own, came)
    set_rows(3, y_ref, own, came_too)

    @pl.loop(0, held, unroll=2)
    def _(e):
        start(e + 1)
        gate_sum[e] = gate[e] + times(x_ref, hg, e)
        up_sum[e] = up[e] + times(x_ref, hu, e)

    @pl.loop(0, experts - held)
    def _(e):
        wait_few(e)

        @pl.when(held + e + 1 < experts)
        def _():
            start(held + e + 1)

        gate_sum[held + e] = gate[held + e] + times(x_ref, tg, e)
        up_sum[held + e] = up[held + e] + times(x_ref, tu, e)

    @pl.loop(0, experts)
    def _(e):
        wait(e)
        gate_sum[e] += times(y_ref, gb, e)
        up_sum[e] += times(y_ref, ub, e)

    for e in range(experts):
        gate_part = gate_sum[e]
        hidden = (gate_part * jax.nn.sigmoid(gate_part) * up_sum[e]).astype(jnp.bfloat16)
        back = jnp.dot(
            slots_ref[e * n_ep * slots : (e + 1) * n_ep * slots, :],
            hidden,
            preferred_element_type=jnp.float32,
        ).astype(jnp.bfloat16)
        for d in range(n_ep):
            outs[d][e] = back[d * slots : (d + 1) * slots]


def last(n_ep, own, came, came_too, held, gate, up, slots, w_gate, w_up):
    experts, depth, wide = w_gate.shape
    rows, part = own.shape[0] + came.shape[0], depth // 4
    rest = experts - AHEAD
    out = jax.ShapeDtypeStruct((experts, own.shape[0] // 2, wide), jnp.bfloat16)
    return pl.pallas_call(
        functools.partial(last_kernel, n_ep),
        in_specs=[VM] * 5 + [HBM] * 2 + [VM] * 3,
        out_specs=[VM] * n_ep,
        out_shape=[out] * n_ep,
        scratch_shapes=[pltpu.VMEM((experts, rows, wide), jnp.float32)] * 2
        + [pltpu.VMEM((n, part, wide), jnp.bfloat16) for n in (rest, rest, experts, experts)]
        + [pltpu.VMEM((2 * rows, part), jnp.bfloat16)] * 2
        + [pltpu.SemaphoreType.DMA((2, rest)), pltpu.SemaphoreType.DMA((2, experts))],
        cost_estimate=pl.CostEstimate(
            flops=2 * rows * depth * wide * experts,
            bytes_accessed=(experts + rest) * depth * wide,
            transcendentals=experts * rows * wide,
        ),
        compiler_params=pltpu.CompilerParams(
            vmem_limit_bytes=GRANT + (experts + EARLY) * 4 * part * wide
        ),
        name="last",
    )(own, came, came_too, *[in_vmem(x) for x in held], w_gate, w_up, gate, up, slots)


def pick_kernel(select_ref, column_ref, *refs):
    blocks, o_ref = refs[:-1], refs[-1]
    experts, rows, wide = blocks[0].shape
    total = jnp.zeros((select_ref.shape[0], wide), jnp.float32)
    for d, block in enumerate(blocks):
        total += jnp.dot(
            select_ref[:, d * experts * rows : (d + 1) * experts * rows],
            block[...].reshape(experts * rows, wide),
            preferred_element_type=jnp.float32,
        )
    o_ref[...] = (total * column_ref[...]).astype(jnp.bfloat16)


def pick(select, column, blocks):
    pairs, wide = select.shape[0], blocks[0].shape[2]
    return pl.pallas_call(
        pick_kernel,
        in_specs=[VM] * (2 + len(blocks)),
        out_specs=VM,
        out_shape=jax.ShapeDtypeStruct((pairs, wide), jnp.bfloat16),
        compiler_params=pltpu.CompilerParams(vmem_limit_bytes=SCOPE),
        name="pick",
    )(select, column, *blocks)


def crossed(x, axis, bit):
    n = lax.axis_size(axis)
    return lax.ppermute(x, axis, [(s, s ^ bit) for s in range(n)])


def local_ring(
    cache_codes,
    cache_scales,
    queries,
    new_latent,
    prompt_lengths,
    tokens,
    expert_ids,
    routing_weights,
    w_gate,
    w_up,
):
    n_ep = lax.axis_size("ep")
    per = cache_codes.shape[1]
    half = tokens.shape[1] // 8
    rows = tokens.shape[0]
    *sent, own_piece = pack(cache_codes, cache_scales, tokens, expert_ids, n_ep)
    came = [crossed(x, "ep", d) for d, x in zip(ORDER, sent)]
    w_gate, w_up = in_hbm(w_gate), in_hbm(w_up)
    *held, select, column = hold(expert_ids, routing_weights, w_gate, w_up, n_ep)
    came, held, select, column = lax.optimization_barrier((came, held, select, column))
    came = [came[ORDER.index(d)] for d in range(1, n_ep)]
    x0 = merge(came, rows, half)
    x1 = crossed(x0, "pf", 1)
    x2 = crossed(x0, "pf", 2)
    x3 = crossed(x0, "pf", 3)
    pieces = [own_piece] + came
    sums, held, slots = front(tokens, x0, x1, held, pieces, w_gate, w_up)
    blocks = last(n_ep, tokens, x2, x3, held, *sums, slots, w_gate, w_up)
    back = [blocks[0]] + [crossed(blocks[d], "ep", d) for d in ORDER]
    attention_out = attend(queries, new_latent, prompt_lengths, per, pieces)
    moe_hidden = pick(select, column, back)
    return attention_out, moe_hidden.reshape(rows, -1, moe_hidden.shape[1])


def local_wide(
    cache_codes,
    cache_scales,
    queries,
    new_latent,
    prompt_lengths,
    tokens,
    expert_ids,
    routing_weights,
    w_gate,
    w_up,
):
    latent = decode_cache(cache_codes, cache_scales)
    cache = lax.all_to_all(latent, "ep", split_axis=0, concat_axis=1, tiled=True)
    per = cache.shape[1]
    cache = jnp.pad(cache, ((0, 0), (0, 0), (0, CHANNELS - cache.shape[2])))
    cache = cache.reshape(-1, CHANNELS)
    attention_out = attend(queries, new_latent, prompt_lengths, per, [cache])
    x = lax.all_gather(tokens, "ep", axis=0, tiled=True)
    gate = jnp.einsum("rd,edf->erf", x, w_gate, preferred_element_type=jnp.float32)
    up = jnp.einsum("rd,edf->erf", x, w_up, preferred_element_type=jnp.float32)
    hidden = (jax.nn.silu(gate) * up).astype(jnp.bfloat16)
    back = lax.all_to_all(hidden, "ep", split_axis=1, concat_axis=0, tiled=True)
    match = expert_ids[:, :, None] == jnp.arange(back.shape[0], dtype=jnp.int32)
    picked = jnp.einsum(
        "rke,erf->rkf", match.astype(jnp.bfloat16), back, preferred_element_type=jnp.float32
    )
    return attention_out, (picked * routing_weights[:, :, None]).astype(jnp.bfloat16)


def solution(mesh):
    near = mesh.shape["ep"] == 4 and mesh.shape["pf"] == 4
    return jax.shard_map(
        local_ring if near else local_wide,
        mesh=mesh,
        in_specs=(
            P(("groups", "pf"), "ep", None),
            P(("groups", "pf"), "ep", None),
            P(("groups", "pf", "ep"), None, None),
            P(("groups", "pf", "ep"), None),
            P(("groups", "pf", "ep")),
            P(("groups", "ep"), None),
            P(("groups", "ep"), None),
            P(("groups", "ep"), None),
            P("ep", None, "pf"),
            P("ep", None, "pf"),
        ),
        out_specs=(P(("groups", "pf", "ep"), None, None), P(("groups", "ep"), None, "pf")),
        check_vma=False,
    )
```

```python
import functools

import jax
import jax.numpy as jnp
from jax import lax
from jax.experimental import pallas as pl
from jax.experimental.pallas import tpu as pltpu
from jax.sharding import PartitionSpec as P

LAT = 512
ROPE = 64
GROUP = 128
TOP = 8
EARLY = 3
AHEAD = 6
CHANNELS = 640
SCOPE = 4 << 20
GRANT = 16 << 20
PARTS = {1: (0, 2), 2: (0,), 3: (0,)}
ORDER = (2, 3, 1)
BACK = (3, 2, 1)
HELD = 14 << 20

qk_scale = 192.0 ** (-0.5)
VM = pl.BlockSpec(memory_space=pltpu.VMEM)
SM = pl.BlockSpec(memory_space=pltpu.SMEM)
HBM = pl.BlockSpec(memory_space=pltpu.HBM)


def spread_scales(scale_block):
    latent_part = jnp.repeat(scale_block[..., :-1], GROUP, axis=-1, total_repeat_length=LAT)
    rope_part = jnp.repeat(scale_block[..., -1:], ROPE, axis=-1, total_repeat_length=ROPE)
    return jnp.concatenate([latent_part, rope_part], axis=-1)


def decode_cache(codes, scales):
    return (codes.astype(jnp.float32) * spread_scales(scales.astype(jnp.float32))).astype(
        jnp.bfloat16
    )


def attend_kernel(per, q_ref, new_ref, len_ref, *refs):
    pieces, (o_ref, kv_ref) = refs[:-2], refs[-2:]
    rows, width, heads = q_ref.shape
    total = kv_ref.shape[0]
    block = rows * per
    count = len(pieces) * block
    kv_ref[pl.ds(count, total - count), :] = jnp.zeros((total - count, width), jnp.bfloat16)
    for d, piece in enumerate(pieces):
        kv_ref[pl.ds(d * block, block), :] = piece[:, piece.shape[1] - CHANNELS :][:, :width]
    kv_ref[pl.ds(count, rows), :] = new_ref[...]
    kv = kv_ref[...]
    place = lax.broadcasted_iota(jnp.int32, (total, 1), 0)
    start = jnp.zeros_like(place)
    for d in range(len(pieces)) if len(pieces) > 1 else ():
        start = jnp.where(place // block == d, (lax.axis_index("ep") ^ d) * per, start)
    row_of = place % block // per
    position = start + place % per
    for r in range(rows):
        live = ((place < count) & (row_of == r) & (position < len_ref[r])) | (place == count + r)
        scores = jnp.dot(kv, q_ref[r], preferred_element_type=jnp.float32) * qk_scale
        scores = jnp.where(live, scores, -jnp.inf)
        exponent = jnp.exp(scores - jnp.max(scores, axis=0, keepdims=True))
        weights = exponent / jnp.sum(exponent, axis=0, keepdims=True)
        o_ref[r] = lax.dot_general(
            weights.astype(jnp.bfloat16),
            kv[:, :LAT],
            (((0,), (0,)), ((), ())),
            preferred_element_type=jnp.float32,
        ).astype(jnp.bfloat16)


def attend(queries, new_latent, prompt_lengths, per, pieces):
    rows, heads, width = queries.shape
    count = sum(p.shape[0] for p in pieces)
    total = -(-(count + rows) // 128) * 128
    return pl.pallas_call(
        functools.partial(attend_kernel, per),
        in_specs=[VM, VM, SM] + [VM] * len(pieces),
        out_specs=VM,
        out_shape=jax.ShapeDtypeStruct((rows, heads, LAT), jnp.bfloat16),
        scratch_shapes=[pltpu.VMEM((total, width), jnp.bfloat16)],
        cost_estimate=pl.CostEstimate(
            flops=4 * rows * heads * total * width,
            bytes_accessed=2 * rows * heads * (width + LAT),
            transcendentals=rows * heads * total,
        ),
        compiler_params=pltpu.CompilerParams(vmem_limit_bytes=SCOPE),
        name="attend",
    )(queries.swapaxes(1, 2), new_latent, prompt_lengths, *pieces)


def pack_kernel(codes_hbm, scales_hbm, tokens_hbm, ids_hbm, *refs):
    outs, own, (codes_ref, scales_ref, ids_ref, lat_ref, sems, token_sems) = (
        refs[:-7],
        refs[-7],
        refs[-6:],
    )
    rows, per, width = codes_ref.shape
    groups = scales_ref.shape[0]
    block = own.shape[0]
    half = tokens_hbm.shape[1] // 8
    here, me = lax.axis_index("ep"), lax.axis_index("pf")
    cache = [
        pltpu.make_async_copy(codes_hbm, codes_ref, sems.at[0]),
        pltpu.make_async_copy(scales_hbm, scales_ref, sems.at[1]),
        pltpu.make_async_copy(ids_hbm, ids_ref, sems.at[2]),
    ]
    token_copies = []
    for i, out in enumerate(outs):
        for j, b in enumerate(PARTS[ORDER[i]]):
            for c in range(2):
                start = pl.multiple_of((2 * (me ^ b) + c) * half, 128)
                token_copies.append(
                    pltpu.make_async_copy(
                        tokens_hbm.at[:, pl.ds(start, half)],
                        out.at[pl.ds(c * block // 2, block // 2), pl.ds(j * half, half)],
                        token_sems.at[i, 2 * j + c],
                    )
                )
    for copy in cache + token_copies:
        copy.start()
    lat_ref[:, width:] = jnp.zeros((rows * per, CHANNELS - width), jnp.float32)
    for copy in cache:
        copy.wait()
    scales = scales_ref[...].astype(jnp.float32)
    top, named = ids_ref.shape
    for d in range(len(outs) + 1):
        lat_ref[d * block : d * block + top, width : width + named] = ids_ref[...].astype(
            jnp.float32
        )
    for r in range(rows):
        for g in range(groups):
            columns = slice(g * GROUP, min((g + 1) * GROUP, width))
            lat_ref[r * per : (r + 1) * per, columns] = (
                codes_ref[r, :, columns].astype(jnp.float32) * scales[g, :, r : r + 1]
            )
    for d in range(len(outs) + 1):
        start = pl.multiple_of((here ^ d) * block, block)
        part = lat_ref[pl.ds(start, block), :].astype(jnp.bfloat16)
        if d == 0:
            own[...] = part
        else:
            outs[ORDER.index(d)][:, len(PARTS[d]) * half :] = part
    for copy in token_copies:
        copy.wait()


def in_hbm(x):
    return pltpu.with_memory_space_constraint(x, pltpu.HBM)


def in_vmem(x):
    return pltpu.with_memory_space_constraint(x, pltpu.VMEM)


def pack(codes, scales, tokens, expert_ids, n_ep):
    rows, per, width = codes.shape
    block = rows * per // n_ep
    wide = [len(PARTS[d]) * tokens.shape[1] // 8 + CHANNELS for d in ORDER]
    scales, ids = scales.transpose(2, 1, 0), expert_ids.T
    return pl.pallas_call(
        pack_kernel,
        in_specs=[HBM] * 4,
        out_specs=[VM] * n_ep,
        out_shape=[jax.ShapeDtypeStruct((block, w), jnp.bfloat16) for w in wide]
        + [jax.ShapeDtypeStruct((block, CHANNELS), jnp.bfloat16)],
        scratch_shapes=[
            pltpu.VMEM(codes.shape, jnp.bfloat16),
            pltpu.VMEM(scales.shape, jnp.bfloat16),
            pltpu.VMEM(ids.shape, jnp.int32),
            pltpu.VMEM((rows * per, CHANNELS), jnp.float32),
            pltpu.SemaphoreType.DMA((3,)),
            pltpu.SemaphoreType.DMA((n_ep - 1, 4)),
        ],
        compiler_params=pltpu.CompilerParams(vmem_limit_bytes=SCOPE),
        name="pack",
    )(in_hbm(codes), in_hbm(scales), in_hbm(tokens), in_hbm(ids))


def set_part(ref, at, source, j):
    rows, half = source.shape[0] // 2, ref.shape[1] // 2
    for c in range(2):
        ref[at : at + rows, c * half : (c + 1) * half] = source[
            c * rows : (c + 1) * rows, j * half : (j + 1) * half
        ]


def merge_kernel(near, *refs):
    sources, (out, far) = refs[:-2], refs[-2:]
    rows = near.shape[0] // 2
    set_part(out, 0, near, 0)
    for d, source in enumerate(sources):
        set_part(out, (d + 1) * rows, source, 0)
        set_part(far, d * rows, source, 0)


def merge(came, rows, quarter):
    return pl.pallas_call(
        merge_kernel,
        in_specs=[VM] * len(came),
        out_specs=[VM] * 2,
        out_shape=[
            jax.ShapeDtypeStruct((n * rows, quarter), jnp.bfloat16)
            for n in (len(came), len(came) - 1)
        ],
        compiler_params=pltpu.CompilerParams(vmem_limit_bytes=SCOPE),
        name="merge",
    )(*came)


def part_copies(b, first, g_ref, u_ref, g_to, u_to, sems):
    depth = g_to.shape[1]
    rows = pl.ds(pl.multiple_of((lax.axis_index("pf") ^ b) * depth, 128), depth)

    def pair(e):
        return (
            pltpu.make_async_copy(g_ref.at[first + e, rows], g_to.at[e], sems.at[0, e]),
            pltpu.make_async_copy(u_ref.at[first + e, rows], u_to.at[e], sems.at[1, e]),
        )

    def start(e):
        for copy in pair(e):
            copy.start()

    def wait(e):
        for copy in pair(e):
            copy.wait()

    return start, wait


def for_all(act, count):
    @pl.loop(0, count)
    def _(e):
        act(e)


def hold_kernel(ids_hbm, weight_hbm, g_ref, u_ref, *refs):
    own_gate, own_up, next_gate, next_up, select_ref, column_ref = refs[:6]
    ids_ref, weight_ref, few_sems, sems, next_sems = refs[6:]
    few = [
        pltpu.make_async_copy(ids_hbm, ids_ref, few_sems.at[0]),
        pltpu.make_async_copy(weight_hbm, weight_ref, few_sems.at[1]),
    ]
    for copy in few:
        copy.start()
    start, wait = part_copies(0, 0, g_ref, u_ref, own_gate, own_up, sems)
    start_next, wait_next = part_copies(1, 0, g_ref, u_ref, next_gate, next_up, next_sems)
    for_all(start, g_ref.shape[0])
    for_all(start_next, EARLY)
    for copy in few:
        copy.wait()
    top, rows = ids_ref.shape
    experts = g_ref.shape[0]
    slots = rows // 2
    here = lax.axis_index("ep")
    pair = lax.broadcasted_iota(jnp.int32, (top * rows, 1), 0)
    other = lax.broadcasted_iota(jnp.int32, (top * rows, rows), 1)
    ids = jnp.zeros((top * rows, rows), jnp.int32)
    weight = jnp.zeros((top * rows, rows), jnp.float32)
    for k in range(top):
        chosen = (other == pair // top) & (pair % top == k)
        ids = jnp.where(chosen, ids_ref[k : k + 1, :], ids)
        weight = jnp.where(chosen, weight_ref[k : k + 1, :], weight)
    ids = jnp.sum(ids, axis=1, keepdims=True)
    column_ref[...] = jnp.sum(weight, axis=1, keepdims=True)
    earlier = jnp.zeros((top * rows, rows), jnp.int32)
    for k in range(top):
        earlier += jnp.where((ids_ref[k : k + 1, :] == ids) & (other < pair // top), 1, 0)
    slot = jnp.sum(earlier, axis=1, keepdims=True)
    column = lax.broadcasted_iota(jnp.int32, (1, experts * slots), 1)
    for i, d in enumerate((0,) + BACK):
        match = (ids == (here ^ d) * experts + column // slots) & (column % slots == slot)
        select_ref[:, i * experts * slots : (i + 1) * experts * slots] = jnp.where(
            match, 1.0, 0.0
        ).astype(jnp.bfloat16)
    for_all(wait, experts)
    for_all(wait_next, EARLY)


def hold(expert_ids, routing_weights, w_gate, w_up, n_ep):
    experts, depth, wide = w_gate.shape
    rows, top = expert_ids.shape
    shapes = [(n, depth // 4, wide) for n in (experts, experts, EARLY, EARLY)]
    return pl.pallas_call(
        hold_kernel,
        in_specs=[HBM] * 4,
        out_specs=[VM] * 6,
        out_shape=[pltpu.VMEM(shape, jnp.bfloat16) for shape in shapes]
        + [
            jax.ShapeDtypeStruct((rows * top, n_ep * experts * rows // 2), jnp.bfloat16),
            jax.ShapeDtypeStruct((rows * top, 1), jnp.float32),
        ],
        scratch_shapes=[
            pltpu.VMEM((top, rows), jnp.int32),
            pltpu.VMEM((top, rows), jnp.float32),
            pltpu.SemaphoreType.DMA((2,)),
            pltpu.SemaphoreType.DMA((2, experts)),
            pltpu.SemaphoreType.DMA((2, EARLY)),
        ],
        cost_estimate=pl.CostEstimate(
            flops=0, bytes_accessed=(experts + EARLY) * depth * wide, transcendentals=0
        ),
        compiler_params=pltpu.CompilerParams(vmem_limit_bytes=GRANT),
        name="hold",
    )(in_hbm(expert_ids.T), in_hbm(routing_weights.T), w_gate, w_up)


def set_rows(b, x_ref, own_ref, came_ref):
    rows, quarter = own_ref.shape[0], came_ref.shape[1]
    start = pl.multiple_of((lax.axis_index("pf") ^ b) * quarter, 128)
    x_ref[:rows, :] = own_ref[:, pl.ds(start, quarter)]
    x_ref[rows : rows + came_ref.shape[0], :] = came_ref[...]


def set_far_rows(b, x_ref, own_ref, near_ref, far_ref):
    rows, quarter = own_ref.shape[0], far_ref.shape[1]
    start = pl.multiple_of((lax.axis_index("pf") ^ b) * quarter, 128)
    x_ref[:rows, :] = own_ref[:, pl.ds(start, quarter)]
    set_part(x_ref, rows, near_ref, PARTS[1].index(b))
    x_ref[2 * rows : 2 * rows + far_ref.shape[0], :] = far_ref[...]


def times(x_ref, w_ref, e):
    rows = x_ref.shape[0] // 2
    return jnp.dot(x_ref[...], w_ref[e], preferred_element_type=jnp.float32)[:rows]


def set_slots(pieces, slots_ref, experts, rows, top):
    n_ep = len(pieces)
    slots = rows // 2
    wide = CHANNELS - LAT
    ids = jnp.zeros((top, n_ep * rows), jnp.float32)
    for d, piece in enumerate(pieces):
        tail = piece[: 2 * top, piece.shape[1] - wide :][:top]
        lane = lax.broadcasted_iota(jnp.int32, (wide, n_ep * rows), 0)
        column = lax.broadcasted_iota(jnp.int32, (wide, n_ep * rows), 1)
        take = (lane == ROPE + column % rows) & (column // rows == d)
        ids += jnp.dot(
            tail, jnp.where(take, 1.0, 0.0).astype(jnp.bfloat16), preferred_element_type=jnp.float32
        )
    shape = slots_ref.shape
    place = lax.broadcasted_iota(jnp.int32, shape, 0)
    column = lax.broadcasted_iota(jnp.int32, shape, 1)
    expert = lax.axis_index("ep") * experts + place // (n_ep * slots)
    named = jnp.zeros(shape, jnp.float32)
    for k in range(top):
        named += jnp.where(ids[k : k + 1, :].astype(jnp.int32) == expert, 1.0, 0.0)
    named = jnp.where(place % (n_ep * slots) // slots == column // rows, named, 0.0)
    above = lax.broadcasted_iota(jnp.int32, (n_ep * rows,) * 2, 0)
    below = lax.broadcasted_iota(jnp.int32, (n_ep * rows,) * 2, 1)
    before = jnp.where((above // rows == below // rows) & (above < below), 1.0, 0.0)
    rank = jnp.dot(
        named.astype(jnp.bfloat16), before.astype(jnp.bfloat16), preferred_element_type=jnp.float32
    )
    slot = (place % slots).astype(jnp.float32)
    slots_ref[...] = jnp.where((named > 0.5) & (rank == slot), 1.0, 0.0).astype(jnp.bfloat16)


def front_kernel(own, came, came_too, hg, hu, mg, mu, g_hbm, u_hbm, *refs):
    pieces, (gate, up, g_to, u_to, slots_ref) = refs[:-11], refs[-11:-6]
    tg, tu, x_ref, y_ref, few_sems, sems = refs[-6:]
    experts, early = hg.shape[0], mg.shape[0]
    start_few, wait_few = part_copies(1, early, g_hbm, u_hbm, tg, tu, few_sems)
    start, wait = part_copies(2, 0, g_hbm, u_hbm, g_to, u_to, sems)
    for_all(start_few, experts - early)
    set_rows(0, x_ref, own, came)
    set_rows(1, y_ref, own, came_too)

    @pl.loop(0, early)
    def _(e):
        gate[e] = times(x_ref, hg, e) + times(y_ref, mg, e)
        up[e] = times(x_ref, hu, e) + times(y_ref, mu, e)

    @pl.loop(0, experts - early)
    def _(e):
        for at in (2 * e, 2 * e + 1):

            @pl.when(at < AHEAD)
            def _():
                start(at)

        wait_few(e)
        at = early + e
        gate[at] = times(x_ref, hg, at) + times(y_ref, tg, e)
        up[at] = times(x_ref, hu, at) + times(y_ref, tu, e)

    set_slots(pieces, slots_ref, experts, own.shape[0], TOP)
    for_all(wait, AHEAD)


def front(own, x0, x1, held, pieces, w_gate, w_up):
    experts, depth, wide = w_gate.shape
    rows = own.shape[0] + x0.shape[0]
    part = depth // 4
    rest = experts - EARLY
    sums = [jax.ShapeDtypeStruct((experts, rows, wide), jnp.float32)] * 2
    *sums, gate, up, slots = pl.pallas_call(
        front_kernel,
        in_specs=[VM] * 7 + [HBM] * 2 + [VM] * len(pieces),
        out_specs=[VM] * 5,
        out_shape=sums
        + [pltpu.VMEM((AHEAD, part, wide), jnp.bfloat16)] * 2
        + [jax.ShapeDtypeStruct((experts * rows // 2, rows), jnp.bfloat16)],
        scratch_shapes=[pltpu.VMEM((rest, part, wide), jnp.bfloat16)] * 2
        + [pltpu.VMEM((2 * rows, part), jnp.bfloat16)] * 2
        + [pltpu.SemaphoreType.DMA((2, rest)), pltpu.SemaphoreType.DMA((2, AHEAD))],
        cost_estimate=pl.CostEstimate(
            flops=2 * rows * depth * wide * experts,
            bytes_accessed=(rest + AHEAD) * depth * wide,
            transcendentals=0,
        ),
        compiler_params=pltpu.CompilerParams(vmem_limit_bytes=GRANT),
        name="front",
    )(own, x0, x1, *map(in_vmem, held), w_gate, w_up, *pieces)
    return sums, (gate, up), slots


def last_kernel(n_ep, own, near, far, far_too, hg, hu, g_hbm, u_hbm, gate, up, slots_ref, *refs):
    outs, (gate_sum, up_sum, tg, tu, gb, ub, x_ref, y_ref, few_sems, sems) = refs[:-10], refs[-10:]
    experts, held = gate.shape[0], hg.shape[0]
    slots = outs[0].shape[1]
    start_few, wait_few = part_copies(2, held, g_hbm, u_hbm, tg, tu, few_sems)
    start, wait = part_copies(3, 0, g_hbm, u_hbm, gb, ub, sems)
    for_all(start_few, experts - held)
    start(0)
    set_far_rows(2, x_ref, own, near, far)
    set_rows(3, y_ref, own, far_too)

    @pl.loop(0, held, unroll=2)
    def _(e):
        start(e + 1)
        gate_sum[e] = gate[e] + times(x_ref, hg, e)
        up_sum[e] = up[e] + times(x_ref, hu, e)

    @pl.loop(0, experts - held)
    def _(e):
        wait_few(e)

        @pl.when(held + e + 1 < experts)
        def _():
            start(held + e + 1)

        gate_sum[held + e] = gate[held + e] + times(x_ref, tg, e)
        up_sum[held + e] = up[held + e] + times(x_ref, tu, e)

    def add(e):
        wait(e)
        gate_sum[e] += times(y_ref, gb, e)
        up_sum[e] += times(y_ref, ub, e)

    def finish(e):
        gate_part = gate_sum[e]
        hidden = (gate_part * jax.nn.sigmoid(gate_part) * up_sum[e]).astype(jnp.bfloat16)
        places = pl.ds(pl.multiple_of(e * n_ep * slots, n_ep * slots), n_ep * slots)
        back = jnp.dot(slots_ref[places, :], hidden, preferred_element_type=jnp.float32)
        back = back.astype(jnp.bfloat16)
        for d in range(n_ep):
            outs[d][e] = back[d * slots : (d + 1) * slots]

    add(0)

    @pl.loop(1, experts)
    def _(e):
        add(e)
        finish(e - 1)

    finish(experts - 1)


def last(n_ep, own, near, far, far_too, held, gate, up, slots, w_gate, w_up):
    experts, depth, wide = w_gate.shape
    rows, part = n_ep * own.shape[0], depth // 4
    rest = experts - AHEAD
    out = jax.ShapeDtypeStruct((experts, own.shape[0] // 2, wide), jnp.bfloat16)
    return pl.pallas_call(
        functools.partial(last_kernel, n_ep),
        in_specs=[VM] * 6 + [HBM] * 2 + [VM] * 3,
        out_specs=[VM] * n_ep,
        out_shape=[out] * n_ep,
        scratch_shapes=[pltpu.VMEM((experts, rows, wide), jnp.float32)] * 2
        + [pltpu.VMEM((n, part, wide), jnp.bfloat16) for n in (rest, rest, experts, experts)]
        + [pltpu.VMEM((2 * rows, part), jnp.bfloat16)] * 2
        + [pltpu.SemaphoreType.DMA((2, rest)), pltpu.SemaphoreType.DMA((2, experts))],
        cost_estimate=pl.CostEstimate(
            flops=2 * rows * depth * wide * experts,
            bytes_accessed=(experts + rest) * depth * wide,
            transcendentals=experts * rows * wide,
        ),
        compiler_params=pltpu.CompilerParams(
            vmem_limit_bytes=GRANT + (experts + EARLY) * 4 * part * wide
        ),
        name="last",
    )(own, near, far, far_too, *[in_vmem(x) for x in held], w_gate, w_up, gate, up, slots)


def pick_kernel(select_ref, column_ref, *refs):
    blocks, o_ref = refs[:-1], refs[-1]
    experts, rows, wide = blocks[0].shape
    total = jnp.zeros((select_ref.shape[0], wide), jnp.float32)
    for d, block in enumerate(blocks):
        total += jnp.dot(
            select_ref[:, d * experts * rows : (d + 1) * experts * rows],
            block[...].reshape(experts * rows, wide),
            preferred_element_type=jnp.float32,
        )
    o_ref[...] = (total * column_ref[...]).astype(jnp.bfloat16)


def pick(select, column, blocks):
    pairs, wide = select.shape[0], blocks[0].shape[2]
    return pl.pallas_call(
        pick_kernel,
        in_specs=[VM] * (2 + len(blocks)),
        out_specs=VM,
        out_shape=jax.ShapeDtypeStruct((pairs, wide), jnp.bfloat16),
        compiler_params=pltpu.CompilerParams(vmem_limit_bytes=SCOPE),
        name="pick",
    )(select, column, *blocks)


def crossed(x, axis, bit):
    n = lax.axis_size(axis)
    return lax.ppermute(x, axis, [(s, s ^ bit) for s in range(n)])


def local_ring(
    cache_codes,
    cache_scales,
    queries,
    new_latent,
    prompt_lengths,
    tokens,
    expert_ids,
    routing_weights,
    w_gate,
    w_up,
):
    n_ep = lax.axis_size("ep")
    per = cache_codes.shape[1]
    half = tokens.shape[1] // 8
    rows = tokens.shape[0]
    *sent, own_piece = pack(cache_codes, cache_scales, tokens, expert_ids, n_ep)
    came = [crossed(x, "ep", d) for d, x in zip(ORDER, sent)]
    w_gate, w_up = in_hbm(w_gate), in_hbm(w_up)
    *held, select, column = hold(expert_ids, routing_weights, w_gate, w_up, n_ep)
    came, held, select, column = lax.optimization_barrier((came, held, select, column))
    came = [came[ORDER.index(d)] for d in range(1, n_ep)]
    x0, far = merge(came, rows, 2 * half)
    x1 = crossed(x0, "pf", 1)
    x2 = crossed(far, "pf", 2)
    x3 = crossed(x0, "pf", 3)
    pieces = [own_piece] + came
    sums, held, slots = front(tokens, x0, x1, held, pieces, w_gate, w_up)
    blocks = last(n_ep, tokens, came[0], x2, x3, held, *sums, slots, w_gate, w_up)
    back = [blocks[0]] + [crossed(blocks[d], "ep", d) for d in BACK]
    attention_out = attend(queries, new_latent, prompt_lengths, per, pieces)
    moe_hidden = pick(select, column, back)
    return attention_out, moe_hidden.reshape(rows, -1, moe_hidden.shape[1])


def local_wide(
    cache_codes,
    cache_scales,
    queries,
    new_latent,
    prompt_lengths,
    tokens,
    expert_ids,
    routing_weights,
    w_gate,
    w_up,
):
    latent = decode_cache(cache_codes, cache_scales)
    cache = lax.all_to_all(latent, "ep", split_axis=0, concat_axis=1, tiled=True)
    per = cache.shape[1]
    cache = jnp.pad(cache, ((0, 0), (0, 0), (0, CHANNELS - cache.shape[2])))
    cache = cache.reshape(-1, CHANNELS)
    attention_out = attend(queries, new_latent, prompt_lengths, per, [cache])
    x = lax.all_gather(tokens, "ep", axis=0, tiled=True)
    gate = jnp.einsum("rd,edf->erf", x, w_gate, preferred_element_type=jnp.float32)
    up = jnp.einsum("rd,edf->erf", x, w_up, preferred_element_type=jnp.float32)
    hidden = (jax.nn.silu(gate) * up).astype(jnp.bfloat16)
    back = lax.all_to_all(hidden, "ep", split_axis=1, concat_axis=0, tiled=True)
    match = expert_ids[:, :, None] == jnp.arange(back.shape[0], dtype=jnp.int32)
    picked = jnp.einsum(
        "rke,erf->rkf", match.astype(jnp.bfloat16), back, preferred_element_type=jnp.float32
    )
    return attention_out, (picked * routing_weights[:, :, None]).astype(jnp.bfloat16)


def solution(mesh):
    near = mesh.shape["ep"] == 4 and mesh.shape["pf"] == 4
    return jax.shard_map(
        local_ring if near else local_wide,
        mesh=mesh,
        in_specs=(
            P(("groups", "pf"), "ep", None),
            P(("groups", "pf"), "ep", None),
            P(("groups", "pf", "ep"), None, None),
            P(("groups", "pf", "ep"), None),
            P(("groups", "pf", "ep")),
            P(("groups", "ep"), None),
            P(("groups", "ep"), None),
            P(("groups", "ep"), None),
            P("ep", None, "pf"),
            P("ep", None, "pf"),
        ),
        out_specs=(P(("groups", "pf", "ep"), None, None), P(("groups", "ep"), None, "pf")),
        check_vma=False,
    )
```

```python
import functools

import jax
import jax.numpy as jnp
from jax import lax
from jax.experimental import pallas as pl
from jax.experimental.pallas import tpu as pltpu
from jax.sharding import PartitionSpec as P

LAT = 512
ROPE = 64
GROUP = 128
TOP = 8
EARLY = 3
AHEAD = 6
CHANNELS = 640
SCOPE = 4 << 20
GRANT = 16 << 20
PARTS = {1: (0, 2), 2: (0,), 3: (0,)}
ORDER = (2, 3, 1)
BACK = (3, 2, 1)
HELD = 14 << 20

qk_scale = 192.0 ** (-0.5)
VM = pl.BlockSpec(memory_space=pltpu.VMEM)
SM = pl.BlockSpec(memory_space=pltpu.SMEM)
HBM = pl.BlockSpec(memory_space=pltpu.HBM)


def spread_scales(scale_block):
    latent_part = jnp.repeat(scale_block[..., :-1], GROUP, axis=-1, total_repeat_length=LAT)
    rope_part = jnp.repeat(scale_block[..., -1:], ROPE, axis=-1, total_repeat_length=ROPE)
    return jnp.concatenate([latent_part, rope_part], axis=-1)


def decode_cache(codes, scales):
    return (codes.astype(jnp.float32) * spread_scales(scales.astype(jnp.float32))).astype(
        jnp.bfloat16
    )


def attend_kernel(per, q_ref, new_ref, len_ref, *refs):
    pieces, (o_ref, kv_ref) = refs[:-2], refs[-2:]
    rows, width, heads = q_ref.shape
    total = kv_ref.shape[0]
    block = rows * per
    count = len(pieces) * block
    kv_ref[pl.ds(count, total - count), :] = jnp.zeros((total - count, width), jnp.bfloat16)
    for d, piece in enumerate(pieces):
        kv_ref[pl.ds(d * block, block), :] = piece[:, piece.shape[1] - CHANNELS :][:, :width]
    kv_ref[pl.ds(count, rows), :] = new_ref[...]
    kv = kv_ref[...]
    place = lax.broadcasted_iota(jnp.int32, (total, 1), 0)
    start = jnp.zeros_like(place)
    for d in range(len(pieces)) if len(pieces) > 1 else ():
        start = jnp.where(place // block == d, (lax.axis_index("ep") ^ d) * per, start)
    row_of = place % block // per
    position = start + place % per
    for r in range(rows):
        live = ((place < count) & (row_of == r) & (position < len_ref[r])) | (place == count + r)
        scores = jnp.dot(kv, q_ref[r], preferred_element_type=jnp.float32) * qk_scale
        scores = jnp.where(live, scores, -jnp.inf)
        exponent = jnp.exp(scores - jnp.max(scores, axis=0, keepdims=True))
        weights = exponent / jnp.sum(exponent, axis=0, keepdims=True)
        o_ref[r] = lax.dot_general(
            weights.astype(jnp.bfloat16),
            kv[:, :LAT],
            (((0,), (0,)), ((), ())),
            preferred_element_type=jnp.float32,
        ).astype(jnp.bfloat16)


def attend(queries, new_latent, prompt_lengths, per, pieces):
    rows, heads, width = queries.shape
    count = sum(p.shape[0] for p in pieces)
    total = -(-(count + rows) // 128) * 128
    return pl.pallas_call(
        functools.partial(attend_kernel, per),
        in_specs=[VM, VM, SM] + [VM] * len(pieces),
        out_specs=VM,
        out_shape=jax.ShapeDtypeStruct((rows, heads, LAT), jnp.bfloat16),
        scratch_shapes=[pltpu.VMEM((total, width), jnp.bfloat16)],
        cost_estimate=pl.CostEstimate(
            flops=4 * rows * heads * total * width,
            bytes_accessed=2 * rows * heads * (width + LAT),
            transcendentals=rows * heads * total,
        ),
        compiler_params=pltpu.CompilerParams(vmem_limit_bytes=SCOPE),
        name="attend",
    )(queries.swapaxes(1, 2), new_latent, prompt_lengths, *pieces)


def pack_kernel(codes_hbm, scales_hbm, tokens_hbm, ids_hbm, *refs):
    outs, own, (codes_ref, scales_ref, ids_ref, lat_ref, sems, token_sems) = (
        refs[:-7],
        refs[-7],
        refs[-6:],
    )
    rows, per, width = codes_ref.shape
    groups = scales_ref.shape[0]
    block = own.shape[0]
    half = tokens_hbm.shape[1] // 8
    here, me = lax.axis_index("ep"), lax.axis_index("pf")
    cache = [
        pltpu.make_async_copy(codes_hbm, codes_ref, sems.at[0]),
        pltpu.make_async_copy(scales_hbm, scales_ref, sems.at[1]),
        pltpu.make_async_copy(ids_hbm, ids_ref, sems.at[2]),
    ]
    token_copies = []
    for i, out in enumerate(outs):
        for j, b in enumerate(PARTS[ORDER[i]]):
            for c in range(2):
                start = pl.multiple_of((2 * (me ^ b) + c) * half, 128)
                token_copies.append(
                    pltpu.make_async_copy(
                        tokens_hbm.at[:, pl.ds(start, half)],
                        out.at[pl.ds(c * block // 2, block // 2), pl.ds(j * half, half)],
                        token_sems.at[i, 2 * j + c],
                    )
                )
    for copy in cache + token_copies:
        copy.start()
    lat_ref[:, width:] = jnp.zeros((rows * per, CHANNELS - width), jnp.float32)
    for copy in cache:
        copy.wait()
    scales = scales_ref[...].astype(jnp.float32)
    top, named = ids_ref.shape
    for d in range(len(outs) + 1):
        lat_ref[d * block : d * block + top, width : width + named] = ids_ref[...].astype(
            jnp.float32
        )
    for r in range(rows):
        for g in range(groups):
            columns = slice(g * GROUP, min((g + 1) * GROUP, width))
            lat_ref[r * per : (r + 1) * per, columns] = (
                codes_ref[r, :, columns].astype(jnp.float32) * scales[g, :, r : r + 1]
            )
    for d in range(len(outs) + 1):
        start = pl.multiple_of((here ^ d) * block, block)
        part = lat_ref[pl.ds(start, block), :].astype(jnp.bfloat16)
        if d == 0:
            own[...] = part
        else:
            outs[ORDER.index(d)][:, len(PARTS[d]) * half :] = part
    for copy in token_copies:
        copy.wait()


def in_hbm(x):
    return pltpu.with_memory_space_constraint(x, pltpu.HBM)


def in_vmem(x):
    return pltpu.with_memory_space_constraint(x, pltpu.VMEM)


def pack(codes, scales, tokens, expert_ids, n_ep):
    rows, per, width = codes.shape
    block = rows * per // n_ep
    wide = [len(PARTS[d]) * tokens.shape[1] // 8 + CHANNELS for d in ORDER]
    scales, ids = scales.transpose(2, 1, 0), expert_ids.T
    return pl.pallas_call(
        pack_kernel,
        in_specs=[HBM] * 4,
        out_specs=[VM] * n_ep,
        out_shape=[jax.ShapeDtypeStruct((block, w), jnp.bfloat16) for w in wide]
        + [jax.ShapeDtypeStruct((block, CHANNELS), jnp.bfloat16)],
        scratch_shapes=[
            pltpu.VMEM(codes.shape, jnp.bfloat16),
            pltpu.VMEM(scales.shape, jnp.bfloat16),
            pltpu.VMEM(ids.shape, jnp.int32),
            pltpu.VMEM((rows * per, CHANNELS), jnp.float32),
            pltpu.SemaphoreType.DMA((3,)),
            pltpu.SemaphoreType.DMA((n_ep - 1, 4)),
        ],
        compiler_params=pltpu.CompilerParams(vmem_limit_bytes=SCOPE),
        name="pack",
    )(in_hbm(codes), in_hbm(scales), in_hbm(tokens), in_hbm(ids))


def set_part(ref, at, source, j):
    rows, half = source.shape[0] // 2, ref.shape[1] // 2
    for c in range(2):
        ref[at : at + rows, c * half : (c + 1) * half] = source[
            c * rows : (c + 1) * rows, j * half : (j + 1) * half
        ]


def merge_kernel(near, *refs):
    sources, (out, far) = refs[:-2], refs[-2:]
    rows = near.shape[0] // 2
    set_part(out, 0, near, 0)
    for d, source in enumerate(sources):
        set_part(out, (d + 1) * rows, source, 0)
        set_part(far, d * rows, source, 0)


def merge(came, rows, quarter):
    return pl.pallas_call(
        merge_kernel,
        in_specs=[VM] * len(came),
        out_specs=[VM] * 2,
        out_shape=[
            jax.ShapeDtypeStruct((n * rows, quarter), jnp.bfloat16)
            for n in (len(came), len(came) - 1)
        ],
        compiler_params=pltpu.CompilerParams(vmem_limit_bytes=SCOPE),
        name="merge",
    )(*came)


def part_copies(b, first, g_ref, u_ref, g_to, u_to, sems):
    depth = g_to.shape[1]
    rows = pl.ds(pl.multiple_of((lax.axis_index("pf") ^ b) * depth, 128), depth)

    def pair(e):
        return (
            pltpu.make_async_copy(g_ref.at[first + e, rows], g_to.at[e], sems.at[0, e]),
            pltpu.make_async_copy(u_ref.at[first + e, rows], u_to.at[e], sems.at[1, e]),
        )

    def start(e):
        for copy in pair(e):
            copy.start()

    def wait(e):
        for copy in pair(e):
            copy.wait()

    return start, wait


def for_all(act, count):
    @pl.loop(0, count)
    def _(e):
        act(e)


def hold_kernel(ids_hbm, weight_hbm, g_ref, u_ref, *refs):
    own_gate, own_up, next_gate, next_up, select_ref, column_ref = refs[:6]
    ids_ref, weight_ref, few_sems, sems, next_sems = refs[6:]
    few = [
        pltpu.make_async_copy(ids_hbm, ids_ref, few_sems.at[0]),
        pltpu.make_async_copy(weight_hbm, weight_ref, few_sems.at[1]),
    ]
    for copy in few:
        copy.start()
    start, wait = part_copies(0, 0, g_ref, u_ref, own_gate, own_up, sems)
    start_next, wait_next = part_copies(1, 0, g_ref, u_ref, next_gate, next_up, next_sems)
    for_all(start, g_ref.shape[0])
    for_all(start_next, EARLY)
    for copy in few:
        copy.wait()
    top, rows = ids_ref.shape
    experts = g_ref.shape[0]
    slots = rows // 2
    here = lax.axis_index("ep")
    pair = lax.broadcasted_iota(jnp.int32, (top * rows, 1), 0)
    other = lax.broadcasted_iota(jnp.int32, (top * rows, rows), 1)
    ids = jnp.zeros((top * rows, rows), jnp.int32)
    weight = jnp.zeros((top * rows, rows), jnp.float32)
    for k in range(top):
        chosen = (other == pair // top) & (pair % top == k)
        ids = jnp.where(chosen, ids_ref[k : k + 1, :], ids)
        weight = jnp.where(chosen, weight_ref[k : k + 1, :], weight)
    ids = jnp.sum(ids, axis=1, keepdims=True)
    column_ref[...] = jnp.sum(weight, axis=1, keepdims=True)
    earlier = jnp.zeros((top * rows, rows), jnp.int32)
    for k in range(top):
        earlier += jnp.where((ids_ref[k : k + 1, :] == ids) & (other < pair // top), 1, 0)
    slot = jnp.sum(earlier, axis=1, keepdims=True)
    column = lax.broadcasted_iota(jnp.int32, (1, experts * slots), 1)
    for i, d in enumerate((0,) + BACK):
        match = (ids == (here ^ d) * experts + column // slots) & (column % slots == slot)
        select_ref[:, i * experts * slots : (i + 1) * experts * slots] = jnp.where(
            match, 1.0, 0.0
        ).astype(jnp.bfloat16)
    for_all(wait, experts)
    for_all(wait_next, EARLY)


def hold(expert_ids, routing_weights, w_gate, w_up, n_ep):
    experts, depth, wide = w_gate.shape
    rows, top = expert_ids.shape
    shapes = [(n, depth // 4, wide) for n in (experts, experts, EARLY, EARLY)]
    return pl.pallas_call(
        hold_kernel,
        in_specs=[HBM] * 4,
        out_specs=[VM] * 6,
        out_shape=[pltpu.VMEM(shape, jnp.bfloat16) for shape in shapes]
        + [
            jax.ShapeDtypeStruct((rows * top, n_ep * experts * rows // 2), jnp.bfloat16),
            jax.ShapeDtypeStruct((rows * top, 1), jnp.float32),
        ],
        scratch_shapes=[
            pltpu.VMEM((top, rows), jnp.int32),
            pltpu.VMEM((top, rows), jnp.float32),
            pltpu.SemaphoreType.DMA((2,)),
            pltpu.SemaphoreType.DMA((2, experts)),
            pltpu.SemaphoreType.DMA((2, EARLY)),
        ],
        cost_estimate=pl.CostEstimate(
            flops=0, bytes_accessed=(experts + EARLY) * depth * wide, transcendentals=0
        ),
        compiler_params=pltpu.CompilerParams(vmem_limit_bytes=GRANT),
        name="hold",
    )(in_hbm(expert_ids.T), in_hbm(routing_weights.T), w_gate, w_up)


def set_rows(b, x_ref, own_ref, came_ref):
    rows, quarter = own_ref.shape[0], came_ref.shape[1]
    start = pl.multiple_of((lax.axis_index("pf") ^ b) * quarter, 128)
    x_ref[:rows, :] = own_ref[:, pl.ds(start, quarter)]
    x_ref[rows : rows + came_ref.shape[0], :] = came_ref[...]


def set_far_rows(b, x_ref, own_ref, near_ref, far_ref):
    rows, quarter = own_ref.shape[0], far_ref.shape[1]
    start = pl.multiple_of((lax.axis_index("pf") ^ b) * quarter, 128)
    x_ref[:rows, :] = own_ref[:, pl.ds(start, quarter)]
    set_part(x_ref, rows, near_ref, PARTS[1].index(b))
    x_ref[2 * rows : 2 * rows + far_ref.shape[0], :] = far_ref[...]


def times(x_ref, w_ref, e):
    rows = x_ref.shape[0] // 2
    return jnp.dot(x_ref[...], w_ref[e], preferred_element_type=jnp.float32)[:rows]


def set_slots(pieces, slots_ref, experts, rows, top):
    n_ep = len(pieces)
    slots = rows // 2
    wide = CHANNELS - LAT
    ids = jnp.zeros((top, n_ep * rows), jnp.float32)
    for d, piece in enumerate(pieces):
        tail = piece[: 2 * top, piece.shape[1] - wide :][:top]
        lane = lax.broadcasted_iota(jnp.int32, (wide, n_ep * rows), 0)
        column = lax.broadcasted_iota(jnp.int32, (wide, n_ep * rows), 1)
        take = (lane == ROPE + column % rows) & (column // rows == d)
        ids += jnp.dot(
            tail, jnp.where(take, 1.0, 0.0).astype(jnp.bfloat16), preferred_element_type=jnp.float32
        )
    shape = slots_ref.shape
    place = lax.broadcasted_iota(jnp.int32, shape, 0)
    column = lax.broadcasted_iota(jnp.int32, shape, 1)
    expert = lax.axis_index("ep") * experts + place // (n_ep * slots)
    named = jnp.zeros(shape, jnp.float32)
    for k in range(top):
        named += jnp.where(ids[k : k + 1, :].astype(jnp.int32) == expert, 1.0, 0.0)
    named = jnp.where(place % (n_ep * slots) // slots == column // rows, named, 0.0)
    above = lax.broadcasted_iota(jnp.int32, (n_ep * rows,) * 2, 0)
    below = lax.broadcasted_iota(jnp.int32, (n_ep * rows,) * 2, 1)
    before = jnp.where((above // rows == below // rows) & (above < below), 1.0, 0.0)
    rank = jnp.dot(
        named.astype(jnp.bfloat16), before.astype(jnp.bfloat16), preferred_element_type=jnp.float32
    )
    slot = (place % slots).astype(jnp.float32)
    slots_ref[...] = jnp.where((named > 0.5) & (rank == slot), 1.0, 0.0).astype(jnp.bfloat16)


def front_kernel(own, came, came_too, hg, hu, mg, mu, g_hbm, u_hbm, *refs):
    pieces, (gate, up, g_to, u_to, slots_ref) = refs[:-11], refs[-11:-6]
    tg, tu, x_ref, y_ref, few_sems, sems = refs[-6:]
    experts, early = hg.shape[0], mg.shape[0]
    start_few, wait_few = part_copies(1, early, g_hbm, u_hbm, tg, tu, few_sems)
    start, wait = part_copies(2, 0, g_hbm, u_hbm, g_to, u_to, sems)
    for_all(start_few, experts - early)
    set_rows(0, x_ref, own, came)
    set_rows(1, y_ref, own, came_too)

    gate[0] = times(x_ref, hg, 0) + times(y_ref, mg, 0)
    set_slots(pieces, slots_ref, experts, own.shape[0], TOP)
    up[0] = times(x_ref, hu, 0) + times(y_ref, mu, 0)

    @pl.loop(1, early)
    def _(e):
        gate[e] = times(x_ref, hg, e) + times(y_ref, mg, e)
        up[e] = times(x_ref, hu, e) + times(y_ref, mu, e)

    @pl.loop(0, experts - early)
    def _(e):
        for at in (2 * e, 2 * e + 1):

            @pl.when(at < AHEAD)
            def _():
                start(at)

        wait_few(e)
        at = early + e
        gate[at] = times(x_ref, hg, at) + times(y_ref, tg, e)
        up[at] = times(x_ref, hu, at) + times(y_ref, tu, e)

    for_all(wait, AHEAD)


def front(own, x0, x1, held, pieces, w_gate, w_up):
    experts, depth, wide = w_gate.shape
    rows = own.shape[0] + x0.shape[0]
    part = depth // 4
    rest = experts - EARLY
    sums = [jax.ShapeDtypeStruct((experts, rows, wide), jnp.float32)] * 2
    *sums, gate, up, slots = pl.pallas_call(
        front_kernel,
        in_specs=[VM] * 7 + [HBM] * 2 + [VM] * len(pieces),
        out_specs=[VM] * 5,
        out_shape=sums
        + [pltpu.VMEM((AHEAD, part, wide), jnp.bfloat16)] * 2
        + [jax.ShapeDtypeStruct((experts * rows // 2, rows), jnp.bfloat16)],
        scratch_shapes=[pltpu.VMEM((rest, part, wide), jnp.bfloat16)] * 2
        + [pltpu.VMEM((2 * rows, part), jnp.bfloat16)] * 2
        + [pltpu.SemaphoreType.DMA((2, rest)), pltpu.SemaphoreType.DMA((2, AHEAD))],
        cost_estimate=pl.CostEstimate(
            flops=2 * rows * depth * wide * experts,
            bytes_accessed=(rest + AHEAD) * depth * wide,
            transcendentals=0,
        ),
        compiler_params=pltpu.CompilerParams(vmem_limit_bytes=GRANT),
        name="front",
    )(own, x0, x1, *map(in_vmem, held), w_gate, w_up, *pieces)
    return sums, (gate, up), slots


def last_kernel(n_ep, own, near, far, far_too, hg, hu, g_hbm, u_hbm, gate, up, slots_ref, *refs):
    outs, (gate_sum, up_sum, tg, tu, gb, ub, x_ref, y_ref, few_sems, sems) = refs[:-10], refs[-10:]
    experts, held = gate.shape[0], hg.shape[0]
    slots = outs[0].shape[1]
    start_few, wait_few = part_copies(2, held, g_hbm, u_hbm, tg, tu, few_sems)
    start, wait = part_copies(3, 0, g_hbm, u_hbm, gb, ub, sems)
    for_all(start_few, experts - held)
    start(0)
    set_far_rows(2, x_ref, own, near, far)
    set_rows(3, y_ref, own, far_too)

    @pl.loop(0, held, unroll=2)
    def _(e):
        start(e + 1)
        gate_sum[e] = gate[e] + times(x_ref, hg, e)
        up_sum[e] = up[e] + times(x_ref, hu, e)

    @pl.loop(0, experts - held)
    def _(e):
        wait_few(e)

        @pl.when(held + e + 1 < experts)
        def _():
            start(held + e + 1)

        gate_sum[held + e] = gate[held + e] + times(x_ref, tg, e)
        up_sum[held + e] = up[held + e] + times(x_ref, tu, e)

    def add(e):
        wait(e)
        gate_sum[e] += times(y_ref, gb, e)
        up_sum[e] += times(y_ref, ub, e)

    def finish(e):
        gate_part = gate_sum[e]
        hidden = (gate_part * jax.nn.sigmoid(gate_part) * up_sum[e]).astype(jnp.bfloat16)
        places = pl.ds(pl.multiple_of(e * n_ep * slots, n_ep * slots), n_ep * slots)
        back = jnp.dot(slots_ref[places, :], hidden, preferred_element_type=jnp.float32)
        back = back.astype(jnp.bfloat16)
        for d in range(n_ep):
            outs[d][e] = back[d * slots : (d + 1) * slots]

    add(0)

    @pl.loop(1, experts)
    def _(e):
        add(e)
        finish(e - 1)

    finish(experts - 1)


def last(n_ep, own, near, far, far_too, held, gate, up, slots, w_gate, w_up):
    experts, depth, wide = w_gate.shape
    rows, part = n_ep * own.shape[0], depth // 4
    rest = experts - AHEAD
    out = jax.ShapeDtypeStruct((experts, own.shape[0] // 2, wide), jnp.bfloat16)
    return pl.pallas_call(
        functools.partial(last_kernel, n_ep),
        in_specs=[VM] * 6 + [HBM] * 2 + [VM] * 3,
        out_specs=[VM] * n_ep,
        out_shape=[out] * n_ep,
        scratch_shapes=[pltpu.VMEM((experts, rows, wide), jnp.float32)] * 2
        + [pltpu.VMEM((n, part, wide), jnp.bfloat16) for n in (rest, rest, experts, experts)]
        + [pltpu.VMEM((2 * rows, part), jnp.bfloat16)] * 2
        + [pltpu.SemaphoreType.DMA((2, rest)), pltpu.SemaphoreType.DMA((2, experts))],
        cost_estimate=pl.CostEstimate(
            flops=2 * rows * depth * wide * experts,
            bytes_accessed=(experts + rest) * depth * wide,
            transcendentals=experts * rows * wide,
        ),
        compiler_params=pltpu.CompilerParams(
            vmem_limit_bytes=GRANT + (experts + EARLY) * 4 * part * wide
        ),
        name="last",
    )(own, near, far, far_too, *[in_vmem(x) for x in held], w_gate, w_up, gate, up, slots)


def pick_kernel(select_ref, column_ref, *refs):
    blocks, o_ref = refs[:-1], refs[-1]
    experts, rows, wide = blocks[0].shape
    total = jnp.zeros((select_ref.shape[0], wide), jnp.float32)
    for d, block in enumerate(blocks):
        total += jnp.dot(
            select_ref[:, d * experts * rows : (d + 1) * experts * rows],
            block[...].reshape(experts * rows, wide),
            preferred_element_type=jnp.float32,
        )
    o_ref[...] = (total * column_ref[...]).astype(jnp.bfloat16)


def pick(select, column, blocks):
    pairs, wide = select.shape[0], blocks[0].shape[2]
    return pl.pallas_call(
        pick_kernel,
        in_specs=[VM] * (2 + len(blocks)),
        out_specs=VM,
        out_shape=jax.ShapeDtypeStruct((pairs, wide), jnp.bfloat16),
        compiler_params=pltpu.CompilerParams(vmem_limit_bytes=SCOPE),
        name="pick",
    )(select, column, *blocks)


def crossed(x, axis, bit):
    n = lax.axis_size(axis)
    return lax.ppermute(x, axis, [(s, s ^ bit) for s in range(n)])


def local_ring(
    cache_codes,
    cache_scales,
    queries,
    new_latent,
    prompt_lengths,
    tokens,
    expert_ids,
    routing_weights,
    w_gate,
    w_up,
):
    n_ep = lax.axis_size("ep")
    per = cache_codes.shape[1]
    half = tokens.shape[1] // 8
    rows = tokens.shape[0]
    *sent, own_piece = pack(cache_codes, cache_scales, tokens, expert_ids, n_ep)
    came = [crossed(x, "ep", d) for d, x in zip(ORDER, sent)]
    w_gate, w_up = in_hbm(w_gate), in_hbm(w_up)
    *held, select, column = hold(expert_ids, routing_weights, w_gate, w_up, n_ep)
    came, held, select, column = lax.optimization_barrier((came, held, select, column))
    came = [came[ORDER.index(d)] for d in range(1, n_ep)]
    x0, far = merge(came, rows, 2 * half)
    x1 = crossed(x0, "pf", 1)
    x2 = crossed(far, "pf", 2)
    x3 = crossed(x0, "pf", 3)
    pieces = [own_piece] + came
    sums, held, slots = front(tokens, x0, x1, held, pieces, w_gate, w_up)
    blocks = last(n_ep, tokens, came[0], x2, x3, held, *sums, slots, w_gate, w_up)
    back = [blocks[0]] + [crossed(blocks[d], "ep", d) for d in BACK]
    attention_out = attend(queries, new_latent, prompt_lengths, per, pieces)
    moe_hidden = pick(select, column, back)
    return attention_out, moe_hidden.reshape(rows, -1, moe_hidden.shape[1])


def local_wide(
    cache_codes,
    cache_scales,
    queries,
    new_latent,
    prompt_lengths,
    tokens,
    expert_ids,
    routing_weights,
    w_gate,
    w_up,
):
    latent = decode_cache(cache_codes, cache_scales)
    cache = lax.all_to_all(latent, "ep", split_axis=0, concat_axis=1, tiled=True)
    per = cache.shape[1]
    cache = jnp.pad(cache, ((0, 0), (0, 0), (0, CHANNELS - cache.shape[2])))
    cache = cache.reshape(-1, CHANNELS)
    attention_out = attend(queries, new_latent, prompt_lengths, per, [cache])
    x = lax.all_gather(tokens, "ep", axis=0, tiled=True)
    gate = jnp.einsum("rd,edf->erf", x, w_gate, preferred_element_type=jnp.float32)
    up = jnp.einsum("rd,edf->erf", x, w_up, preferred_element_type=jnp.float32)
    hidden = (jax.nn.silu(gate) * up).astype(jnp.bfloat16)
    back = lax.all_to_all(hidden, "ep", split_axis=1, concat_axis=0, tiled=True)
    match = expert_ids[:, :, None] == jnp.arange(back.shape[0], dtype=jnp.int32)
    picked = jnp.einsum(
        "rke,erf->rkf", match.astype(jnp.bfloat16), back, preferred_element_type=jnp.float32
    )
    return attention_out, (picked * routing_weights[:, :, None]).astype(jnp.bfloat16)


def solution(mesh):
    near = mesh.shape["ep"] == 4 and mesh.shape["pf"] == 4
    return jax.shard_map(
        local_ring if near else local_wide,
        mesh=mesh,
        in_specs=(
            P(("groups", "pf"), "ep", None),
            P(("groups", "pf"), "ep", None),
            P(("groups", "pf", "ep"), None, None),
            P(("groups", "pf", "ep"), None),
            P(("groups", "pf", "ep")),
            P(("groups", "ep"), None),
            P(("groups", "ep"), None),
            P(("groups", "ep"), None),
            P("ep", None, "pf"),
            P("ep", None, "pf"),
        ),
        out_specs=(P(("groups", "pf", "ep"), None, None), P(("groups", "ep"), None, "pf")),
        check_vma=False,
    )
```

```python
import functools

import jax
import jax.numpy as jnp
from jax import lax
from jax.experimental import pallas as pl
from jax.experimental.pallas import tpu as pltpu
from jax.sharding import PartitionSpec as P

LAT = 512
ROPE = 64
GROUP = 128
TOP = 8
EARLY = 3
AHEAD = 6
CHANNELS = 640
SCOPE = 4 << 20
GRANT = 16 << 20
PARTS = {1: (0, 2), 2: (0,), 3: (0,)}
ORDER = (2, 1, 3)
BACK = (3, 2, 1)
HELD = 14 << 20

qk_scale = 192.0 ** (-0.5)
VM = pl.BlockSpec(memory_space=pltpu.VMEM)
SM = pl.BlockSpec(memory_space=pltpu.SMEM)
HBM = pl.BlockSpec(memory_space=pltpu.HBM)


def spread_scales(scale_block):
    latent_part = jnp.repeat(scale_block[..., :-1], GROUP, axis=-1, total_repeat_length=LAT)
    rope_part = jnp.repeat(scale_block[..., -1:], ROPE, axis=-1, total_repeat_length=ROPE)
    return jnp.concatenate([latent_part, rope_part], axis=-1)


def decode_cache(codes, scales):
    return (codes.astype(jnp.float32) * spread_scales(scales.astype(jnp.float32))).astype(
        jnp.bfloat16
    )


def attend_kernel(per, q_ref, new_ref, len_ref, *refs):
    pieces, (o_ref, kv_ref) = refs[:-2], refs[-2:]
    rows, width, heads = q_ref.shape
    total = kv_ref.shape[0]
    block = rows * per
    count = len(pieces) * block
    kv_ref[pl.ds(count, total - count), :] = jnp.zeros((total - count, width), jnp.bfloat16)
    for d, piece in enumerate(pieces):
        kv_ref[pl.ds(d * block, block), :] = piece[:, piece.shape[1] - CHANNELS :][:, :width]
    kv_ref[pl.ds(count, rows), :] = new_ref[...]
    kv = kv_ref[...]
    place = lax.broadcasted_iota(jnp.int32, (total, 1), 0)
    start = jnp.zeros_like(place)
    for d in range(len(pieces)) if len(pieces) > 1 else ():
        start = jnp.where(place // block == d, (lax.axis_index("ep") ^ d) * per, start)
    row_of = place % block // per
    position = start + place % per
    for r in range(rows):
        live = ((place < count) & (row_of == r) & (position < len_ref[r])) | (place == count + r)
        scores = jnp.dot(kv, q_ref[r], preferred_element_type=jnp.float32) * qk_scale
        scores = jnp.where(live, scores, -jnp.inf)
        exponent = jnp.exp(scores - jnp.max(scores, axis=0, keepdims=True))
        weights = exponent / jnp.sum(exponent, axis=0, keepdims=True)
        o_ref[r] = lax.dot_general(
            weights.astype(jnp.bfloat16),
            kv[:, :LAT],
            (((0,), (0,)), ((), ())),
            preferred_element_type=jnp.float32,
        ).astype(jnp.bfloat16)


def attend(queries, new_latent, prompt_lengths, per, pieces):
    rows, heads, width = queries.shape
    count = sum(p.shape[0] for p in pieces)
    total = -(-(count + rows) // 128) * 128
    return pl.pallas_call(
        functools.partial(attend_kernel, per),
        in_specs=[VM, VM, SM] + [VM] * len(pieces),
        out_specs=VM,
        out_shape=jax.ShapeDtypeStruct((rows, heads, LAT), jnp.bfloat16),
        scratch_shapes=[pltpu.VMEM((total, width), jnp.bfloat16)],
        cost_estimate=pl.CostEstimate(
            flops=4 * rows * heads * total * width,
            bytes_accessed=2 * rows * heads * (width + LAT),
            transcendentals=rows * heads * total,
        ),
        compiler_params=pltpu.CompilerParams(vmem_limit_bytes=SCOPE),
        name="attend",
    )(queries.swapaxes(1, 2), new_latent, prompt_lengths, *pieces)


def pack_kernel(codes_hbm, scales_hbm, tokens_hbm, ids_hbm, *refs):
    outs, own, (codes_ref, scales_ref, ids_ref, lat_ref, sems, token_sems) = (
        refs[:-7],
        refs[-7],
        refs[-6:],
    )
    rows, per, width = codes_ref.shape
    groups = scales_ref.shape[0]
    block = own.shape[0]
    half = tokens_hbm.shape[1] // 8
    here, me = lax.axis_index("ep"), lax.axis_index("pf")
    cache = [
        pltpu.make_async_copy(codes_hbm, codes_ref, sems.at[0]),
        pltpu.make_async_copy(scales_hbm, scales_ref, sems.at[1]),
        pltpu.make_async_copy(ids_hbm, ids_ref, sems.at[2]),
    ]
    token_copies = []
    for i, out in enumerate(outs):
        for j, b in enumerate(PARTS[ORDER[i]]):
            for c in range(2):
                start = pl.multiple_of((2 * (me ^ b) + c) * half, 128)
                token_copies.append(
                    pltpu.make_async_copy(
                        tokens_hbm.at[:, pl.ds(start, half)],
                        out.at[pl.ds(c * block // 2, block // 2), pl.ds(j * half, half)],
                        token_sems.at[i, 2 * j + c],
                    )
                )
    for copy in cache + token_copies:
        copy.start()
    lat_ref[:, width:] = jnp.zeros((rows * per, CHANNELS - width), jnp.float32)
    for copy in cache:
        copy.wait()
    scales = scales_ref[...].astype(jnp.float32)
    top, named = ids_ref.shape
    for d in range(len(outs) + 1):
        lat_ref[d * block : d * block + top, width : width + named] = ids_ref[...].astype(
            jnp.float32
        )
    for r in range(rows):
        for g in range(groups):
            columns = slice(g * GROUP, min((g + 1) * GROUP, width))
            lat_ref[r * per : (r + 1) * per, columns] = (
                codes_ref[r, :, columns].astype(jnp.float32) * scales[g, :, r : r + 1]
            )
    for d in range(len(outs) + 1):
        start = pl.multiple_of((here ^ d) * block, block)
        part = lat_ref[pl.ds(start, block), :].astype(jnp.bfloat16)
        if d == 0:
            own[...] = part
        else:
            outs[ORDER.index(d)][:, len(PARTS[d]) * half :] = part
    for copy in token_copies:
        copy.wait()


def in_hbm(x):
    return pltpu.with_memory_space_constraint(x, pltpu.HBM)


def in_vmem(x):
    return pltpu.with_memory_space_constraint(x, pltpu.VMEM)


def pack(codes, scales, tokens, expert_ids, n_ep):
    rows, per, width = codes.shape
    block = rows * per // n_ep
    wide = [len(PARTS[d]) * tokens.shape[1] // 8 + CHANNELS for d in ORDER]
    scales, ids = scales.transpose(2, 1, 0), expert_ids.T
    return pl.pallas_call(
        pack_kernel,
        in_specs=[HBM] * 4,
        out_specs=[VM] * n_ep,
        out_shape=[jax.ShapeDtypeStruct((block, w), jnp.bfloat16) for w in wide]
        + [jax.ShapeDtypeStruct((block, CHANNELS), jnp.bfloat16)],
        scratch_shapes=[
            pltpu.VMEM(codes.shape, jnp.bfloat16),
            pltpu.VMEM(scales.shape, jnp.bfloat16),
            pltpu.VMEM(ids.shape, jnp.int32),
            pltpu.VMEM((rows * per, CHANNELS), jnp.float32),
            pltpu.SemaphoreType.DMA((3,)),
            pltpu.SemaphoreType.DMA((n_ep - 1, 4)),
        ],
        compiler_params=pltpu.CompilerParams(vmem_limit_bytes=SCOPE),
        name="pack",
    )(in_hbm(codes), in_hbm(scales), in_hbm(tokens), in_hbm(ids))


def set_part(ref, at, source, j):
    rows, half = source.shape[0] // 2, ref.shape[1] // 2
    for c in range(2):
        ref[at : at + rows, c * half : (c + 1) * half] = source[
            c * rows : (c + 1) * rows, j * half : (j + 1) * half
        ]


def merge_kernel(near, *refs):
    sources, (out, far) = refs[:-2], refs[-2:]
    rows = near.shape[0] // 2
    set_part(out, 0, near, 0)
    for d, source in enumerate(sources):
        set_part(out, (d + 1) * rows, source, 0)
        set_part(far, d * rows, source, 0)


def merge(came, rows, quarter):
    return pl.pallas_call(
        merge_kernel,
        in_specs=[VM] * len(came),
        out_specs=[VM] * 2,
        out_shape=[
            jax.ShapeDtypeStruct((n * rows, quarter), jnp.bfloat16)
            for n in (len(came), len(came) - 1)
        ],
        compiler_params=pltpu.CompilerParams(vmem_limit_bytes=SCOPE),
        name="merge",
    )(*came)


def part_copies(b, first, g_ref, u_ref, g_to, u_to, sems):
    depth = g_to.shape[1]
    rows = pl.ds(pl.multiple_of((lax.axis_index("pf") ^ b) * depth, 128), depth)

    def pair(e):
        return (
            pltpu.make_async_copy(g_ref.at[first + e, rows], g_to.at[e], sems.at[0, e]),
            pltpu.make_async_copy(u_ref.at[first + e, rows], u_to.at[e], sems.at[1, e]),
        )

    def start(e):
        for copy in pair(e):
            copy.start()

    def wait(e):
        for copy in pair(e):
            copy.wait()

    return start, wait


def for_all(act, count):
    @pl.loop(0, count)
    def _(e):
        act(e)


def hold_kernel(ids_hbm, weight_hbm, g_ref, u_ref, *refs):
    own_gate, own_up, next_gate, next_up, select_ref, column_ref = refs[:6]
    ids_ref, weight_ref, few_sems, sems, next_sems = refs[6:]
    few = [
        pltpu.make_async_copy(ids_hbm, ids_ref, few_sems.at[0]),
        pltpu.make_async_copy(weight_hbm, weight_ref, few_sems.at[1]),
    ]
    for copy in few:
        copy.start()
    start, wait = part_copies(0, 0, g_ref, u_ref, own_gate, own_up, sems)
    start_next, wait_next = part_copies(1, 0, g_ref, u_ref, next_gate, next_up, next_sems)
    for_all(start, g_ref.shape[0])
    for_all(start_next, EARLY)
    for copy in few:
        copy.wait()
    top, rows = ids_ref.shape
    experts = g_ref.shape[0]
    slots = rows // 2
    here = lax.axis_index("ep")
    pair = lax.broadcasted_iota(jnp.int32, (top * rows, 1), 0)
    other = lax.broadcasted_iota(jnp.int32, (top * rows, rows), 1)
    ids = jnp.zeros((top * rows, rows), jnp.int32)
    weight = jnp.zeros((top * rows, rows), jnp.float32)
    for k in range(top):
        chosen = (other == pair // top) & (pair % top == k)
        ids = jnp.where(chosen, ids_ref[k : k + 1, :], ids)
        weight = jnp.where(chosen, weight_ref[k : k + 1, :], weight)
    ids = jnp.sum(ids, axis=1, keepdims=True)
    column_ref[...] = jnp.sum(weight, axis=1, keepdims=True)
    earlier = jnp.zeros((top * rows, rows), jnp.int32)
    for k in range(top):
        earlier += jnp.where((ids_ref[k : k + 1, :] == ids) & (other < pair // top), 1, 0)
    slot = jnp.sum(earlier, axis=1, keepdims=True)
    column = lax.broadcasted_iota(jnp.int32, (1, experts * slots), 1)
    for i, d in enumerate((0,) + BACK):
        match = (ids == (here ^ d) * experts + column // slots) & (column % slots == slot)
        select_ref[:, i * experts * slots : (i + 1) * experts * slots] = jnp.where(
            match, 1.0, 0.0
        ).astype(jnp.bfloat16)
    for_all(wait, experts)
    for_all(wait_next, EARLY)


def hold(expert_ids, routing_weights, w_gate, w_up, n_ep):
    experts, depth, wide = w_gate.shape
    rows, top = expert_ids.shape
    shapes = [(n, depth // 4, wide) for n in (experts, experts, EARLY, EARLY)]
    return pl.pallas_call(
        hold_kernel,
        in_specs=[HBM] * 4,
        out_specs=[VM] * 6,
        out_shape=[pltpu.VMEM(shape, jnp.bfloat16) for shape in shapes]
        + [
            jax.ShapeDtypeStruct((rows * top, n_ep * experts * rows // 2), jnp.bfloat16),
            jax.ShapeDtypeStruct((rows * top, 1), jnp.float32),
        ],
        scratch_shapes=[
            pltpu.VMEM((top, rows), jnp.int32),
            pltpu.VMEM((top, rows), jnp.float32),
            pltpu.SemaphoreType.DMA((2,)),
            pltpu.SemaphoreType.DMA((2, experts)),
            pltpu.SemaphoreType.DMA((2, EARLY)),
        ],
        cost_estimate=pl.CostEstimate(
            flops=0, bytes_accessed=(experts + EARLY) * depth * wide, transcendentals=0
        ),
        compiler_params=pltpu.CompilerParams(vmem_limit_bytes=GRANT),
        name="hold",
    )(in_hbm(expert_ids.T), in_hbm(routing_weights.T), w_gate, w_up)


def set_rows(b, x_ref, own_ref, came_ref):
    rows, quarter = own_ref.shape[0], came_ref.shape[1]
    start = pl.multiple_of((lax.axis_index("pf") ^ b) * quarter, 128)
    x_ref[:rows, :] = own_ref[:, pl.ds(start, quarter)]
    x_ref[rows : rows + came_ref.shape[0], :] = came_ref[...]


def set_far_rows(b, x_ref, own_ref, near_ref, far_ref):
    rows, quarter = own_ref.shape[0], far_ref.shape[1]
    start = pl.multiple_of((lax.axis_index("pf") ^ b) * quarter, 128)
    x_ref[:rows, :] = own_ref[:, pl.ds(start, quarter)]
    set_part(x_ref, rows, near_ref, PARTS[1].index(b))
    x_ref[2 * rows : 2 * rows + far_ref.shape[0], :] = far_ref[...]


def times(x_ref, w_ref, e):
    rows = x_ref.shape[0] // 2
    return jnp.dot(x_ref[...], w_ref[e], preferred_element_type=jnp.float32)[:rows]


def set_slots(pieces, slots_ref, experts, rows, top):
    n_ep = len(pieces)
    slots = rows // 2
    wide = CHANNELS - LAT
    ids = jnp.zeros((top, n_ep * rows), jnp.float32)
    for d, piece in enumerate(pieces):
        tail = piece[: 2 * top, piece.shape[1] - wide :][:top]
        lane = lax.broadcasted_iota(jnp.int32, (wide, n_ep * rows), 0)
        column = lax.broadcasted_iota(jnp.int32, (wide, n_ep * rows), 1)
        take = (lane == ROPE + column % rows) & (column // rows == d)
        ids += jnp.dot(
            tail, jnp.where(take, 1.0, 0.0).astype(jnp.bfloat16), preferred_element_type=jnp.float32
        )
    shape = slots_ref.shape
    place = lax.broadcasted_iota(jnp.int32, shape, 0)
    column = lax.broadcasted_iota(jnp.int32, shape, 1)
    expert = lax.axis_index("ep") * experts + place // (n_ep * slots)
    named = jnp.zeros(shape, jnp.float32)
    for k in range(top):
        named += jnp.where(ids[k : k + 1, :].astype(jnp.int32) == expert, 1.0, 0.0)
    named = jnp.where(place % (n_ep * slots) // slots == column // rows, named, 0.0)
    above = lax.broadcasted_iota(jnp.int32, (n_ep * rows,) * 2, 0)
    below = lax.broadcasted_iota(jnp.int32, (n_ep * rows,) * 2, 1)
    before = jnp.where((above // rows == below // rows) & (above < below), 1.0, 0.0)
    rank = jnp.dot(
        named.astype(jnp.bfloat16), before.astype(jnp.bfloat16), preferred_element_type=jnp.float32
    )
    slot = (place % slots).astype(jnp.float32)
    slots_ref[...] = jnp.where((named > 0.5) & (rank == slot), 1.0, 0.0).astype(jnp.bfloat16)


def front_kernel(own, came, came_too, hg, hu, mg, mu, g_hbm, u_hbm, *refs):
    pieces, (gate, up, g_to, u_to, slots_ref) = refs[:-11], refs[-11:-6]
    tg, tu, x_ref, y_ref, few_sems, sems = refs[-6:]
    experts, early = hg.shape[0], mg.shape[0]
    start_few, wait_few = part_copies(1, early, g_hbm, u_hbm, tg, tu, few_sems)
    start, wait = part_copies(2, 0, g_hbm, u_hbm, g_to, u_to, sems)
    for_all(start_few, experts - early)
    set_rows(0, x_ref, own, came)
    set_rows(1, y_ref, own, came_too)

    gate[0] = times(x_ref, hg, 0) + times(y_ref, mg, 0)
    set_slots(pieces, slots_ref, experts, own.shape[0], TOP)
    up[0] = times(x_ref, hu, 0) + times(y_ref, mu, 0)

    @pl.loop(1, early)
    def _(e):
        gate[e] = times(x_ref, hg, e) + times(y_ref, mg, e)
        up[e] = times(x_ref, hu, e) + times(y_ref, mu, e)

    @pl.loop(0, experts - early)
    def _(e):
        for at in (2 * e, 2 * e + 1):

            @pl.when(at < AHEAD)
            def _():
                start(at)

        wait_few(e)
        at = early + e
        gate[at] = times(x_ref, hg, at) + times(y_ref, tg, e)
        up[at] = times(x_ref, hu, at) + times(y_ref, tu, e)

    for_all(wait, AHEAD)


def front(own, x0, x1, held, pieces, w_gate, w_up):
    experts, depth, wide = w_gate.shape
    rows = own.shape[0] + x0.shape[0]
    part = depth // 4
    rest = experts - EARLY
    sums = [jax.ShapeDtypeStruct((experts, rows, wide), jnp.float32)] * 2
    *sums, gate, up, slots = pl.pallas_call(
        front_kernel,
        in_specs=[VM] * 7 + [HBM] * 2 + [VM] * len(pieces),
        out_specs=[VM] * 5,
        out_shape=sums
        + [pltpu.VMEM((AHEAD, part, wide), jnp.bfloat16)] * 2
        + [jax.ShapeDtypeStruct((experts * rows // 2, rows), jnp.bfloat16)],
        scratch_shapes=[pltpu.VMEM((rest, part, wide), jnp.bfloat16)] * 2
        + [pltpu.VMEM((2 * rows, part), jnp.bfloat16)] * 2
        + [pltpu.SemaphoreType.DMA((2, rest)), pltpu.SemaphoreType.DMA((2, AHEAD))],
        cost_estimate=pl.CostEstimate(
            flops=2 * rows * depth * wide * experts,
            bytes_accessed=(rest + AHEAD) * depth * wide,
            transcendentals=0,
        ),
        compiler_params=pltpu.CompilerParams(vmem_limit_bytes=GRANT),
        name="front",
    )(own, x0, x1, *map(in_vmem, held), w_gate, w_up, *pieces)
    return sums, (gate, up), slots


def last_kernel(n_ep, own, near, far, far_too, hg, hu, g_hbm, u_hbm, gate, up, slots_ref, *refs):
    outs, (gate_sum, up_sum, tg, tu, gb, ub, x_ref, y_ref, few_sems, sems) = refs[:-10], refs[-10:]
    experts, held = gate.shape[0], hg.shape[0]
    slots = outs[0].shape[1]
    start_few, wait_few = part_copies(2, held, g_hbm, u_hbm, tg, tu, few_sems)
    start, wait = part_copies(3, 0, g_hbm, u_hbm, gb, ub, sems)
    for_all(start_few, experts - held)
    start(0)
    set_far_rows(2, x_ref, own, near, far)
    set_rows(3, y_ref, own, far_too)

    @pl.loop(0, held, unroll=2)
    def _(e):
        start(e + 1)
        gate_sum[e] = gate[e] + times(x_ref, hg, e)
        up_sum[e] = up[e] + times(x_ref, hu, e)

    @pl.loop(0, experts - held)
    def _(e):
        wait_few(e)

        @pl.when(held + e + 1 < experts)
        def _():
            start(held + e + 1)

        gate_sum[held + e] = gate[held + e] + times(x_ref, tg, e)
        up_sum[held + e] = up[held + e] + times(x_ref, tu, e)

    def add(e):
        wait(e)
        gate_sum[e] += times(y_ref, gb, e)
        up_sum[e] += times(y_ref, ub, e)

    def finish(e):
        gate_part = gate_sum[e]
        hidden = (gate_part * jax.nn.sigmoid(gate_part) * up_sum[e]).astype(jnp.bfloat16)
        places = pl.ds(pl.multiple_of(e * n_ep * slots, n_ep * slots), n_ep * slots)
        back = jnp.dot(slots_ref[places, :], hidden, preferred_element_type=jnp.float32)
        back = back.astype(jnp.bfloat16)
        for d in range(n_ep):
            outs[d][e] = back[d * slots : (d + 1) * slots]

    add(0)

    @pl.loop(1, experts)
    def _(e):
        add(e)
        finish(e - 1)

    finish(experts - 1)


def last(n_ep, own, near, far, far_too, held, gate, up, slots, w_gate, w_up):
    experts, depth, wide = w_gate.shape
    rows, part = n_ep * own.shape[0], depth // 4
    rest = experts - AHEAD
    out = jax.ShapeDtypeStruct((experts, own.shape[0] // 2, wide), jnp.bfloat16)
    return pl.pallas_call(
        functools.partial(last_kernel, n_ep),
        in_specs=[VM] * 6 + [HBM] * 2 + [VM] * 3,
        out_specs=[VM] * n_ep,
        out_shape=[out] * n_ep,
        scratch_shapes=[pltpu.VMEM((experts, rows, wide), jnp.float32)] * 2
        + [pltpu.VMEM((n, part, wide), jnp.bfloat16) for n in (rest, rest, experts, experts)]
        + [pltpu.VMEM((2 * rows, part), jnp.bfloat16)] * 2
        + [pltpu.SemaphoreType.DMA((2, rest)), pltpu.SemaphoreType.DMA((2, experts))],
        cost_estimate=pl.CostEstimate(
            flops=2 * rows * depth * wide * experts,
            bytes_accessed=(experts + rest) * depth * wide,
            transcendentals=experts * rows * wide,
        ),
        compiler_params=pltpu.CompilerParams(
            vmem_limit_bytes=GRANT + (experts + EARLY) * 4 * part * wide
        ),
        name="last",
    )(own, near, far, far_too, *[in_vmem(x) for x in held], w_gate, w_up, gate, up, slots)


def pick_kernel(select_ref, column_ref, *refs):
    blocks, o_ref = refs[:-1], refs[-1]
    experts, rows, wide = blocks[0].shape
    total = jnp.zeros((select_ref.shape[0], wide), jnp.float32)
    for d, block in enumerate(blocks):
        total += jnp.dot(
            select_ref[:, d * experts * rows : (d + 1) * experts * rows],
            block[...].reshape(experts * rows, wide),
            preferred_element_type=jnp.float32,
        )
    o_ref[...] = (total * column_ref[...]).astype(jnp.bfloat16)


def pick(select, column, blocks):
    pairs, wide = select.shape[0], blocks[0].shape[2]
    return pl.pallas_call(
        pick_kernel,
        in_specs=[VM] * (2 + len(blocks)),
        out_specs=VM,
        out_shape=jax.ShapeDtypeStruct((pairs, wide), jnp.bfloat16),
        compiler_params=pltpu.CompilerParams(vmem_limit_bytes=SCOPE),
        name="pick",
    )(select, column, *blocks)


def crossed(x, axis, bit):
    n = lax.axis_size(axis)
    return lax.ppermute(x, axis, [(s, s ^ bit) for s in range(n)])


def local_ring(
    cache_codes,
    cache_scales,
    queries,
    new_latent,
    prompt_lengths,
    tokens,
    expert_ids,
    routing_weights,
    w_gate,
    w_up,
):
    n_ep = lax.axis_size("ep")
    per = cache_codes.shape[1]
    half = tokens.shape[1] // 8
    rows = tokens.shape[0]
    *sent, own_piece = pack(cache_codes, cache_scales, tokens, expert_ids, n_ep)
    came = [crossed(x, "ep", d) for d, x in zip(ORDER, sent)]
    w_gate, w_up = in_hbm(w_gate), in_hbm(w_up)
    *held, select, column = hold(expert_ids, routing_weights, w_gate, w_up, n_ep)
    came, held, select, column = lax.optimization_barrier((came, held, select, column))
    came = [came[ORDER.index(d)] for d in range(1, n_ep)]
    x0, far = merge(came, rows, 2 * half)
    x1 = crossed(x0, "pf", 1)
    x2 = crossed(far, "pf", 2)
    x3 = crossed(x0, "pf", 3)
    pieces = [own_piece] + came
    sums, held, slots = front(tokens, x0, x1, held, pieces, w_gate, w_up)
    blocks = last(n_ep, tokens, came[0], x2, x3, held, *sums, slots, w_gate, w_up)
    back = [blocks[0]] + [crossed(blocks[d], "ep", d) for d in BACK]
    attention_out = attend(queries, new_latent, prompt_lengths, per, pieces)
    moe_hidden = pick(select, column, back)
    return attention_out, moe_hidden.reshape(rows, -1, moe_hidden.shape[1])


def local_wide(
    cache_codes,
    cache_scales,
    queries,
    new_latent,
    prompt_lengths,
    tokens,
    expert_ids,
    routing_weights,
    w_gate,
    w_up,
):
    latent = decode_cache(cache_codes, cache_scales)
    cache = lax.all_to_all(latent, "ep", split_axis=0, concat_axis=1, tiled=True)
    per = cache.shape[1]
    cache = jnp.pad(cache, ((0, 0), (0, 0), (0, CHANNELS - cache.shape[2])))
    cache = cache.reshape(-1, CHANNELS)
    attention_out = attend(queries, new_latent, prompt_lengths, per, [cache])
    x = lax.all_gather(tokens, "ep", axis=0, tiled=True)
    gate = jnp.einsum("rd,edf->erf", x, w_gate, preferred_element_type=jnp.float32)
    up = jnp.einsum("rd,edf->erf", x, w_up, preferred_element_type=jnp.float32)
    hidden = (jax.nn.silu(gate) * up).astype(jnp.bfloat16)
    back = lax.all_to_all(hidden, "ep", split_axis=1, concat_axis=0, tiled=True)
    match = expert_ids[:, :, None] == jnp.arange(back.shape[0], dtype=jnp.int32)
    picked = jnp.einsum(
        "rke,erf->rkf", match.astype(jnp.bfloat16), back, preferred_element_type=jnp.float32
    )
    return attention_out, (picked * routing_weights[:, :, None]).astype(jnp.bfloat16)


def solution(mesh):
    near = mesh.shape["ep"] == 4 and mesh.shape["pf"] == 4
    return jax.shard_map(
        local_ring if near else local_wide,
        mesh=mesh,
        in_specs=(
            P(("groups", "pf"), "ep", None),
            P(("groups", "pf"), "ep", None),
            P(("groups", "pf", "ep"), None, None),
            P(("groups", "pf", "ep"), None),
            P(("groups", "pf", "ep")),
            P(("groups", "ep"), None),
            P(("groups", "ep"), None),
            P(("groups", "ep"), None),
            P("ep", None, "pf"),
            P("ep", None, "pf"),
        ),
        out_specs=(P(("groups", "pf", "ep"), None, None), P(("groups", "ep"), None, "pf")),
        check_vma=False,
    )
```
